32 devices in a mesh: ctx: 8 (over z, core), fsdp: 4 (over y, x).
Axes of the slice: x: 2, y: 2, z: 4, core: 2. Of those that a mesh axis runs over, the one named last changes fastest.
Arguments:
- tokens: bfloat16 [4, 2048, 1600], P('fsdp', 'ctx'), may hold values from -6 to 6
- out_grad: bfloat16 [4, 2048, 1600], P('fsdp', 'ctx'), may hold values from -6 to 6
- teacher: bfloat16 [4, 2048, 1600], P('fsdp', 'ctx'), may hold values from -9 to 9
- valid: int32 [4, 2048], P('fsdp', 'ctx'), may hold values from 0 to 1, as said below
- w_query: bfloat16 [1600, 1600], P('ctx', 'fsdp'), may hold values from -0.15625 to 0.15625
- w_keyval: bfloat16 [1600, 640], P('ctx', 'fsdp'), may hold values from -0.15625 to 0.15625
- w_attn_out: bfloat16 [1600, 1600], P('ctx', 'fsdp'), may hold values from -0.15625 to 0.15625
- w_in: bfloat16 [1600, 6400], P('ctx', 'fsdp'), may hold values from -0.15625 to 0.15625
- w_mamba_out: bfloat16 [3200, 1600], P('ctx', 'fsdp'), may hold values from -0.109375 to 0.109375
- w_gate: bfloat16 [1600, 5504], P('ctx', 'fsdp'), may hold values from -0.15625 to 0.15625
- w_up: bfloat16 [1600, 5504], P('ctx', 'fsdp'), may hold values from -0.15625 to 0.15625
- w_down: bfloat16 [5504, 1600], P('ctx', 'fsdp'), may hold values from -0.078125 to 0.078125
- x_proj: bfloat16 [3200, 132], P(('ctx', 'fsdp')), may hold values from -0.109375 to 0.109375
- dt_proj: bfloat16 [3200, 100], P(('ctx', 'fsdp')), may hold values from -0.625 to 0.625
- a_log: bfloat16 [3200, 16], P(('ctx', 'fsdp')), may hold values from -9 to -1
- conv_taps: bfloat16 [3200, 4], P(('ctx', 'fsdp')), may hold values from -3 to 3
- conv_bias: bfloat16 [3200], P(('ctx', 'fsdp')), may hold values from -3 to 3
- dt_bias: bfloat16 [3200], P(('ctx', 'fsdp')), may hold values from -4.5 to -2
- skip_gain: bfloat16 [3200], P(('ctx', 'fsdp')), may hold values from 0.5 to 1.5
- norm_gains: bfloat16 [6400], P(('ctx', 'fsdp')), may hold values from 0.5 to 1.5
Outputs:
- loss: float32 [], replicated
- output: bfloat16 [4, 2048, 1600], P('fsdp', 'ctx')
- input_grad: float32 [4, 2048, 1600], P('fsdp', 'ctx')
- w_query_grad: float32 [1600, 1600], P('ctx', 'fsdp')
- w_keyval_grad: float32 [1600, 640], P('ctx', 'fsdp')
- w_attn_out_grad: float32 [1600, 1600], P('ctx', 'fsdp')
- w_in_grad: float32 [1600, 6400], P('ctx', 'fsdp')
- w_mamba_out_grad: float32 [3200, 1600], P('ctx', 'fsdp')
- w_gate_grad: float32 [1600, 5504], P('ctx', 'fsdp')
- w_up_grad: float32 [1600, 5504], P('ctx', 'fsdp')
- w_down_grad: float32 [5504, 1600], P('ctx', 'fsdp')
- x_proj_grad: float32 [3200, 132], P(('ctx', 'fsdp'))
- dt_proj_grad: float32 [3200, 100], P(('ctx', 'fsdp'))
- a_log_grad: float32 [3200, 16], P(('ctx', 'fsdp'))
- conv_taps_grad: float32 [3200, 4], P(('ctx', 'fsdp'))
- conv_bias_grad: float32 [3200], P(('ctx', 'fsdp'))
- dt_bias_grad: float32 [3200], P(('ctx', 'fsdp'))
- skip_gain_grad: float32 [3200], P(('ctx', 'fsdp'))
- norm_gains_grad: float32 [6400], P(('ctx', 'fsdp'))
The draws below stay inside these ranges and needn't reach their ends.
Inputs may be any that keep to these rules, and one draw needn't show every extreme that they name: `valid`: 1 marks a token that counts in the loss; the last token of every sequence counts.
All inputs are finite; a program needn't handle non-finite values.
Results may differ from the reference program's by a relative error of at most 0.014.
The reference program's roundings to bfloat16 on the way count: a program that leaves them out, or rounds other values in their place, can miss the bound.
Values may be sent and summed in bfloat16 or wider, within the bound.
A program may use at most 448 MiB of HBM per device.

```python
import jax
import jax.numpy as jnp
from jax import lax

D = 1600
H = 25
HD = 64
KVH = 5
WINDOW = 1024
DI = 3200
DS = 16
KC = 4
R = 100
FF = 5504
LENGTH = 2048
SEQS = 4


def draw_teacher(key, part):
    position = jnp.arange(LENGTH, dtype=jnp.int32).astype(jnp.float32)
    ramp = 1.0 + 2.0 * position / (LENGTH - 1)
    values = jnp.clip(jax.random.normal(key, (SEQS, LENGTH, D), jnp.float32), -3.0, 3.0) * ramp[None, :, None]
    return values.astype(jnp.bfloat16)


def draw_valid(key, part):
    position = jnp.arange(LENGTH, dtype=jnp.int32)
    limit = 300 + 600 * position // LENGTH
    drawn = jax.random.randint(key, (SEQS, LENGTH), 0, 1000, dtype=jnp.int32)
    marked = (drawn < limit[None, :]).astype(jnp.int32)
    return jnp.where(position[None, :] == LENGTH - 1, jnp.ones_like(marked), marked)


def level_of(own_key, dims, cuts, smallest, high):
    level = 1.0
    for dim, shards_of in cuts:
        steps = jax.random.uniform(jax.random.fold_in(jax.random.fold_in(own_key, 6), dim), (shards_of,), jnp.float32, smallest / len(cuts), high / len(cuts))
        level = level * jnp.repeat(jnp.exp(steps), dims[dim] // shards_of).reshape((-1,) + (1,) * (len(dims) - 1 - dim))
    return level


def scatter_about(own_key, dims, width, reach, cuts=(), kind=jnp.bfloat16):
    array = width * jax.random.normal(own_key, dims, jnp.float32)
    if cuts:
        array = array * level_of(own_key, dims, cuts, -0.22, 0.18)
    return jnp.clip(array, -reach, reach).astype(kind)


def setup_inputs(seed: int = 0) -> dict:
    seeds = jax.random.split(jax.random.key(seed), 21)
    return {
        "tokens": scatter_about(seeds[0], (SEQS, LENGTH, D), 1.0, 6.0, ((0, 4), (1, 8))),
        "out_grad": scatter_about(seeds[1], (SEQS, LENGTH, D), 1.0, 6.0, ((0, 4), (1, 8))),
        "teacher": draw_teacher(jax.random.fold_in(seeds[20], 71), 0),
        "valid": draw_valid(jax.random.fold_in(seeds[20], 71), 0),
        "w_query": scatter_about(seeds[4], (D, H * HD), D ** -0.5, 0.15625, ((0, 8), (1, 4))),
        "w_keyval": scatter_about(seeds[5], (D, 2 * KVH * HD), D ** -0.5, 0.15625, ((0, 8), (1, 4))),
        "w_attn_out": scatter_about(seeds[6], (H * HD, D), (H * HD) ** -0.5, 0.15625, ((0, 8), (1, 4))),
        "w_in": scatter_about(seeds[7], (D, 2 * DI), D ** -0.5, 0.15625, ((0, 8), (1, 4))),
        "w_mamba_out": scatter_about(seeds[8], (DI, D), DI ** -0.5, 0.109375, ((0, 8), (1, 4))),
        "w_gate": scatter_about(seeds[9], (D, FF), D ** -0.5, 0.15625, ((0, 8), (1, 4))),
        "w_up": scatter_about(seeds[10], (D, FF), D ** -0.5, 0.15625, ((0, 8), (1, 4))),
        "w_down": scatter_about(seeds[11], (FF, D), FF ** -0.5, 0.078125, ((0, 8), (1, 4))),
        "x_proj": scatter_about(seeds[12], (DI, R + 2 * DS), DI ** -0.5, 0.109375, ((0, 32),)),
        "dt_proj": scatter_about(seeds[13], (DI, R), R ** -0.5, 0.625, ((0, 32),)),
        "a_log": jnp.clip(-9.0 + 8.0 * jax.random.uniform(seeds[14], (DI, DS), jnp.float32) ** level_of(seeds[14], (DI, DS), ((0, 32),), -0.2, 0.2), -9.0, -1.0).astype(jnp.bfloat16),
        "conv_taps": scatter_about(seeds[15], (DI, KC), KC ** -0.5, 3.0, ((0, 32),)),
        "conv_bias": scatter_about(seeds[16], (DI,), 0.5, 3.0, ((0, 32),)),
        "dt_bias": jnp.clip(-4.5 + 2.5 * jax.random.uniform(seeds[17], (DI,), jnp.float32) ** level_of(seeds[17], (DI,), ((0, 32),), -0.2, 0.2), -4.5, -2.0).astype(jnp.bfloat16),
        "skip_gain": jnp.clip(0.5 + 1.0 * jax.random.uniform(seeds[18], (DI,), jnp.float32) ** level_of(seeds[18], (DI,), ((0, 32),), -0.2, 0.2), 0.5, 1.5).astype(jnp.bfloat16),
        "norm_gains": jnp.clip(1.0 + 0.1 * jax.random.normal(seeds[19], (4 * D,), jnp.float32), 0.5, 1.5).astype(jnp.bfloat16),
    }


@jax.custom_vjp
def low(v):
    return lax.optimization_barrier(v.astype(jnp.bfloat16)).astype(jnp.float32)

@jax.custom_vjp
def low_back(v):
    return v

def low_keep(v):
    return (low(v), None)

def low_pass(kept, grad):
    return (grad,)

def back_keep(v):
    return (v, None)

def back_low(kept, grad):
    return (low(grad),)
low.defvjp(low_keep, low_pass)
low_back.defvjp(back_keep, back_low)

def low_both(values):
    return low(low_back(values))

def matmul_high(left, right):
    return jnp.dot(left, right, precision=lax.Precision.HIGHEST, preferred_element_type=jnp.float32)

def rms_norm(values, gain_vec):
    return values * lax.rsqrt(lax.optimization_barrier(jnp.mean(values * values, axis=-1, keepdims=True)) + 1e-06) * gain_vec

def attend_block(block_index, query_block, keys_pad, values_pad):
    block_len = query_block.shape[0]
    start_row = block_index * block_len
    key_block = lax.dynamic_slice_in_dim(keys_pad, start_row, block_len + WINDOW, 0).reshape(block_len + WINDOW, KVH, HD)
    value_block = lax.dynamic_slice_in_dim(values_pad, start_row, block_len + WINDOW, 0).reshape(block_len + WINDOW, KVH, HD)
    query_pos = start_row + jnp.arange(block_len, dtype=jnp.int32)
    key_pos = start_row - WINDOW + jnp.arange(block_len + WINDOW, dtype=jnp.int32)
    distance = query_pos[:, None] - key_pos[None, :]
    visible = (distance >= 0) & (distance < WINDOW) & (key_pos[None, :] >= 0)
    scores = jnp.einsum('ikgd,jkd->kgij', query_block, key_block, precision=lax.Precision.HIGHEST) * HD ** (-0.5)
    scores = jnp.where(visible, low_back(scores), -1e+30)
    row_max = lax.optimization_barrier(jnp.max(scores, axis=-1, keepdims=True))
    exponent = jnp.exp(scores - row_max)
    prob_rows = low(exponent / lax.optimization_barrier(jnp.sum(exponent, axis=-1, keepdims=True)))
    mixed_heads = jnp.einsum('kgij,jkd->ikgd', prob_rows, value_block, precision=lax.Precision.HIGHEST)
    return mixed_heads.reshape(block_len, H * HD)

def attend(queries, key_rows, value_rows):
    length = queries.shape[0]
    block_len = min(512, length)
    group_size = H // KVH
    query_blocks = queries.reshape(length // block_len, block_len, KVH, group_size, HD)
    padding = jnp.zeros((WINDOW, KVH * HD), jnp.float32)
    keys_pad = jnp.concatenate([padding, key_rows], 0)
    values_pad = jnp.concatenate([padding, value_rows], 0)
    checked = jax.checkpoint(attend_block)
    outputs = lax.map(lambda block_item: checked(block_item[0], block_item[1], keys_pad, values_pad), (jnp.arange(length // block_len, dtype=jnp.int32), query_blocks))
    return outputs.reshape(length, H * HD)

def scan_rows(carry_state, block_item, a_mat):

    def advance(running, row_item):
        step_row, input_row, b_row, c_row = row_item
        running = jnp.exp(step_row[:, None] * a_mat) * running + (step_row * input_row)[:, None] * b_row[None, :]
        return (running, lax.optimization_barrier(jnp.sum(running * c_row[None, :], axis=1)))
    return lax.scan(advance, carry_state, block_item)

def mamba(x_in, x_proj, dt_proj, a_log, conv_taps, conv_bias, dt_bias, skip_gain):
    length = x_in.shape[0]
    padded = jnp.concatenate([jnp.zeros((KC - 1, DI), jnp.float32), x_in], 0)
    pre_conv = conv_bias
    for shift_index in range(KC):
        pre_conv = pre_conv + conv_taps[:, shift_index] * padded[shift_index:shift_index + length]
    ssm_in = jax.nn.silu(pre_conv)
    x_dbl = low_both(matmul_high(low(ssm_in), x_proj))
    dt_in = x_dbl[:, :R]
    b_sel = x_dbl[:, R:R + DS]
    c_sel = x_dbl[:, R + DS:]
    dt_pre = low_back(lax.dot_general(dt_in, dt_proj, (((1,), (1,)), ((), ())), precision=lax.Precision.HIGHEST, preferred_element_type=jnp.float32) + dt_bias)
    step_size = jax.nn.softplus(dt_pre)
    a_mat = -jnp.exp(a_log)
    block_rows = min(64, length)
    count_blocks = length // block_rows
    checked = jax.checkpoint(scan_rows)

    def scan_block(carry_state, block_item):
        return checked(carry_state, block_item, a_mat)

    def in_blocks(arrays):
        return arrays.reshape((count_blocks, block_rows) + arrays.shape[1:])
    final_state, outputs = lax.scan(scan_block, jnp.zeros((DI, DS), jnp.float32), (in_blocks(step_size), in_blocks(ssm_in), in_blocks(b_sel), in_blocks(c_sel)))
    return outputs.reshape(length, DI) + skip_gain * ssm_in

def layer_seq(hidden, params):
    w_query, w_keyval, w_attn_out, w_in, w_mamba_out, w_gate, w_up, w_down, x_proj, dt_proj, a_log, conv_taps, conv_bias, dt_bias, skip_gain, norm_gains = params
    gain_rows = norm_gains.reshape(4, D)
    normed = low(rms_norm(hidden, gain_rows[0]))
    queries = low_both(matmul_high(normed, w_query))
    keyval = low_both(matmul_high(normed, w_keyval))
    attn = low_both(attend(queries, keyval[:, :KVH * HD], keyval[:, KVH * HD:]))
    attn_proj = low_back(matmul_high(attn, w_attn_out))
    inner_proj = low_both(matmul_high(normed, w_in))
    ssm_out = mamba(inner_proj[:, :DI], x_proj, dt_proj, a_log, conv_taps, conv_bias, dt_bias, skip_gain)
    mixed = low(ssm_out * jax.nn.silu(inner_proj[:, DI:]))
    mamba_proj = low_back(matmul_high(mixed, w_mamba_out))
    residual = hidden + 0.5 * (rms_norm(attn_proj, gain_rows[1]) + rms_norm(mamba_proj, gain_rows[2]))
    ffn_in = low(rms_norm(residual, gain_rows[3]))
    gate_pre = low_back(matmul_high(ffn_in, w_gate))
    up_pre = low_back(matmul_high(ffn_in, w_up))
    hidden_act = low(jax.nn.silu(gate_pre) * up_pre)
    return residual + low_back(matmul_high(hidden_act, w_down))

def reference(tokens, out_grad, teacher, valid, w_query, w_keyval, w_attn_out, w_in, w_mamba_out, w_gate, w_up, w_down, x_proj, dt_proj, a_log, conv_taps, conv_bias, dt_bias, skip_gain, norm_gains):
    params = tuple((weight.astype(jnp.float32) for weight in (w_query, w_keyval, w_attn_out, w_in, w_mamba_out, w_gate, w_up, w_down, x_proj, dt_proj, a_log, conv_taps, conv_bias, dt_bias, skip_gain, norm_gains)))
    hidden = tokens.astype(jnp.float32)
    targets = teacher.astype(jnp.float32)
    masks = valid.astype(jnp.float32)
    valid_count = jnp.sum(masks)
    checked = jax.checkpoint(layer_seq)

    def objective(hidden_all, param_set):

        def per_sequence(carried, seq_item):
            seq_in, seq_target, seq_mask = seq_item
            layer_out = checked(seq_in, param_set)
            mismatch = layer_out - seq_target
            return (carried + jnp.sum(seq_mask[:, None] * mismatch * mismatch), layer_out)
        error_sum, layer_all = lax.scan(per_sequence, jnp.zeros((), jnp.float32), (hidden_all, targets, masks))
        return (layer_all, error_sum / (valid_count * D))
    (layer_all, loss), pull_back = jax.vjp(objective, hidden, params)
    input_grad, grads = pull_back((out_grad.astype(jnp.float32), jnp.ones((), jnp.float32)))
    return (loss, layer_all.astype(jnp.bfloat16), input_grad, grads[0], grads[1], grads[2], grads[3], grads[4], grads[5], grads[6], grads[7], grads[8], grads[9], grads[10], grads[11], grads[12], grads[13], grads[14], grads[15])
```

```python
from typing import Any, NamedTuple

import jax
import jax.numpy as jnp
from jax import lax
from jax.experimental import pallas as pl
from jax.experimental.pallas import tpu as pltpu
from jax.sharding import PartitionSpec as P

D = 1600
H = 25
HD = 64
KVH = 5
WINDOW = 1024
DI = 3200
DS = 16
KC = 4
R = 100
LOG2E = 1.4426950408889634
BF = jnp.bfloat16
F32 = jnp.float32

TC = 128
LW = 512

def fold_rows(parts):
    row = lax.broadcasted_iota(jnp.int32, parts[0].shape, 0)
    for shift in (1, 2, 4):
        keep = (row & shift) == 0
        merged = []
        for first, second in zip(parts[0::2], parts[1::2]):
            stay = jnp.where(keep, first, second)
            move = jnp.where(keep, second, first)
            merged.append(stay + pltpu.roll(move, shift, 0))
        parts = merged
    return parts[0]

def spread(column, lanes):
    return jnp.concatenate([column] * (lanes // 128), 1)

def ssm_forward_kernel(step_ref, u_ref, b_ref, c_ref, rate_ref, y_ref, start_ref, state):
    @pl.when(pl.program_id(0) == 0)
    def _():
        state[...] = jnp.zeros_like(state)
    start_ref[0] = state[...]
    width = state.shape[1]
    lw = min(LW, width)
    for low in range(0, width, lw):
        lanes = slice(low, low + lw)
        rate = rate_ref[:, lanes]

        def group(index, running):
            row = pl.multiple_of(index * 8, 8)
            steps = step_ref[pl.ds(row, 8), lanes]
            drive = steps * u_ref[pl.ds(row, 8), lanes]
            sums = []
            for k in range(8):
                b_now, c_now = spread(b_ref[row + k], lw), spread(c_ref[row + k], lw)
                running = jnp.exp2(rate * steps[k : k + 1]) * running + b_now * drive[k : k + 1]
                seen = running * c_now
                sums.append(seen[:8] + seen[8:])
            y_ref[pl.ds(row, 8), lanes] = fold_rows(sums)
            return running

        state[:, lanes] = lax.fori_loop(0, TC // 8, group, state[:, lanes])

def ssm_forward(step, u, b_t, c_t, rate, parcels, number):
    length, width = step.shape
    states = rate.shape[0]
    count = length // TC
    rows = pl.BlockSpec((TC, width), lambda i: (i, 0))
    cols = pl.BlockSpec((TC, states, 128), lambda i: (i, 0, 0))
    return talk(
        ssm_forward_kernel,
        [step, u, b_t, c_t, rate],
        [rows, rows, cols, cols, pl.BlockSpec((states, width), lambda i: (0, 0))],
        [jax.ShapeDtypeStruct((length, width), jnp.float32), jax.ShapeDtypeStruct((count, states, width), jnp.float32)],
        [rows, pl.BlockSpec((1, states, width), lambda i: (i, 0, 0))],
        [pltpu.VMEM((states, width), jnp.float32)],
        parcels,
        number,
        32 << 20,
        "ssm_forward",
        steps=count,
    )

def lane_sums(values):
    high = values.astype(jnp.bfloat16)
    low = (values - high.astype(jnp.float32)).astype(jnp.bfloat16)
    ones = jnp.ones((8, values.shape[1]), jnp.bfloat16)
    dims = (((1,), (1,)), ((), ()))
    return lax.dot_general(ones, high, dims, preferred_element_type=jnp.float32) + lax.dot_general(
        ones, low, dims, preferred_element_type=jnp.float32
    )

def ssm_backward_kernel(
    step_ref, u_ref, dy_ref, b_ref, c_ref, rate_ref, amat_ref, start_ref,
    dstep_ref, along_ref, db_ref, dc_ref, da_ref,
    adjoint, history, decays, b_part, c_part,
):
    states, width = adjoint.shape
    lw = min(LW, width)

    @pl.when(pl.program_id(0) == 0)
    def _():
        adjoint[...] = jnp.zeros_like(adjoint)
        da_ref[...] = jnp.zeros_like(da_ref)

    for low in range(0, width, lw):
        lanes = slice(low, low + lw)
        rate = rate_ref[:, lanes]
        amat = amat_ref[:, lanes]

        def replay(index, running):
            row = pl.multiple_of(index * 8, 8)
            steps = step_ref[pl.ds(row, 8), lanes]
            drive = steps * u_ref[pl.ds(row, 8), lanes]
            for k in range(8):
                decay = jnp.exp2(rate * steps[k : k + 1])
                history[row + k] = running
                decays[row + k] = decay
                running = decay * running + spread(b_ref[row + k], lw) * drive[k : k + 1]
            return running

        final = lax.fori_loop(0, TC // 8, replay, start_ref[0, :, lanes])

        def group(index, carry):
            lam, grown, after = carry
            row = pl.multiple_of(TC - 8 - index * 8, 8)
            steps = step_ref[pl.ds(row, 8), lanes]
            inputs = u_ref[pl.ds(row, 8), lanes]
            drive = steps * inputs
            dys = dy_ref[pl.ds(row, 8), lanes]
            through_sums = [None] * 8
            along_sums = [None] * 8
            for k in reversed(range(8)):
                before = history[row + k]
                lam = lam + spread(c_ref[row + k], lw) * dys[k : k + 1]
                passed = lam * decays[row + k]
                through = passed * before
                grown = grown + through * steps[k : k + 1]
                scaled = through * amat
                through_sums[k] = scaled[:8] + scaled[8:]
                along = lam * spread(b_ref[row + k], lw)
                along_sums[k] = along[:8] + along[8:]
                b_term = lam * drive[k : k + 1]
                c_term = after * dys[k : k + 1]
                b_sum = b_term[:, :128]
                c_sum = c_term[:, :128]
                for more in range(128, lw, 128):
                    b_sum = b_sum + b_term[:, more : more + 128]
                    c_sum = c_sum + c_term[:, more : more + 128]
                place = pl.ds(pl.multiple_of((row + k) * states, states), states)
                if low == 0:
                    b_part[place, :] = b_sum
                    c_part[place, :] = c_sum
                else:
                    b_part[place, :] += b_sum
                    c_part[place, :] += c_sum
                lam = passed
                after = before
            along_all = fold_rows(along_sums)
            along_ref[pl.ds(row, 8), lanes] = along_all
            dstep_ref[pl.ds(row, 8), lanes] = fold_rows(through_sums) + inputs * along_all
            return lam, grown, after

        lam, grown, _ = lax.fori_loop(0, TC // 8, group, (adjoint[:, lanes], da_ref[:, lanes], final))
        adjoint[:, lanes] = lam
        da_ref[:, lanes] = grown
    db_ref[0] = lane_sums(b_part[...])
    dc_ref[0] = lane_sums(c_part[...])

def ssm_backward(step, u, dy, b_t, c_t, rate, amat, starts, parcels, number):
    length, width = step.shape
    states = rate.shape[0]
    count = length // TC
    last = count - 1
    lw = min(LW, width)
    rows = pl.BlockSpec((TC, width), lambda i: (last - i, 0))
    cols = pl.BlockSpec((TC, states, 128), lambda i: (last - i, 0, 0))
    whole = pl.BlockSpec((states, width), lambda i: (0, 0))
    sums = pl.BlockSpec((1, 8, TC * states), lambda i: (last - i, 0, 0))
    (dstep, along, db, dc, da), extra = talk(
        ssm_backward_kernel,
        [step, u, dy, b_t, c_t, rate, amat, starts],
        [rows, rows, rows, cols, cols, whole, whole, pl.BlockSpec((1, states, width), lambda i: (last - i, 0, 0))],
        [
            jax.ShapeDtypeStruct((length, width), jnp.float32),
            jax.ShapeDtypeStruct((length, width), jnp.float32),
            jax.ShapeDtypeStruct((count, 8, TC * states), jnp.float32),
            jax.ShapeDtypeStruct((count, 8, TC * states), jnp.float32),
            jax.ShapeDtypeStruct((states, width), jnp.float32),
        ],
        [rows, rows, sums, sums, whole],
        [
            pltpu.VMEM((states, width), jnp.float32),
            pltpu.VMEM((TC, states, lw), jnp.float32),
            pltpu.VMEM((TC, states, lw), jnp.float32),
            pltpu.VMEM((TC * states, 128), jnp.float32),
            pltpu.VMEM((TC * states, 128), jnp.float32),
        ],
        parcels,
        number,
        40 << 20,
        "ssm_backward",
        steps=count,
    )
    return dstep, along, db[:, 0].reshape(length, states), dc[:, 0].reshape(length, states), da, extra

QB = 256

def dot_nn(a, b):
    return lax.dot_general(a, b, (((1,), (0,)), ((), ())), preferred_element_type=jnp.float32)

def dot_nt(a, b):
    return lax.dot_general(a, b, (((1,), (1,)), ((), ())), preferred_element_type=jnp.float32)

def fill_bias(bias, first_key):
    span, queries = bias.shape
    key = first_key + lax.broadcasted_iota(jnp.int32, bias.shape, 0)
    query = pl.program_id(0) * queries + lax.broadcasted_iota(jnp.int32, bias.shape, 1)
    gap = query - key
    bias[...] = jnp.where((gap >= 0) & (gap < WINDOW), 0.0, -1e30)

def first_key_of(span):
    return pl.multiple_of(jnp.maximum(pl.program_id(0) * QB - (span - QB), 0), QB)

def slot_of(heads, j):
    first = heads * lax.axis_index("ctx")
    group = H // KVH
    return lax.div(jnp.minimum(first + j, H - 1), group) - lax.div(jnp.minimum(first, H - 1), group)

def attend_kernel(q_ref, k_ref, v_ref, o_ref, lse_ref, bias):
    span = bias.shape[0]
    first = first_key_of(span)
    fill_bias(bias, first)
    lse_ref[...] = jnp.zeros_like(lse_ref)

    def head(j, _):
        slot = slot_of(q_ref.shape[0] // HD, j)
        feats = pl.ds(pl.multiple_of(j * HD, HD), HD)
        scores = dot_nn(k_ref[slot, pl.ds(first, span), :], q_ref[feats, :]) + bias[...]
        top = jnp.max(scores, axis=0, keepdims=True)
        grown = jnp.exp(scores - top)
        total = jnp.sum(grown, axis=0, keepdims=True)
        probs = (grown * (1.0 / total)).astype(jnp.bfloat16)
        o_ref[feats, :] = dot_nn(v_ref[slot, :, pl.ds(first, span)], probs).astype(o_ref.dtype)
        lse_ref[pl.ds(j, 1), :] = top + jnp.log(total)
        return 0

    lax.fori_loop(0, q_ref.shape[0] // HD, head, 0)

def attend(q_t, k, v_t, parcels, number):
    feats, length = q_t.shape
    span = min(WINDOW + QB, length)
    tokens = pl.BlockSpec((feats, QB), lambda i: (0, i))
    whole = lambda a: pl.BlockSpec(a.shape, lambda i: (0,) * a.ndim)
    return talk(
        attend_kernel,
        [q_t, k, v_t],
        [tokens, whole(k), whole(v_t)],
        [jax.ShapeDtypeStruct((feats, length), jnp.bfloat16), jax.ShapeDtypeStruct((8, length), jnp.float32)],
        [tokens, pl.BlockSpec((8, QB), lambda i: (0, i))],
        [pltpu.VMEM((span, QB), jnp.float32)],
        parcels,
        number,
        40 << 20,
        "attend",
        steps=length // QB,
    )

def attend_back_kernel(q_ref, do_ref, k_ref, kt_ref, v_ref, lse_ref, dq_ref, dk_ref, dv_ref, bias):
    span = bias.shape[0]
    first = first_key_of(span)
    fill_bias(bias, first)

    @pl.when(pl.program_id(0) == 0)
    def _():
        dk_ref[...] = jnp.zeros_like(dk_ref)
        dv_ref[...] = jnp.zeros_like(dv_ref)

    def head(j, _):
        slot = slot_of(q_ref.shape[0] // HD, j)
        feats = pl.ds(pl.multiple_of(j * HD, HD), HD)
        keys = pl.ds(first, span)
        query = q_ref[feats, :]
        grad = do_ref[feats, :]
        probs = jnp.exp(dot_nn(k_ref[slot, keys, :], query) + bias[...] - lse_ref[pl.ds(j, 1), :])
        slopes = dot_nn(v_ref[slot, keys, :], grad)
        inner = jnp.sum(probs * slopes, axis=0, keepdims=True)
        ds = (probs * (slopes - inner)).astype(jnp.bfloat16)
        dq_ref[feats, :] = (dot_nn(kt_ref[slot, :, keys], ds) * HD**-0.5).astype(dq_ref.dtype)
        dk_ref[slot, keys, :] += dot_nt(ds, query)
        dv_ref[slot, keys, :] += dot_nt(probs.astype(jnp.bfloat16), grad)
        return 0

    lax.fori_loop(0, q_ref.shape[0] // HD, head, 0)

def attend_back(q_t, do_t, k, k_t, v, lse, parcels, number):
    feats, length = q_t.shape
    span = min(WINDOW + QB, length)
    tokens = pl.BlockSpec((feats, QB), lambda i: (0, i))
    whole = lambda a: pl.BlockSpec(a.shape, lambda i: (0,) * a.ndim)
    return talk(
        attend_back_kernel,
        [q_t, do_t, k, k_t, v, lse],
        [tokens, tokens, whole(k), whole(k_t), whole(v), pl.BlockSpec((8, QB), lambda i: (0, i))],
        [
            jax.ShapeDtypeStruct((feats, length), jnp.bfloat16),
            jax.ShapeDtypeStruct(k.shape, jnp.float32),
            jax.ShapeDtypeStruct(k.shape, jnp.float32),
        ],
        [tokens, whole(k), whole(k)],
        [pltpu.VMEM((span, QB), jnp.float32)],
        parcels,
        number,
        40 << 20,
        "attend_back",
        steps=length // QB,
    )


def contract(left, right, left_dim, right_dim):
    return lax.dot_general(left, right, (((left_dim,), (right_dim,)), ((), ())), preferred_element_type=F32)


def matmul(left, right):
    return contract(left, right, 1, 0)


def matmul_tn(left, right):
    return contract(left, right, 0, 0)


def matmul_nt(left, right):
    return contract(left, right, 1, 1)


def norm_forward(values, gain_vec):
    factor = lax.rsqrt(jnp.mean(values * values, axis=-1, keepdims=True) + 1e-06)
    return (values * factor * gain_vec, factor)


def norm_backward(values, factor, gain_vec, grad_out):
    weighted = grad_out * gain_vec
    inner_mean = jnp.mean(weighted * values, axis=-1, keepdims=True)
    grad_in = factor * weighted - values * (factor * factor * factor) * inner_mean
    return (grad_in, jnp.sum(grad_out * values * factor, axis=0))


def silu_slope(values):
    sigmoid_v = jax.nn.sigmoid(values)
    return sigmoid_v * (1.0 + values * (1.0 - sigmoid_v))


def pad_to(array, size, dim):
    widths = [(0, 0)] * array.ndim
    widths[dim] = (0, size - array.shape[dim])
    return jnp.pad(array, widths)


MESH = pl.DeviceIdType.MESH


BULK = 9


class Parcel(NamedTuple):
    source: Any
    kind: str
    axis: str
    group: int
    pick: Any = None


class Line(NamedTuple):
    size: int
    me: Any
    device: Any


def line_of(axis, sizes):
    n, m = sizes
    if axis == "ctx":
        return Line(n, lax.axis_index("ctx"), lambda peer: {"ctx": peer})
    me = lax.axis_index("fsdp")
    if axis == "fsdp":
        return Line(m, me, lambda peer: {"fsdp": peer})
    half = m // 2
    own = lax.rem(me, half)
    return Line(half, own, lambda peer: {"fsdp": me - own + peer})


def parcel_shapes(parcels, sizes):
    n, m = sizes
    sizes_of = {"ctx": n, "fsdp": m, "pair": m // 2}
    shapes = []
    for parcel in parcels:
        source = shapes[parcel.source] if isinstance(parcel.source, int) else parcel.source
        size = sizes_of[parcel.axis]
        shape = source.shape
        if parcel.kind == "gather":
            shape = (size,) + shape
        elif parcel.kind == "lanes":
            shape = shape[:-1] + (size * shape[-1],)
        elif parcel.pick is not None:
            shape = (size,) + parcel.pick(None, None, shape)
        shapes.append(jax.ShapeDtypeStruct(shape, source.dtype))
    return shapes


class Mail:
    def __init__(self, parcels, sizes, in_refs, out_refs, sems):
        self.parcels, self.sizes, self.outs = parcels, sizes, out_refs
        self.send, self.recv, self.local = sems if sems else (None,) * 3
        given = iter(in_refs)
        self.sources = [out_refs[p.source] if isinstance(p.source, int) else next(given) for p in parcels]
        self.base = []
        total = 0
        for p in parcels:
            self.base.append(total)
            total += {"ctx": sizes[0], "fsdp": sizes[1], "pair": sizes[1] // 2}[p.axis]

    def parts(self, number, line, peer, owner):
        parcel, source, out = self.parcels[number], self.sources[number], self.outs[number]
        if parcel.kind == "swap":
            source = parcel.pick(source, peer, None) if parcel.pick else source.at[peer]
        if parcel.kind == "lanes":
            lanes = self.sources[number].shape[-1]
            spot = pl.ds(pl.multiple_of(owner * lanes, lanes), lanes)
            return source, out.at[(slice(None),) * (len(out.shape) - 1) + (spot,)]
        return source, out.at[owner]

    def copies(self, group, incoming):
        for number, parcel in enumerate(self.parcels):
            if parcel.group != group:
                continue
            line = line_of(parcel.axis, self.sizes)
            for d in range(1, line.size):
                peer = lax.rem(line.me + d, line.size)
                owner = lax.rem(line.me + line.size - d, line.size) if incoming else line.me
                source, target = self.parts(number, line, peer, owner)
                spot = self.base[number] + d
                yield pltpu.make_async_remote_copy(
                    src_ref=source,
                    dst_ref=target,
                    send_sem=self.send.at[spot],
                    recv_sem=self.recv.at[spot],
                    device_id=line.device(peer),
                    device_id_type=MESH,
                )

    def kept(self, group):
        for number, parcel in enumerate(self.parcels):
            if parcel.group == group:
                line = line_of(parcel.axis, self.sizes)
                source, target = self.parts(number, line, line.me, line.me)
                yield pltpu.make_async_copy(source, target, self.local.at[number])

    def start(self, group):
        for copy in self.copies(group, False):
            copy.start()
        for copy in self.kept(group):
            copy.start()

    def wait(self, group):
        for copy in self.copies(group, True):
            copy.wait_recv()
        for copy in self.copies(group, False):
            copy.wait_send()
        for copy in self.kept(group):
            copy.wait()

    def step(self, done, begun):
        if self.has(done):
            self.wait(done)
            if self.has(begun):
                self.start(begun)

    def begin(self):
        for group in (0, BULK):
            if self.has(group):
                self.start(group)

    def end(self, last):
        for group in (last, BULK):
            if self.has(group):
                self.wait(group)

    def has(self, group):
        return any(p.group == group for p in self.parcels)


def ctx_copy(source, target, send, recv, device):
    return pltpu.make_async_remote_copy(
        src_ref=source, dst_ref=target, send_sem=send, recv_sem=recv, device_id={"ctx": device}, device_id_type=MESH
    )


def line_place(n):
    me = lax.axis_index("ctx")
    core = lax.rem(me, 2)
    return me, core, me // 2, me + 1 - 2 * core


def greet(sizes, everyone, fsdp):
    n, m = sizes
    chips = n // 2
    me, core, chip, sibling = line_place(n)
    barrier = pltpu.get_barrier_semaphore()

    def hello(device):
        pl.semaphore_signal(barrier, inc=1, device_id=device, device_id_type=MESH)

    expected = 0
    if everyone:
        for d in range(1, n):
            hello({"ctx": lax.rem(me + d, n)})
        expected = n - 1
    else:
        hello({"ctx": sibling})

        @pl.when(chip > 0)
        def _():
            hello({"ctx": me - 2})

        @pl.when(chip < chips - 1)
        def _():
            hello({"ctx": me + 2})

        expected = 3 - (chip == 0).astype(jnp.int32) - (chip == chips - 1).astype(jnp.int32)
    if fsdp:
        own = lax.axis_index("fsdp")
        for d in range(1, m):
            hello({"fsdp": lax.rem(own + d, m)})
        expected = expected + m - 1
    pl.semaphore_wait(barrier, expected)


def talk(core_kernel, args, in_specs, out_shapes, out_specs, scratch, parcels, number, vmem, name, everyone=False, steps=0):
    sizes = (lax.axis_size("ctx"), lax.axis_size("fsdp"))
    arrays = [p.source for p in parcels if not isinstance(p.source, int)]
    shapes = parcel_shapes(parcels, sizes)
    total = sum({"ctx": sizes[0], "fsdp": sizes[1], "pair": sizes[1] // 2}[p.axis] for p in parcels)
    everyone = everyone or any(p.axis == "ctx" for p in parcels)
    fsdp = any(p.axis != "ctx" for p in parcels)
    anywhere = pl.BlockSpec(memory_space=pl.ANY)
    sems = []
    if parcels:
        sems = [pltpu.SemaphoreType.DMA((total,)), pltpu.SemaphoreType.DMA((total,)), pltpu.SemaphoreType.DMA((len(parcels),))]

    def kernel(*refs):
        refs = list(refs)
        take = lambda count: [refs.pop(0) for _ in range(count)]
        ins, mail_in, outs, mail_out = take(len(args)), take(len(arrays)), take(len(out_shapes)), take(len(shapes))
        own = take(len(scratch))
        mail = Mail(parcels, sizes, mail_in, mail_out, refs)
        if not steps:
            greet(sizes, everyone, fsdp)
            core_kernel(sizes[0], ins, outs, own, mail)
            return

        @pl.when(pl.program_id(0) == 0)
        def _():
            greet(sizes, everyone, fsdp)
            mail.begin()

        core_kernel(*ins, *outs, *own)

        @pl.when(pl.program_id(0) == steps - 1)
        def _():
            mail.end(0)

    results = pl.pallas_call(
        kernel,
        grid=(steps,) if steps else (),
        out_shape=list(out_shapes) + shapes,
        in_specs=list(in_specs) + [anywhere] * len(arrays),
        out_specs=list(out_specs) + [anywhere] * len(shapes),
        scratch_shapes=list(scratch) + sems,
        compiler_params=pltpu.CompilerParams(collective_id=number, has_side_effects=True, vmem_limit_bytes=vmem),
        name=name,
    )(*args, *arrays)
    return results[: len(out_shapes)], results[len(out_shapes) :]


def share_core(n, xs, outs, sems, mail):
    chips = n // 2
    me, core, chip, sibling = line_place(n)
    send, recv, side_send, side_recv, local = sems
    several = range(len(xs))
    ways = ((0, 1), (1, -1))

    def spot(hop, sign):
        held = chip - sign * hop
        onward = chip + sign
        have = (held >= 0) & (held < chips)
        return 2 * held, have, have & (onward >= 0) & (onward < chips), 2 * onward + core

    def line_copy(a, way, hop, source, block, device):
        return ctx_copy(source, outs[a].at[block], send.at[a, way, hop], recv.at[a, way, hop], device)

    def side_copy(a, way, hop, source, block):
        return ctx_copy(source, outs[a].at[block], side_send.at[a, way, hop], side_recv.at[a, way, hop], sibling)

    keeps = [pltpu.make_async_copy(xs[a], outs[a].at[me], local.at[a]) for a in several]
    for a in several:
        keeps[a].start()
        side_copy(a, 0, 0, xs[a], me).start()
    for hop in range(chips):
        for way, sign in ways:
            base, have, go, onward = spot(hop, sign)
            block = base + core
            if hop > 0:

                @pl.when(have)
                def _():
                    for a in several:
                        line_copy(a, way, hop - 1, xs[a], block, sibling).wait_recv()
                        side_copy(a, way, hop, outs[a].at[block], block).start()

            if hop < chips - 1:

                @pl.when(go)
                def _():
                    for a in several:
                        source = xs[a] if hop == 0 else outs[a].at[block]
                        line_copy(a, way, hop, source, block, onward).start()

        if hop == 0:
            mail.begin()
            mail.step(0, 1)
        if hop == 1:
            mail.step(1, 2)

    for hop in range(chips):
        for way, sign in ways:
            base, have, go, onward = spot(hop, sign)
            block = base + core
            other = base + 1 - core
            if hop > 0:

                @pl.when(have)
                def _():
                    for a in several:
                        side_copy(a, way, hop, outs[a].at[block], block).wait_send()
                        side_copy(a, way, hop, xs[a], other).wait_recv()

            if hop < chips - 1:

                @pl.when(go)
                def _():
                    for a in several:
                        line_copy(a, way, hop, xs[a], block, onward).wait_send()

    for a in several:
        side_copy(a, 0, 0, xs[a], me).wait_send()
        side_copy(a, 0, 0, xs[a], sibling).wait_recv()
        keeps[a].wait()
    mail.end(2)


def share_tokens(blocks, number, parcels=()):
    n = lax.axis_size("ctx")
    anywhere = pl.BlockSpec(memory_space=pl.ANY)
    count = len(blocks)
    return talk(
        share_core,
        blocks,
        [anywhere] * count,
        [jax.ShapeDtypeStruct((n,) + b.shape, b.dtype) for b in blocks],
        [anywhere] * count,
        [pltpu.SemaphoreType.DMA((count, 2, n // 2))] * 4 + [pltpu.SemaphoreType.DMA((count,))],
        list(parcels),
        number,
        16 << 20,
        "share_tokens",
    )


def reduce_core(n, ins, outs, own, mail):
    pairs = list(zip(ins[: len(ins) // 2], ins[len(ins) // 2 :]))
    o_ref = outs[0]
    total, to_side, from_side, inbox, side_send, side_recv, send, recv = own
    chips = n // 2
    me, core, chip, sibling = line_place(n)
    rows = o_ref.shape[0]

    def partial(block):
        place = pl.ds(pl.multiple_of(block * rows, rows), rows)
        return sum(jnp.dot(a[place, :], w[...], preferred_element_type=jnp.float32) for a, w in pairs)

    def side_copy(dest):
        return ctx_copy(to_side.at[dest], from_side.at[dest], side_send.at[dest], side_recv.at[dest], sibling)

    def line_copy(way, dest, onward):
        return ctx_copy(from_side.at[dest], inbox.at[dest + way], send.at[dest], recv.at[dest + way], onward)

    mail.begin()

    def begin(k, _):
        dest = jnp.where(chip >= chips // 2, k, chips - 1 - k)
        to_side[dest] = partial(2 * dest + 1 - core).astype(jnp.bfloat16)
        side_copy(dest).start()
        total[dest] = partial(2 * dest + core)
        return 0

    lax.fori_loop(0, chips, begin, 0)

    def spot(tick, way):
        far = (chips - 1 - chip) if way == 0 else chip
        k = tick - far
        dest = k if way == 0 else chips - 1 - k
        active = (k >= 0) & ((dest < chip) if way == 0 else (dest > chip))
        return far, k, dest, active, (me - 2 if way == 0 else me + 2)

    def advance(tick, _):
        for way in (0, 1):
            far, k, dest, active, onward = spot(tick, way)
            before = dest - 1 if way == 0 else dest + 1

            @pl.when(active)
            def _():
                side_copy(dest).wait_recv()
                total[dest] += from_side[dest].astype(jnp.float32)

                @pl.when(far > 0)
                def _():
                    line_copy(way, dest, onward).wait_recv()
                    total[dest] += inbox[dest + way].astype(jnp.float32)

                @pl.when((far == 0) & (k > 0))
                def _():
                    line_copy(way, before, onward).wait_send()

                from_side[dest] = total[dest].astype(jnp.bfloat16)
                line_copy(way, dest, onward).start()

        return 0

    lax.fori_loop(0, chips, advance, 0)
    side_copy(chip).wait_recv()
    total[chip] += from_side[chip].astype(jnp.float32)

    @pl.when(chip < chips - 1)
    def _():
        line_copy(0, chip, me - 2).wait_recv()
        total[chip] += inbox[chip].astype(jnp.float32)

    @pl.when(chip > 0)
    def _():
        line_copy(1, chip, me + 2).wait_recv()
        total[chip] += inbox[chip + 1].astype(jnp.float32)

    o_ref[...] = total[chip]

    def finish(tick, _):
        side_copy(tick).wait_send()
        for way in (0, 1):
            far, k, dest, active, onward = spot(tick, way)

            @pl.when(active & ((far > 0) | (k == chips - 2)))
            def _():
                line_copy(way, dest, onward).wait_send()

        return 0

    lax.fori_loop(0, chips, finish, 0)
    mail.end(0)


def reduce_tokens(lefts, rights, number, parcels=()):
    n = lax.axis_size("ctx")
    chips = n // 2
    rows, width = lefts[0].shape[0] // n, rights[0].shape[1]
    buffer = lambda *lead: pltpu.VMEM(lead + (rows, width), jnp.bfloat16)
    vmem = pl.BlockSpec(memory_space=pltpu.VMEM)

    outs, extra = talk(
        reduce_core,
        lefts + rights,
        [vmem] * (2 * len(lefts)),
        [jax.ShapeDtypeStruct((rows, width), jnp.float32)],
        [vmem],
        [pltpu.VMEM((chips, rows, width), jnp.float32), buffer(chips), buffer(chips), buffer(chips + 1)]
        + [pltpu.SemaphoreType.DMA((chips,))] * 3
        + [pltpu.SemaphoreType.DMA((chips + 1,))],
        list(parcels),
        number,
        56 << 20,
        "reduce_tokens",
    )
    return outs[0], extra


def total_core(n, ins, outs, own, mail):
    (x_ref,), (o_ref,) = ins, outs
    from_side, summed, inbox, outbox, side_send, side_recv, send, recv, out_send, out_recv, back_send, back_recv, local = own
    chips = n // 2
    me, core, chip, sibling = line_place(n)
    cols = outbox.shape[1]

    def place(ref, block):
        return ref.at[:, pl.ds(pl.multiple_of(block * cols, cols), cols)]

    def side_copy(d):
        dest = lax.rem(chip + d, chips)
        return ctx_copy(place(x_ref, 2 * dest + 1 - core), from_side.at[d], side_send.at[d], side_recv.at[d], sibling)

    def line_copy(d):
        return ctx_copy(summed.at[d], inbox.at[d], send.at[d], recv.at[d], lax.rem(me + 2 * d, n))

    def out_copy(d):
        return ctx_copy(outbox, place(o_ref, me), out_send.at[d], out_recv.at[d], lax.rem(me + 2 * d, n))

    order = list(range(1, chips)) + [0]
    for d in order:
        side_copy(d).start()
    mail.begin()
    for d in order:
        dest = lax.rem(chip + d, chips)
        side_copy(d).wait_recv()
        block = pl.ds(pl.multiple_of((2 * dest + core) * cols, cols), cols)
        summed[d] = x_ref[:, block] + from_side[d]
        if d:
            line_copy(d).start()
    result = summed[0]
    for d in range(1, chips):
        line_copy(d).wait_recv()
        result = result + inbox[d]
    outbox[...] = result.astype(jnp.bfloat16)
    keep = pltpu.make_async_copy(outbox, place(o_ref, me), local)
    keep.start()
    for d in range(1, chips):
        out_copy(d).start()
    side = ctx_copy(outbox, place(o_ref, me), back_send.at[0], back_recv.at[0], sibling)
    side.start()
    mail.step(0, 1)
    for d in range(1, chips):
        origin = lax.rem(me + n - 2 * d, n)
        ctx_copy(outbox, place(o_ref, origin), out_send.at[d], out_recv.at[d], origin).wait_recv()
        ctx_copy(place(o_ref, origin), place(o_ref, origin), back_send.at[d], back_recv.at[d], sibling).start()
    for d in range(chips):
        mine = lax.rem(me + n - 2 * d, n)
        theirs = lax.rem(sibling + n - 2 * d, n)
        ctx_copy(place(o_ref, mine), place(o_ref, mine), back_send.at[d], back_recv.at[d], sibling).wait_send()
        ctx_copy(outbox, place(o_ref, theirs), back_send.at[d], back_recv.at[d], sibling).wait_recv()
        side_copy(d).wait_send()
        if d:
            line_copy(d).wait_send()
            out_copy(d).wait_send()
    keep.wait()
    mail.end(1)


def total_columns(partial, number, parcels=()):
    n = lax.axis_size("ctx")
    chips = n // 2
    feats, length = partial.shape
    cols = length // n
    vmem = pl.BlockSpec(memory_space=pltpu.VMEM)
    outs, extra = talk(
        total_core,
        [partial],
        [vmem],
        [jax.ShapeDtypeStruct((feats, length), jnp.bfloat16)],
        [vmem],
        [pltpu.VMEM((chips, feats, cols), jnp.float32)] * 3
        + [pltpu.VMEM((feats, cols), jnp.bfloat16)]
        + [pltpu.SemaphoreType.DMA((chips,))] * 8
        + [pltpu.SemaphoreType.DMA],
        list(parcels),
        number,
        32 << 20,
        "total_columns",
        everyone=True,
    )
    return outs[0], extra


def send_core(n, ins, outs, own, mail):
    mail.begin()
    mail.step(0, 1)
    mail.end(1)


def send_only(parcels, number):
    return talk(send_core, [], [], [], [], [], list(parcels), number, 16 << 20, "send_only", everyone=True)[1]


def body(
    tokens,
    out_grad,
    teacher,
    valid,
    w_query,
    w_keyval,
    w_attn_out,
    w_in,
    w_mamba_out,
    w_gate,
    w_up,
    w_down,
    x_proj,
    dt_proj,
    a_log,
    conv_taps,
    conv_bias,
    dt_bias,
    skip_gain,
    norm_gains,
):
    n = lax.axis_size("ctx")
    m = lax.axis_size("fsdp")
    fsdp_index = lax.axis_index("fsdp")
    rows = tokens.shape[1]
    length = rows * n
    depth = w_in.shape[0]
    half = m // 2
    chunks = n // half
    chans = DI // n
    sub = chans // half
    subp = -(-sub // 128) * 128
    wide = half * subp
    units = w_down.shape[0]
    unit_sub = units // m
    unit_pad = -(-unit_sub // 16) * 16
    unit_wide = m * unit_pad
    heads = -(-H // n)
    group_size = H // KVH
    feats = -(-(R + 2 * DS) // 16) * 16
    slots = (heads + group_size - 2) // group_size + 1
    q_part = heads * HD // m
    kv_part = 2 * slots * HD // m
    head_pad = -(-(q_part + kv_part) // 128) * 128
    bases = [min(heads * c, H - 1) // group_size for c in range(n)]
    slot_heads = [[min(bases[c] + s, KVH - 1) for s in range(slots)] for c in range(n)]

    def wide_chans(array):
        array = array.reshape((half, sub) + array.shape[1:])
        return pad_to(array, subp, 1).reshape((wide,) + array.shape[2:])

    def true_chans(array):
        return array.reshape((half, subp) + array.shape[1:])[:, :sub].reshape((chans,) + array.shape[1:])

    mask_rows = valid[0].astype(F32)
    meta = jnp.stack([pad_to(norm_gains.astype(F32), 256, 0), jnp.full((256,), jnp.sum(mask_rows))])
    meta = pad_to(meta, 8, 0)
    in_send = pad_to(w_in.reshape(depth, chunks, half, sub).transpose(2, 1, 0, 3), subp, 3)
    head_send = jnp.concatenate([w_query, w_keyval], 1)
    ff_send = jnp.concatenate(
        [w.reshape(depth, n // m, m, unit_sub).transpose(2, 1, 0, 3) for w in (w_gate, w_up)], 3
    )
    small_send = jnp.concatenate(
        [x_proj, dt_proj, a_log, conv_taps, conv_bias[:, None], dt_bias[:, None], skip_gain[:, None]], 1
    )

    def by_chunk(ref, peer, shape):
        if ref is None:
            return shape[2:]
        return ref.at[lax.div(peer, chunks), lax.rem(peer, chunks)]

    (tokens_all, attn_rows), entry = share_tokens(
        [tokens[0], w_attn_out],
        0,
        [
            Parcel(in_send, "swap", "pair", 0),
            Parcel(meta, "gather", "fsdp", 0),
            Parcel(0, "swap", "ctx", 1, by_chunk),
            Parcel(1, "gather", "ctx", 1),
            Parcel(2, "lanes", "fsdp", 2),
            Parcel(head_send, "gather", "fsdp", BULK),
            Parcel(small_send, "gather", "fsdp", BULK),
            Parcel(ff_send, "swap", "fsdp", BULK),
        ],
    )
    meta_all, in_all, head_all, small_all, ff_all = entry[3:]
    gain_set = meta_all[:, :, 0, : norm_gains.shape[0]].reshape(4, D)
    valid_sum = jnp.sum(meta_all[:, :, 1, 0])
    in_weight = in_all.reshape(D, 2 * wide)
    small = wide_chans(small_all.reshape(chans, -1))
    xproj_weight = small[:, : R + 2 * DS]
    dtproj_weight = small[:, R + 2 * DS : 2 * R + 2 * DS]
    rest = small[:, 2 * R + 2 * DS :].astype(F32)
    amat = wide_chans(-jnp.exp(small_all.reshape(chans, -1)[:, 2 * R + 2 * DS : 2 * R + 3 * DS].astype(F32))).T
    rate = amat * LOG2E
    taps = rest[:, DS : DS + KC].T
    conv_bias_vec, dt_bias_vec, skip_vec = rest[:, DS + KC], rest[:, DS + KC + 1], rest[:, DS + KC + 2]
    query_rows = head_all[:, :, : w_query.shape[1]].transpose(1, 0, 2).reshape(depth, H * HD)
    query_rows = pad_to(query_rows, n * heads * HD, 1).reshape(depth, n, m, q_part)
    kv_rows = head_all[:, :, w_query.shape[1] :].transpose(1, 0, 2).reshape(depth, 2, KVH, HD)
    kv_rows = jnp.stack([jnp.stack([kv_rows[:, :, h] for h in slot_heads[c]], 2) for c in range(n)], 1)
    kv_rows = kv_rows.reshape(depth, n, m, kv_part)
    head_rows = lax.dynamic_index_in_dim(jnp.concatenate([query_rows, kv_rows], 3), fsdp_index, 2, False)
    head_rows = pad_to(head_rows.transpose(1, 0, 2), head_pad, 2)

    hidden = tokens[0].astype(F32)
    normed_all = norm_forward(tokens_all.reshape(length, D).astype(F32), gain_set[0])[0].astype(BF)
    factor_one = norm_forward(hidden, gain_set[0])[1]

    inner_low = matmul(normed_all, in_weight).astype(BF)
    x_branch = inner_low[:, :wide].astype(F32)
    z_branch = inner_low[:, wide:].astype(F32)
    padded = jnp.pad(x_branch, ((KC - 1, 0), (0, 0)))
    pre_conv = conv_bias_vec
    for k in range(KC):
        pre_conv = pre_conv + taps[k] * padded[k : k + length]
    ssm_in = jax.nn.silu(pre_conv)
    ssm_low = ssm_in.astype(BF)
    xdbl_t, (head_cols, head_cols_all) = total_columns(
        pad_to(contract(xproj_weight, ssm_low, 0, 1), feats, 0),
        1,
        [
            Parcel(head_rows, "swap", "ctx", 0),
            Parcel(0, "lanes", "fsdp", 1),
        ],
    )
    head_weight = head_cols_all.reshape(D, m, head_pad)
    query_weight = head_weight[:, :, :q_part].reshape(D, heads * HD)
    kv_weight = head_weight[:, :, q_part : q_part + kv_part].reshape(D, 2 * slots * HD)
    query_t = contract(query_weight, normed_all, 0, 1).astype(BF) * BF(HD**-0.5)
    kv = matmul(normed_all, kv_weight).astype(BF).reshape(length, 2, slots, HD)
    keys, values = kv[:, 0].transpose(1, 0, 2), kv[:, 1].transpose(1, 0, 2)
    (attn_part, lse), (mamba_all, down_all, ff_cols) = attend(
        query_t,
        keys,
        jnp.swapaxes(values, 1, 2),
        [
            Parcel(w_mamba_out, "gather", "fsdp", BULK),
            Parcel(w_down, "gather", "fsdp", BULK),
            Parcel(ff_all.reshape(n, depth, 2 * unit_sub), "swap", "ctx", BULK),
        ],
        11,
    )
    attn_part = attn_part.reshape(heads * HD, n, rows).transpose(1, 0, 2)
    mamba_weight = wide_chans(mamba_all.transpose(1, 0, 2).reshape(chans, D))
    down_weight = pad_to(down_all.transpose(1, 0, 2).reshape(m, unit_sub, D), unit_pad, 1).reshape(unit_wide, D)
    ff_parts = pad_to(ff_cols.reshape(D, 2, unit_sub).transpose(1, 2, 0), unit_pad, 1)

    dt_in_t = xdbl_t[:R]
    b_wide = jnp.broadcast_to(xdbl_t[R : R + DS].T.astype(F32)[:, :, None], (length, DS, 128))
    c_wide = jnp.broadcast_to(xdbl_t[R + DS : R + 2 * DS].T.astype(F32)[:, :, None], (length, DS, 128))
    dt_pre = contract(dt_in_t, dtproj_weight, 0, 1) + dt_bias_vec
    step_size = jax.nn.softplus(dt_pre)
    (state_rows, starts), (attn_t,) = ssm_forward(
        step_size, ssm_in, b_wide, c_wide, rate, [Parcel(attn_part, "swap", "ctx", BULK)], 12
    )
    ssm_out = state_rows + skip_vec * ssm_in
    gate_z = jax.nn.silu(z_branch)
    mixed_low = (ssm_out * gate_z).astype(BF)
    mamba_proj, (attn_weight_t,) = reduce_tokens(
        [mixed_low], [mamba_weight], 2, [Parcel(attn_rows.reshape(H * HD, -1).T, "gather", "fsdp", BULK)]
    )
    attn_t = attn_t.reshape(n * heads * HD, rows)[: H * HD]
    attn_weight_t = attn_weight_t.reshape(D, H * HD)
    attn_proj = contract(attn_t, attn_weight_t, 0, 1)

    attn_norm, factor_attn = norm_forward(attn_proj, gain_set[1])
    mamba_norm, factor_mamba = norm_forward(mamba_proj, gain_set[2])
    residual = hidden + 0.5 * (attn_norm + mamba_norm)
    ffn_in, factor_ffn = norm_forward(residual, gain_set[3])
    (ffn_all,), (gate_rows, up_rows) = share_tokens(
        [ffn_in.astype(BF)],
        3,
        [Parcel(ff_parts[0], "gather", "fsdp", BULK), Parcel(ff_parts[1], "gather", "fsdp", BULK)],
    )
    ffn_all = ffn_all.reshape(length, D)
    gate_rows, up_rows = gate_rows.reshape(unit_wide, D), up_rows.reshape(unit_wide, D)
    gate_pre = matmul_nt(ffn_all, gate_rows)
    up_pre = matmul_nt(ffn_all, up_rows)
    gate_act = jax.nn.silu(gate_pre)
    hidden_act = (gate_act * up_pre).astype(BF)
    layer_out = residual + reduce_tokens([hidden_act], [down_weight], 4)[0]

    mismatch = layer_out - teacher[0].astype(F32)
    error_part = jnp.sum(mask_rows[:, None] * mismatch * mismatch)
    grad_layer = out_grad[0].astype(F32) + 2.0 / (valid_sum * D) * mask_rows[:, None] * mismatch
    (grad_ffn_all,), _ = share_tokens([grad_layer.astype(BF)], 5)
    grad_ffn_all = grad_ffn_all.reshape(length, D)
    grad_act = matmul_nt(grad_ffn_all, down_weight)
    grad_gate = (grad_act * up_pre * silu_slope(gate_pre)).astype(BF)
    grad_up = (grad_act * gate_act).astype(BF)
    down_grad = matmul_tn(grad_ffn_all, hidden_act).astype(BF).reshape(m, D // m, unit_wide)
    grad_ffn_in, (down_grad,) = reduce_tokens(
        [grad_gate, grad_up], [gate_rows, up_rows], 6, [Parcel(down_grad, "swap", "fsdp", BULK)]
    )
    down_grad = jnp.sum(down_grad.astype(F32), 0).T.reshape(m, unit_pad, D // m)[:, :unit_sub].reshape(units, D // m)
    gate_grad, up_grad = [matmul_tn(g, ffn_all).astype(BF).reshape(m, unit_pad, D) for g in (grad_gate, grad_up)]

    grad_norm_res, gain_four = norm_backward(residual, factor_ffn, gain_set[3], grad_ffn_in)
    grad_resid = grad_layer + grad_norm_res
    half_grad = 0.5 * grad_resid
    grad_attn_proj, gain_two = norm_backward(attn_proj, factor_attn, gain_set[1], half_grad)
    grad_mamba_proj, gain_three = norm_backward(mamba_proj, factor_mamba, gain_set[2], half_grad)
    grad_attn_proj_low = grad_attn_proj.astype(BF)
    (grad_mamba_all,), (gate_grad, up_grad) = share_tokens(
        [grad_mamba_proj.astype(BF)],
        7,
        [Parcel(gate_grad, "swap", "fsdp", BULK), Parcel(up_grad, "swap", "fsdp", BULK)],
    )
    grad_mamba_all = grad_mamba_all.reshape(length, D)
    ff_grad = jnp.stack([jnp.sum(g.astype(F32), 0).astype(BF) for g in (gate_grad, up_grad)])
    ff_grad = ff_grad.reshape(2 * unit_pad, n, depth).transpose(1, 0, 2)
    attn_out_grad = contract(grad_attn_proj_low, attn_t, 0, 1).astype(BF).reshape(m, D // m, H * HD)
    grad_attn = contract(attn_weight_t, grad_attn_proj_low, 0, 1).astype(BF)
    grad_attn = pad_to(grad_attn, n * heads * HD, 0).reshape(n, heads * HD, rows)

    mamba_out_grad = matmul_tn(grad_mamba_all, mixed_low).astype(BF).reshape(m, D // m, wide)
    grad_mixed = matmul_nt(grad_mamba_all, mamba_weight)
    grad_y = grad_mixed * gate_z
    grad_z = grad_mixed * ssm_out * silu_slope(z_branch)
    z_grad = matmul_tn(normed_all, grad_z.astype(BF)).astype(BF)
    step_grad, along_b, b_grad, c_grad, a_accum, (attn_out_grad, grad_attn) = ssm_backward(
        step_size,
        ssm_in,
        grad_y,
        b_wide,
        c_wide,
        rate,
        amat,
        starts,
        [Parcel(attn_out_grad, "swap", "fsdp", BULK), Parcel(grad_attn, "swap", "ctx", BULK)],
        13,
    )
    attn_out_grad = jnp.sum(attn_out_grad.astype(F32), 0).T.astype(BF)
    attn_out_grad = lax.psum_scatter(attn_out_grad, "ctx", scatter_dimension=0, tiled=True).astype(F32)

    grad_attn = grad_attn.transpose(1, 0, 2).reshape(heads * HD, length)
    (grad_query, grad_keys, grad_values), (ff_grad, mamba_out_grad) = attend_back(
        query_t,
        grad_attn,
        keys,
        jnp.swapaxes(keys, 1, 2),
        values,
        lse,
        [Parcel(ff_grad, "swap", "ctx", BULK), Parcel(mamba_out_grad, "swap", "fsdp", BULK)],
        14,
    )
    grad_kv = jnp.stack([grad_keys, grad_values]).astype(BF).transpose(2, 0, 1, 3).reshape(length, 2 * slots * HD)
    mamba_out_grad = true_chans(jnp.sum(mamba_out_grad.astype(F32), 0).T)
    query_grad = contract(grad_query, normed_all, 1, 0).astype(BF).reshape(m, q_part, D)
    kv_grad = matmul_tn(grad_kv, normed_all).astype(BF).reshape(m, kv_part, D)

    grad_dt_pre = (step_grad * jax.nn.sigmoid(dt_pre)).astype(BF)
    dtproj_grad = contract(grad_dt_pre, dt_in_t, 0, 1)
    grad_xdbl_t = jnp.concatenate([contract(dtproj_weight, grad_dt_pre, 0, 1), b_grad.T, c_grad.T], 0)
    grad_xdbl_t, (query_grad, kv_grad) = total_columns(
        pad_to(grad_xdbl_t, feats, 0),
        8,
        [Parcel(query_grad, "swap", "fsdp", BULK), Parcel(kv_grad, "swap", "fsdp", BULK)],
    )
    grad_xdbl_t = grad_xdbl_t[: R + 2 * DS]
    head_grad = jnp.concatenate([jnp.sum(query_grad.astype(F32), 0), jnp.sum(kv_grad.astype(F32), 0)], 0)
    head_grad = pad_to(head_grad.astype(BF).T, head_pad, 1).reshape(n, depth, head_pad)
    xproj_grad = contract(ssm_low, grad_xdbl_t, 0, 1)
    grad_ssm_in = step_size * along_b + skip_vec * grad_y + contract(grad_xdbl_t, xproj_weight, 0, 1)
    grad_pre = grad_ssm_in * silu_slope(pre_conv)
    taps_grad = jnp.stack([jnp.sum(grad_pre * padded[k : k + length], axis=0) for k in range(KC)], 1)
    grad_after = jnp.pad(grad_pre, ((0, KC - 1), (0, 0)))
    grad_x = jnp.zeros_like(grad_pre)
    for k in range(KC):
        grad_x = grad_x + taps[k] * grad_after[KC - 1 - k : KC - 1 - k + length]
    x_grad = matmul_tn(normed_all, grad_x.astype(BF)).astype(BF)
    small_grad = jnp.concatenate(
        [
            xproj_grad,
            dtproj_grad,
            (a_accum * amat).T,
            taps_grad,
            jnp.sum(grad_pre, axis=0)[:, None],
            jnp.sum(grad_dt_pre.astype(F32), axis=0)[:, None],
            jnp.sum(grad_y * ssm_in, axis=0)[:, None],
        ],
        1,
    )
    small_grad = true_chans(small_grad).reshape(m, chans // m, -1)

    def by_lanes(ref, peer, shape):
        if ref is None:
            return (shape[0], subp)
        return ref.at[:, pl.ds(pl.multiple_of(peer * subp, subp), subp)]

    grad_normed, (ff_grad, small_grad, in_grad, head_grad) = reduce_tokens(
        [grad_query.T, grad_kv, grad_x.astype(BF), grad_z.astype(BF)],
        [query_weight.T, kv_weight.T, in_weight[:, :wide].T, in_weight[:, wide:].T],
        9,
        [
            Parcel(ff_grad.reshape(m, n // m, 2, unit_pad, depth), "swap", "fsdp", BULK),
            Parcel(small_grad, "swap", "fsdp", BULK),
            Parcel(jnp.concatenate([x_grad, z_grad], 1), "swap", "fsdp", BULK, by_lanes),
            Parcel(head_grad, "swap", "ctx", BULK),
        ],
    )
    ff_grad = ff_grad[:, :, :, :unit_sub].transpose(2, 4, 1, 0, 3)
    ff_grad = ff_grad.reshape(2, depth, units * n // m).astype(F32)
    small_grad = jnp.sum(small_grad, 0)
    in_grad = jnp.sum(in_grad.astype(F32), 0).astype(BF).reshape(n, depth, subp)

    grad_norm_in, gain_one = norm_backward(hidden, factor_one, gain_set[0], grad_normed)
    input_grad = grad_resid + grad_norm_in
    gain_grads = jnp.concatenate([gain_one, gain_two, gain_three, gain_four]).reshape(n, m, 1, -1)
    gain_grads = pad_to(gain_grads, 256, 3)
    meta_grad = pad_to(jnp.concatenate([gain_grads, jnp.full_like(gain_grads, error_part)], 2), 8, 2)

    def by_fsdp(ref, peer, shape):
        if ref is None:
            return (shape[0],) + shape[2:]
        return ref.at[:, peer]

    def by_run(ref, peer, shape):
        if ref is None:
            return (chunks,) + shape[1:]
        return ref.at[pl.ds(peer * chunks, chunks)]

    _, _, head_grad, meta_grad, in_grad = send_only(
        [
            Parcel(meta_grad, "swap", "ctx", 0),
            Parcel(in_grad, "swap", "ctx", 0),
            Parcel(head_grad, "gather", "fsdp", BULK),
            Parcel(0, "swap", "fsdp", 1, by_fsdp),
            Parcel(1, "swap", "pair", 1, by_run),
        ],
        10,
    )
    meta_grad = jnp.sum(meta_grad, (0, 1))
    gains_grad = meta_grad[0, : norm_gains.shape[0]]
    loss = meta_grad[1, 0] / (valid_sum * D)
    in_grad = in_grad[..., :sub].transpose(2, 1, 0, 3).reshape(depth, w_in.shape[1]).astype(F32)
    query_grad = head_grad[..., :q_part].transpose(2, 1, 0, 3).reshape(depth, n * heads * HD)
    query_grad = lax.dynamic_slice_in_dim(query_grad, fsdp_index * w_query.shape[1], w_query.shape[1], 1).astype(F32)
    kv_parts = head_grad[..., q_part : q_part + kv_part].astype(F32)
    kv_parts = kv_parts.transpose(1, 2, 0, 3).reshape(n, depth, 2, slots, HD)
    kv_sums = []
    for h in range(KVH):
        owners = [(c, h - bases[c]) for c in range(n) if 0 <= h - bases[c] < slots]
        kv_sums.append(sum(kv_parts[c, :, :, s] for c, s in owners))
    kv_grad = jnp.stack(kv_sums, 2).reshape(depth, 2 * KVH * HD)
    kv_grad = lax.dynamic_slice_in_dim(kv_grad, fsdp_index * w_keyval.shape[1], w_keyval.shape[1], 1)

    return (
        loss,
        layer_out.astype(BF)[None],
        input_grad[None],
        query_grad,
        kv_grad,
        attn_out_grad,
        in_grad,
        mamba_out_grad,
        ff_grad[0],
        ff_grad[1],
        down_grad,
        small_grad[:, : R + 2 * DS],
        small_grad[:, R + 2 * DS : 2 * R + 2 * DS],
        small_grad[:, 2 * R + 2 * DS : 2 * R + 3 * DS],
        small_grad[:, 2 * R + 3 * DS : 2 * R + 3 * DS + KC],
        small_grad[:, 2 * R + 3 * DS + KC],
        small_grad[:, 2 * R + 3 * DS + KC + 1],
        small_grad[:, 2 * R + 3 * DS + KC + 2],
        gains_grad,
    )


def solution(mesh):
    in_specs = (
        P("fsdp", "ctx", None),
        P("fsdp", "ctx", None),
        P("fsdp", "ctx", None),
        P("fsdp", "ctx"),
        P("ctx", "fsdp"),
        P("ctx", "fsdp"),
        P("ctx", "fsdp"),
        P("ctx", "fsdp"),
        P("ctx", "fsdp"),
        P("ctx", "fsdp"),
        P("ctx", "fsdp"),
        P("ctx", "fsdp"),
        P(("ctx", "fsdp"), None),
        P(("ctx", "fsdp"), None),
        P(("ctx", "fsdp"), None),
        P(("ctx", "fsdp"), None),
        P(("ctx", "fsdp")),
        P(("ctx", "fsdp")),
        P(("ctx", "fsdp")),
        P(("ctx", "fsdp")),
    )
    out_specs = (
        P(),
        P("fsdp", "ctx", None),
        P("fsdp", "ctx", None),
        P("ctx", "fsdp"),
        P("ctx", "fsdp"),
        P("ctx", "fsdp"),
        P("ctx", "fsdp"),
        P("ctx", "fsdp"),
        P("ctx", "fsdp"),
        P("ctx", "fsdp"),
        P("ctx", "fsdp"),
        P(("ctx", "fsdp"), None),
        P(("ctx", "fsdp"), None),
        P(("ctx", "fsdp"), None),
        P(("ctx", "fsdp"), None),
        P(("ctx", "fsdp")),
        P(("ctx", "fsdp")),
        P(("ctx", "fsdp")),
        P(("ctx", "fsdp")),
    )
    return jax.shard_map(body, mesh=mesh, in_specs=in_specs, out_specs=out_specs, check_vma=False)
```

```python
import functools
from typing import Any, NamedTuple

import jax
import jax.numpy as jnp
from jax import lax
from jax.experimental import pallas as pl
from jax.experimental.pallas import tpu as pltpu
from jax.sharding import PartitionSpec as P

D = 1600
H = 25
HD = 64
KVH = 5
WINDOW = 1024
DI = 3200
DS = 16
KC = 4
R = 100
LOG2E = 1.4426950408889634
BF = jnp.bfloat16
F32 = jnp.float32

TC = 128
LW = 512

def fold_rows(parts):
    row = lax.broadcasted_iota(jnp.int32, parts[0].shape, 0)
    for shift in (1, 2, 4):
        keep = (row & shift) == 0
        merged = []
        for first, second in zip(parts[0::2], parts[1::2]):
            stay = jnp.where(keep, first, second)
            move = jnp.where(keep, second, first)
            merged.append(stay + pltpu.roll(move, shift, 0))
        parts = merged
    return parts[0]

def spread(column, lanes):
    return jnp.concatenate([column.astype(jnp.float32)] * (lanes // 128), 1)

def ssm_forward_kernel(step_ref, u_ref, b_ref, c_ref, rate_ref, y_ref, start_ref, state):
    @pl.when(pl.program_id(0) == 0)
    def _():
        state[...] = jnp.zeros_like(state)
    start_ref[0] = state[...]
    width = state.shape[1]
    lw = min(LW, width)
    for low in range(0, width, lw):
        lanes = slice(low, low + lw)
        rate = rate_ref[:, lanes]

        def group(index, running):
            row = pl.multiple_of(index * 8, 8)
            steps = step_ref[pl.ds(row, 8), lanes]
            drive = steps * u_ref[pl.ds(row, 8), lanes]
            sums = []
            for k in range(8):
                b_now, c_now = spread(b_ref[row + k], lw), spread(c_ref[row + k], lw)
                running = jnp.exp2(rate * steps[k : k + 1]) * running + b_now * drive[k : k + 1]
                seen = running * c_now
                sums.append(seen[:8] + seen[8:])
            y_ref[pl.ds(row, 8), lanes] = fold_rows(sums)
            return running

        state[:, lanes] = lax.fori_loop(0, TC // 8, group, state[:, lanes])

def ssm_forward(step, u, b_t, c_t, rate, parcels, number):
    length, width = step.shape
    states = rate.shape[0]
    count = length // TC
    rows = pl.BlockSpec((TC, width), lambda i: (i, 0))
    cols = pl.BlockSpec((TC, states, 128), lambda i: (i, 0, 0))
    return talk(
        ssm_forward_kernel,
        [step, u, b_t, c_t, rate],
        [rows, rows, cols, cols, pl.BlockSpec((states, width), lambda i: (0, 0))],
        [jax.ShapeDtypeStruct((length, width), jnp.float32), jax.ShapeDtypeStruct((count, states, width), jnp.float32)],
        [rows, pl.BlockSpec((1, states, width), lambda i: (i, 0, 0))],
        [pltpu.VMEM((states, width), jnp.float32)],
        parcels,
        number,
        32 << 20,
        "ssm_forward",
        steps=count,
    )

def lane_sums(values):
    high = values.astype(jnp.bfloat16)
    low = (values - high.astype(jnp.float32)).astype(jnp.bfloat16)
    ones = jnp.ones((8, values.shape[1]), jnp.bfloat16)
    dims = (((1,), (1,)), ((), ()))
    return lax.dot_general(ones, high, dims, preferred_element_type=jnp.float32) + lax.dot_general(
        ones, low, dims, preferred_element_type=jnp.float32
    )

def ssm_backward_kernel(
    step_ref, u_ref, dy_ref, b_ref, c_ref, rate_ref, amat_ref, start_ref,
    dstep_ref, along_ref, db_ref, dc_ref, da_ref,
    adjoint, history, decays, b_part, c_part,
):
    states, width = adjoint.shape
    lw = min(LW, width)

    @pl.when(pl.program_id(0) == 0)
    def _():
        adjoint[...] = jnp.zeros_like(adjoint)
        da_ref[...] = jnp.zeros_like(da_ref)

    for low in range(0, width, lw):
        lanes = slice(low, low + lw)
        rate = rate_ref[:, lanes]
        amat = amat_ref[:, lanes]

        def replay(index, running):
            row = pl.multiple_of(index * 8, 8)
            steps = step_ref[pl.ds(row, 8), lanes]
            drive = steps * u_ref[pl.ds(row, 8), lanes]
            for k in range(8):
                decay = jnp.exp2(rate * steps[k : k + 1])
                history[row + k] = running
                decays[row + k] = decay
                running = decay * running + spread(b_ref[row + k], lw) * drive[k : k + 1]
            return running

        final = lax.fori_loop(0, TC // 8, replay, start_ref[0, :, lanes])

        def group(index, carry):
            lam, grown, after = carry
            row = pl.multiple_of(TC - 8 - index * 8, 8)
            steps = step_ref[pl.ds(row, 8), lanes]
            inputs = u_ref[pl.ds(row, 8), lanes]
            drive = steps * inputs
            dys = dy_ref[pl.ds(row, 8), lanes]
            through_sums = [None] * 8
            along_sums = [None] * 8
            for k in reversed(range(8)):
                before = history[row + k]
                lam = lam + spread(c_ref[row + k], lw) * dys[k : k + 1]
                passed = lam * decays[row + k]
                through = passed * before
                grown = grown + through * steps[k : k + 1]
                scaled = through * amat
                through_sums[k] = scaled[:8] + scaled[8:]
                along = lam * spread(b_ref[row + k], lw)
                along_sums[k] = along[:8] + along[8:]
                b_term = lam * drive[k : k + 1]
                c_term = after * dys[k : k + 1]
                b_sum = b_term[:, :128]
                c_sum = c_term[:, :128]
                for more in range(128, lw, 128):
                    b_sum = b_sum + b_term[:, more : more + 128]
                    c_sum = c_sum + c_term[:, more : more + 128]
                place = pl.ds(pl.multiple_of((row + k) * states, states), states)
                if low == 0:
                    b_part[place, :] = b_sum
                    c_part[place, :] = c_sum
                else:
                    b_part[place, :] += b_sum
                    c_part[place, :] += c_sum
                lam = passed
                after = before
            along_all = fold_rows(along_sums)
            along_ref[pl.ds(row, 8), lanes] = along_all
            dstep_ref[pl.ds(row, 8), lanes] = fold_rows(through_sums) + inputs * along_all
            return lam, grown, after

        lam, grown, _ = lax.fori_loop(0, TC // 8, group, (adjoint[:, lanes], da_ref[:, lanes], final))
        adjoint[:, lanes] = lam
        da_ref[:, lanes] = grown
    db_ref[0] = lane_sums(b_part[...])
    dc_ref[0] = lane_sums(c_part[...])

def ssm_backward(step, u, dy, b_t, c_t, rate, amat, starts, parcels, number):
    length, width = step.shape
    states = rate.shape[0]
    count = length // TC
    last = count - 1
    lw = min(LW, width)
    rows = pl.BlockSpec((TC, width), lambda i: (last - i, 0))
    cols = pl.BlockSpec((TC, states, 128), lambda i: (last - i, 0, 0))
    whole = pl.BlockSpec((states, width), lambda i: (0, 0))
    sums = pl.BlockSpec((1, 8, TC * states), lambda i: (last - i, 0, 0))
    (dstep, along, db, dc, da), extra = talk(
        ssm_backward_kernel,
        [step, u, dy, b_t, c_t, rate, amat, starts],
        [rows, rows, rows, cols, cols, whole, whole, pl.BlockSpec((1, states, width), lambda i: (last - i, 0, 0))],
        [
            jax.ShapeDtypeStruct((length, width), jnp.float32),
            jax.ShapeDtypeStruct((length, width), jnp.float32),
            jax.ShapeDtypeStruct((count, 8, TC * states), jnp.float32),
            jax.ShapeDtypeStruct((count, 8, TC * states), jnp.float32),
            jax.ShapeDtypeStruct((states, width), jnp.float32),
        ],
        [rows, rows, sums, sums, whole],
        [
            pltpu.VMEM((states, width), jnp.float32),
            pltpu.VMEM((TC, states, lw), jnp.float32),
            pltpu.VMEM((TC, states, lw), jnp.float32),
            pltpu.VMEM((TC * states, 128), jnp.float32),
            pltpu.VMEM((TC * states, 128), jnp.float32),
        ],
        parcels,
        number,
        40 << 20,
        "ssm_backward",
        steps=count,
    )
    return dstep, along, db[:, 0].reshape(length, states), dc[:, 0].reshape(length, states), da, extra

QB = 256

def dot_nn(a, b):
    return lax.dot_general(a, b, (((1,), (0,)), ((), ())), preferred_element_type=jnp.float32)

def dot_nt(a, b):
    return lax.dot_general(a, b, (((1,), (1,)), ((), ())), preferred_element_type=jnp.float32)

def fill_bias(bias, first_key):
    span, queries = bias.shape
    key = first_key + lax.broadcasted_iota(jnp.int32, bias.shape, 0)
    query = pl.program_id(0) * queries + lax.broadcasted_iota(jnp.int32, bias.shape, 1)
    gap = query - key
    bias[...] = jnp.where((gap >= 0) & (gap < WINDOW), 0.0, -1e30)

def first_key_of(span):
    return pl.multiple_of(jnp.maximum(pl.program_id(0) * QB - (span - QB), 0), QB)

def slot_of(heads, j):
    first = heads * lax.axis_index("ctx")
    group = H // KVH
    return lax.div(jnp.minimum(first + j, H - 1), group) - lax.div(jnp.minimum(first, H - 1), group)

def attend_kernel(q_ref, k_ref, v_ref, o_ref, lse_ref, bias):
    span = bias.shape[0]
    first = first_key_of(span)
    fill_bias(bias, first)
    lse_ref[...] = jnp.zeros_like(lse_ref)

    def head(j, _):
        slot = slot_of(q_ref.shape[0] // HD, j)
        feats = pl.ds(pl.multiple_of(j * HD, HD), HD)
        scores = dot_nn(k_ref[slot, pl.ds(first, span), :], q_ref[feats, :]) + bias[...]
        top = jnp.max(scores, axis=0, keepdims=True)
        grown = jnp.exp(scores - top)
        total = jnp.sum(grown, axis=0, keepdims=True)
        probs = (grown * (1.0 / total)).astype(jnp.bfloat16)
        o_ref[feats, :] = dot_nn(v_ref[slot, :, pl.ds(first, span)], probs).astype(o_ref.dtype)
        lse_ref[pl.ds(j, 1), :] = top + jnp.log(total)
        return 0

    lax.fori_loop(0, q_ref.shape[0] // HD, head, 0)

def attend(q_t, k, v_t, parcels, number):
    feats, length = q_t.shape
    span = min(WINDOW + QB, length)
    tokens = pl.BlockSpec((feats, QB), lambda i: (0, i))
    whole = lambda a: pl.BlockSpec(a.shape, lambda i: (0,) * a.ndim)
    return talk(
        attend_kernel,
        [q_t, k, v_t],
        [tokens, whole(k), whole(v_t)],
        [jax.ShapeDtypeStruct((feats, length), jnp.bfloat16), jax.ShapeDtypeStruct((8, length), jnp.float32)],
        [tokens, pl.BlockSpec((8, QB), lambda i: (0, i))],
        [pltpu.VMEM((span, QB), jnp.float32)],
        parcels,
        number,
        40 << 20,
        "attend",
        steps=length // QB,
    )

def attend_back_kernel(q_ref, do_ref, k_ref, kt_ref, v_ref, lse_ref, dq_ref, dk_ref, dv_ref, bias):
    span = bias.shape[0]
    first = first_key_of(span)
    fill_bias(bias, first)

    @pl.when(pl.program_id(0) == 0)
    def _():
        dk_ref[...] = jnp.zeros_like(dk_ref)
        dv_ref[...] = jnp.zeros_like(dv_ref)

    def head(j, _):
        slot = slot_of(q_ref.shape[0] // HD, j)
        feats = pl.ds(pl.multiple_of(j * HD, HD), HD)
        keys = pl.ds(first, span)
        query = q_ref[feats, :]
        grad = do_ref[feats, :]
        probs = jnp.exp(dot_nn(k_ref[slot, keys, :], query) + bias[...] - lse_ref[pl.ds(j, 1), :])
        slopes = dot_nn(v_ref[slot, keys, :], grad)
        inner = jnp.sum(probs * slopes, axis=0, keepdims=True)
        ds = (probs * (slopes - inner)).astype(jnp.bfloat16)
        dq_ref[feats, :] = (dot_nn(kt_ref[slot, :, keys], ds) * HD**-0.5).astype(dq_ref.dtype)
        dk_ref[slot, :, keys] += dot_nt(query, ds)
        dv_ref[slot, :, keys] += dot_nt(grad, probs.astype(jnp.bfloat16))
        return 0

    lax.fori_loop(0, q_ref.shape[0] // HD, head, 0)

def attend_back(q_t, do_t, k, k_t, v, lse, parcels, number):
    feats, length = q_t.shape
    span = min(WINDOW + QB, length)
    tokens = pl.BlockSpec((feats, QB), lambda i: (0, i))
    whole = lambda a: pl.BlockSpec(a.shape, lambda i: (0,) * a.ndim)
    return talk(
        attend_back_kernel,
        [q_t, do_t, k, k_t, v, lse],
        [tokens, tokens, whole(k), whole(k_t), whole(v), pl.BlockSpec((8, QB), lambda i: (0, i))],
        [
            jax.ShapeDtypeStruct((feats, length), jnp.bfloat16),
            jax.ShapeDtypeStruct(k_t.shape, jnp.float32),
            jax.ShapeDtypeStruct(k_t.shape, jnp.float32),
        ],
        [tokens, whole(k_t), whole(k_t)],
        [pltpu.VMEM((span, QB), jnp.float32)],
        parcels,
        number,
        40 << 20,
        "attend_back",
        steps=length // QB,
    )


def contract(left, right, left_dim, right_dim):
    return lax.dot_general(left, right, (((left_dim,), (right_dim,)), ((), ())), preferred_element_type=F32)


def matmul(left, right):
    return contract(left, right, 1, 0)


def matmul_tn(left, right):
    return contract(left, right, 0, 0)


def matmul_nt(left, right):
    return contract(left, right, 1, 1)


def norm_forward(values, gain_vec):
    factor = lax.rsqrt(jnp.mean(values * values, axis=-1, keepdims=True) + 1e-06)
    return (values * factor * gain_vec, factor)


def norm_backward(values, factor, gain_vec, grad_out):
    weighted = grad_out * gain_vec
    inner_mean = jnp.mean(weighted * values, axis=-1, keepdims=True)
    grad_in = factor * weighted - values * (factor * factor * factor) * inner_mean
    return (grad_in, jnp.sum(grad_out * values * factor, axis=0))


def silu_slope(values):
    sigmoid_v = jax.nn.sigmoid(values)
    return sigmoid_v * (1.0 + values * (1.0 - sigmoid_v))


def pad_to(array, size, dim):
    widths = [(0, 0)] * array.ndim
    widths[dim] = (0, size - array.shape[dim])
    return jnp.pad(array, widths)


MESH = pl.DeviceIdType.MESH


BULK = 9


class Parcel(NamedTuple):
    source: Any
    kind: str
    axis: str
    group: int
    pick: Any = None


class Line(NamedTuple):
    size: int
    me: Any
    device: Any


def line_of(axis, sizes):
    n, m = sizes
    if axis == "ctx":
        return Line(n, lax.axis_index("ctx"), lambda peer: {"ctx": peer})
    me = lax.axis_index("fsdp")
    if axis == "fsdp":
        return Line(m, me, lambda peer: {"fsdp": peer})
    half = m // 2
    own = lax.rem(me, half)
    return Line(half, own, lambda peer: {"fsdp": me - own + peer})


def parcel_shapes(parcels, sizes):
    n, m = sizes
    sizes_of = {"ctx": n, "fsdp": m, "pair": m // 2}
    shapes = []
    for parcel in parcels:
        source = shapes[parcel.source] if isinstance(parcel.source, int) else parcel.source
        size = sizes_of[parcel.axis]
        shape = source.shape
        if parcel.kind == "gather":
            shape = (size,) + shape
        elif parcel.kind == "lanes":
            shape = shape[:-1] + (size * shape[-1],)
        elif parcel.pick is not None:
            shape = (size,) + parcel.pick(None, None, shape)
        shapes.append(jax.ShapeDtypeStruct(shape, source.dtype))
    return shapes


class Mail:
    def __init__(self, parcels, sizes, in_refs, out_refs, sems):
        self.parcels, self.sizes, self.outs = parcels, sizes, out_refs
        self.send, self.recv, self.local = sems if sems else (None,) * 3
        given = iter(in_refs)
        self.sources = [out_refs[p.source] if isinstance(p.source, int) else next(given) for p in parcels]
        self.base = []
        total = 0
        for p in parcels:
            self.base.append(total)
            total += {"ctx": sizes[0], "fsdp": sizes[1], "pair": sizes[1] // 2}[p.axis]

    def parts(self, number, line, peer, owner):
        parcel, source, out = self.parcels[number], self.sources[number], self.outs[number]
        if parcel.kind == "swap":
            source = parcel.pick(source, peer, None) if parcel.pick else source.at[peer]
        if parcel.kind == "lanes":
            lanes = self.sources[number].shape[-1]
            spot = pl.ds(pl.multiple_of(owner * lanes, lanes), lanes)
            return source, out.at[(slice(None),) * (len(out.shape) - 1) + (spot,)]
        return source, out.at[owner]

    def copies(self, group, incoming):
        for number, parcel in enumerate(self.parcels):
            if parcel.group != group:
                continue
            line = line_of(parcel.axis, self.sizes)
            for d in range(1, line.size):
                peer = lax.rem(line.me + d, line.size)
                owner = lax.rem(line.me + line.size - d, line.size) if incoming else line.me
                source, target = self.parts(number, line, peer, owner)
                spot = self.base[number] + d
                yield pltpu.make_async_remote_copy(
                    src_ref=source,
                    dst_ref=target,
                    send_sem=self.send.at[spot],
                    recv_sem=self.recv.at[spot],
                    device_id=line.device(peer),
                    device_id_type=MESH,
                )

    def kept(self, group):
        for number, parcel in enumerate(self.parcels):
            if parcel.group == group:
                line = line_of(parcel.axis, self.sizes)
                source, target = self.parts(number, line, line.me, line.me)
                yield pltpu.make_async_copy(source, target, self.local.at[number])

    def start(self, group):
        for copy in self.copies(group, False):
            copy.start()
        for copy in self.kept(group):
            copy.start()

    def wait(self, group):
        for copy in self.copies(group, True):
            copy.wait_recv()
        for copy in self.copies(group, False):
            copy.wait_send()
        for copy in self.kept(group):
            copy.wait()

    def step(self, done, begun):
        if self.has(done):
            self.wait(done)
            if self.has(begun):
                self.start(begun)

    def begin(self):
        for group in (0, BULK):
            if self.has(group):
                self.start(group)

    def end(self, last):
        for group in (last, BULK):
            if self.has(group):
                self.wait(group)

    def has(self, group):
        return any(p.group == group for p in self.parcels)


def ctx_copy(source, target, send, recv, device):
    return pltpu.make_async_remote_copy(
        src_ref=source, dst_ref=target, send_sem=send, recv_sem=recv, device_id={"ctx": device}, device_id_type=MESH
    )


def line_place(n):
    me = lax.axis_index("ctx")
    core = lax.rem(me, 2)
    return me, core, me // 2, me + 1 - 2 * core


def greet(sizes, everyone, fsdp):
    n, m = sizes
    chips = n // 2
    me, core, chip, sibling = line_place(n)
    barrier = pltpu.get_barrier_semaphore()

    def hello(device):
        pl.semaphore_signal(barrier, inc=1, device_id=device, device_id_type=MESH)

    expected = 0
    if everyone:
        for d in range(1, n):
            hello({"ctx": lax.rem(me + d, n)})
        expected = n - 1
    else:
        hello({"ctx": sibling})

        @pl.when(chip > 0)
        def _():
            hello({"ctx": me - 2})

        @pl.when(chip < chips - 1)
        def _():
            hello({"ctx": me + 2})

        expected = 3 - (chip == 0).astype(jnp.int32) - (chip == chips - 1).astype(jnp.int32)
    if fsdp:
        own = lax.axis_index("fsdp")
        for d in range(1, m):
            hello({"fsdp": lax.rem(own + d, m)})
        expected = expected + m - 1
    pl.semaphore_wait(barrier, expected)


def talk(core_kernel, args, in_specs, out_shapes, out_specs, scratch, parcels, number, vmem, name, everyone=False, steps=0):
    sizes = (lax.axis_size("ctx"), lax.axis_size("fsdp"))
    arrays = [p.source for p in parcels if not isinstance(p.source, int)]
    shapes = parcel_shapes(parcels, sizes)
    total = sum({"ctx": sizes[0], "fsdp": sizes[1], "pair": sizes[1] // 2}[p.axis] for p in parcels)
    everyone = everyone or any(p.axis == "ctx" for p in parcels)
    fsdp = any(p.axis != "ctx" for p in parcels)
    anywhere = pl.BlockSpec(memory_space=pl.ANY)
    sems = []
    if parcels:
        sems = [pltpu.SemaphoreType.DMA((total,)), pltpu.SemaphoreType.DMA((total,)), pltpu.SemaphoreType.DMA((len(parcels),))]

    def kernel(*refs):
        refs = list(refs)
        take = lambda count: [refs.pop(0) for _ in range(count)]
        ins, mail_in, outs, mail_out = take(len(args)), take(len(arrays)), take(len(out_shapes)), take(len(shapes))
        own = take(len(scratch))
        mail = Mail(parcels, sizes, mail_in, mail_out, refs)
        if not steps:
            greet(sizes, everyone, fsdp)
            core_kernel(sizes[0], ins, outs, own, mail)
            return

        @pl.when(pl.program_id(0) == 0)
        def _():
            greet(sizes, everyone, fsdp)
            mail.begin()

        core_kernel(*ins, *outs, *own)

        @pl.when(pl.program_id(0) == steps - 1)
        def _():
            mail.end(0)

    results = pl.pallas_call(
        kernel,
        grid=(steps,) if steps else (),
        out_shape=list(out_shapes) + shapes,
        in_specs=list(in_specs) + [anywhere] * len(arrays),
        out_specs=list(out_specs) + [anywhere] * len(shapes),
        scratch_shapes=list(scratch) + sems,
        compiler_params=pltpu.CompilerParams(collective_id=number, has_side_effects=True, vmem_limit_bytes=vmem),
        name=name,
    )(*args, *arrays)
    return results[: len(out_shapes)], results[len(out_shapes) :]


def share_core(n, xs, outs, sems, mail):
    chips = n // 2
    me, core, chip, sibling = line_place(n)
    send, recv, side_send, side_recv, local = sems
    several = range(len(xs))
    ways = ((0, 1), (1, -1))

    def spot(hop, sign):
        held = chip - sign * hop
        onward = chip + sign
        have = (held >= 0) & (held < chips)
        return 2 * held, have, have & (onward >= 0) & (onward < chips), 2 * onward + core

    def line_copy(a, way, hop, source, block, device):
        return ctx_copy(source, outs[a].at[block], send.at[a, way, hop], recv.at[a, way, hop], device)

    def side_copy(a, way, hop, source, block):
        return ctx_copy(source, outs[a].at[block], side_send.at[a, way, hop], side_recv.at[a, way, hop], sibling)

    keeps = [pltpu.make_async_copy(xs[a], outs[a].at[me], local.at[a]) for a in several]
    for a in several:
        keeps[a].start()
        side_copy(a, 0, 0, xs[a], me).start()
    for hop in range(chips):
        for way, sign in ways:
            base, have, go, onward = spot(hop, sign)
            block = base + core
            if hop > 0:

                @pl.when(have)
                def _():
                    for a in several:
                        line_copy(a, way, hop - 1, xs[a], block, sibling).wait_recv()
                        side_copy(a, way, hop, outs[a].at[block], block).start()

            if hop < chips - 1:

                @pl.when(go)
                def _():
                    for a in several:
                        source = xs[a] if hop == 0 else outs[a].at[block]
                        line_copy(a, way, hop, source, block, onward).start()

        if hop == 0:
            mail.begin()
            mail.step(0, 1)
        if hop == 1:
            mail.step(1, 2)

    for hop in range(chips):
        for way, sign in ways:
            base, have, go, onward = spot(hop, sign)
            block = base + core
            other = base + 1 - core
            if hop > 0:

                @pl.when(have)
                def _():
                    for a in several:
                        side_copy(a, way, hop, outs[a].at[block], block).wait_send()
                        side_copy(a, way, hop, xs[a], other).wait_recv()

            if hop < chips - 1:

                @pl.when(go)
                def _():
                    for a in several:
                        line_copy(a, way, hop, xs[a], block, onward).wait_send()

    for a in several:
        side_copy(a, 0, 0, xs[a], me).wait_send()
        side_copy(a, 0, 0, xs[a], sibling).wait_recv()
        keeps[a].wait()
    mail.end(2)


def share_tokens(blocks, number, parcels=()):
    n = lax.axis_size("ctx")
    anywhere = pl.BlockSpec(memory_space=pl.ANY)
    count = len(blocks)
    return talk(
        share_core,
        blocks,
        [anywhere] * count,
        [jax.ShapeDtypeStruct((n,) + b.shape, b.dtype) for b in blocks],
        [anywhere] * count,
        [pltpu.SemaphoreType.DMA((count, 2, n // 2))] * 4 + [pltpu.SemaphoreType.DMA((count,))],
        list(parcels),
        number,
        16 << 20,
        "share_tokens",
    )


def feed_core(consume, n, ins, outs, own, mail):
    x_ref, given = ins[0], ins[1:]
    count = len(given)
    gathered, held, more = own[0], own[1 : 1 + count], own[1 + count : -6]
    send, recv, side_send, side_recv, local, load = own[-6:]
    chips = n // 2
    me, core, chip, sibling = line_place(n)

    def line_copy(way, hop, source, block, device):
        return ctx_copy(source, gathered.at[block], send.at[way, hop], recv.at[way, hop], device)

    def side_copy(way, hop, source, block):
        return ctx_copy(source, gathered.at[block], side_send.at[way, hop], side_recv.at[way, hop], sibling)

    def spot(hop, way):
        sign = 1 - 2 * way
        at = chip - sign * hop
        onward = chip + sign
        have = (at >= 0) & (at < chips)
        go = have & (onward >= 0) & (onward < chips)
        return 2 * at + core, 2 * at + 1 - core, have, go, 2 * onward + core

    keep = pltpu.make_async_copy(x_ref, gathered.at[me], local)
    keep.start()
    for way in (0, 1):
        _, _, _, go, onward = spot(0, way)

        @pl.when(go)
        def _():
            line_copy(way, 0, x_ref, me, onward).start()

    side_copy(0, 0, x_ref, me).start()
    loads = [pltpu.make_async_copy(source, target, load.at[i]) for i, (source, target) in enumerate(zip(given, held))]
    for copy in loads:
        copy.start()
    mail.begin()
    for copy in loads:
        copy.wait()
    keep.wait()

    def event(number, _):
        later = jnp.maximum(number - 2, 0)
        hop = 1 + lax.div(later, 4)
        kind = lax.rem(later, 4)
        way = lax.rem(kind, 2)

        @pl.when(number == 1)
        def _():
            side_copy(0, 0, x_ref, sibling).wait_recv()

        @pl.when((number >= 2) & (kind == 0))
        def _():
            for w in (0, 1):
                block, _, have, go, onward = spot(hop, w)

                @pl.when(have)
                def _():
                    line_copy(w, hop - 1, x_ref, block, sibling).wait_recv()
                    side_copy(w, hop, gathered.at[block], block).start()

                @pl.when(go)
                def _():
                    line_copy(w, hop, gathered.at[block], block, onward).start()

        block, other, have, _, _ = spot(hop, way)

        @pl.when((number >= 2) & (kind >= 2) & have)
        def _():
            side_copy(way, hop, x_ref, other).wait_recv()

        block = jnp.where(kind >= 2, other, block)
        block = jnp.where(number == 0, me, jnp.where(number == 1, sibling, block))

        @pl.when((number < 2) | have)
        def _():
            consume(block, gathered, held, outs, more, number == 0)

        return 0

    events = 2 + 4 * (chips - 1)
    lax.fori_loop(0, events, event, 0)
    consume(None, gathered, held, outs, more, None)
    for hop in range(chips):
        for way in (0, 1):
            block, other, have, go, onward = spot(hop, way)
            if hop > 0:

                @pl.when(have)
                def _():
                    side_copy(way, hop, gathered.at[block], block).wait_send()

            if hop < chips - 1:

                @pl.when(go)
                def _():
                    line_copy(way, hop, x_ref, block, onward).wait_send()

    side_copy(0, 0, x_ref, me).wait_send()
    mail.end(0)


def feed_tokens(block, number, consume, given, results, scratch, parcels=()):
    n = lax.axis_size("ctx")
    rows, width = block.shape
    vmem = pl.BlockSpec(memory_space=pltpu.VMEM)
    anywhere = pl.BlockSpec(memory_space=pl.ANY)
    return talk(
        functools.partial(feed_core, consume),
        [block] + list(given),
        [anywhere] * (1 + len(given)),
        list(results),
        [vmem] * len(results),
        [pltpu.VMEM((n, rows, width), block.dtype)]
        + [pltpu.VMEM(g.shape, g.dtype) for g in given]
        + list(scratch)
        + [pltpu.SemaphoreType.DMA((2, n // 2))] * 4
        + [pltpu.SemaphoreType.DMA, pltpu.SemaphoreType.DMA((len(given),))],
        list(parcels),
        number,
        56 << 20,
        "feed_tokens",
    )


def reduce_core(job, count, n, ins, outs, own, mail):
    terms = (len(ins) - count) // 2
    pairs = list(zip(ins[:terms], ins[terms : 2 * terms]))
    o_ref = outs[0]
    total, to_side, from_side, inbox, side_send, side_recv, send, recv = own
    chips = n // 2
    me, core, chip, sibling = line_place(n)
    rows = o_ref.shape[0]

    def partial(block):
        place = pl.ds(pl.multiple_of(block * rows, rows), rows)
        return sum(contract(a[place, :], w[...], 1, 0 if w.shape[0] == a.shape[1] else 1) for a, w in pairs)

    def side_copy(dest):
        return ctx_copy(to_side.at[dest], from_side.at[dest], side_send.at[dest], side_recv.at[dest], sibling)

    def line_copy(way, dest, onward):
        return ctx_copy(from_side.at[dest], inbox.at[dest + way], send.at[dest], recv.at[dest + way], onward)

    mail.begin()

    flip = chip >= chips // 2
    near = jnp.where(flip, chips - 1 - chip, chip)
    lead = chips - 1 - 2 * near

    def begin(k):
        later = jnp.maximum(k - lead, 0)
        high = chips - 1 - jnp.minimum(k, lead) - lax.div(later, 2)
        dest = jnp.where(lax.rem(later, 2) == 1, lax.div(later, 2), high)
        dest = jnp.where(flip, chips - 1 - dest, dest)
        to_side[dest] = partial(2 * dest + 1 - core).astype(jnp.bfloat16)
        side_copy(dest).start()
        total[dest] = partial(2 * dest + core)

    begin(0)

    def spot(tick, way):
        far = (chips - 1 - chip) if way == 0 else chip
        k = tick - far
        dest = k if way == 0 else chips - 1 - k
        active = (k >= 0) & ((dest < chip) if way == 0 else (dest > chip))
        return far, k, dest, active, (me - 2 if way == 0 else me + 2)

    def advance(tick, _):
        @pl.when(tick < chips - 1)
        def _():
            begin(tick + 1)

        for way in (0, 1):
            far, k, dest, active, onward = spot(tick, way)
            before = dest - 1 if way == 0 else dest + 1

            @pl.when(active)
            def _():
                side_copy(dest).wait_recv()
                total[dest] += from_side[dest].astype(jnp.float32)

                @pl.when(far > 0)
                def _():
                    line_copy(way, dest, onward).wait_recv()
                    total[dest] += inbox[dest + way].astype(jnp.float32)

                @pl.when((far == 0) & (k > 0))
                def _():
                    line_copy(way, before, onward).wait_send()

                from_side[dest] = total[dest].astype(jnp.bfloat16)
                line_copy(way, dest, onward).start()

        if job:
            job(tick, ins[: len(ins) - count], ins[len(ins) - count :], outs[1:])
        return 0

    lax.fori_loop(0, chips, advance, 0)
    side_copy(chip).wait_recv()
    total[chip] += from_side[chip].astype(jnp.float32)

    @pl.when(chip < chips - 1)
    def _():
        line_copy(0, chip, me - 2).wait_recv()
        total[chip] += inbox[chip].astype(jnp.float32)

    @pl.when(chip > 0)
    def _():
        line_copy(1, chip, me + 2).wait_recv()
        total[chip] += inbox[chip + 1].astype(jnp.float32)

    o_ref[...] = total[chip]

    def finish(tick, _):
        side_copy(tick).wait_send()
        for way in (0, 1):
            far, k, dest, active, onward = spot(tick, way)

            @pl.when(active & ((far > 0) | (k == chips - 2)))
            def _():
                line_copy(way, dest, onward).wait_send()

        return 0

    lax.fori_loop(0, chips, finish, 0)
    mail.end(0)


def reduce_tokens(lefts, rights, number, parcels=(), job=None, job_in=(), job_out=()):
    n = lax.axis_size("ctx")
    chips = n // 2
    rows, width = lefts[0].shape[0] // n, D
    buffer = lambda *lead: pltpu.VMEM(lead + (rows, width), jnp.bfloat16)
    vmem = pl.BlockSpec(memory_space=pltpu.VMEM)

    outs, extra = talk(
        functools.partial(reduce_core, job, len(job_in)),
        lefts + rights + list(job_in),
        [vmem] * (2 * len(lefts) + len(job_in)),
        [jax.ShapeDtypeStruct((rows, width), jnp.float32)] + list(job_out),
        [vmem] * (1 + len(job_out)),
        [pltpu.VMEM((chips, rows, width), jnp.float32), buffer(chips), buffer(chips), buffer(chips + 1)]
        + [pltpu.SemaphoreType.DMA((chips,))] * 3
        + [pltpu.SemaphoreType.DMA((chips + 1,))],
        list(parcels),
        number,
        (56 if chips <= 4 else 60) << 20,
        "reduce_tokens",
    )
    return outs, extra


def total_core(n, ins, outs, own, mail):
    (x_ref,), (o_ref,) = ins, outs
    from_side, summed, inbox, outbox, side_send, side_recv, send, recv, out_send, out_recv, back_send, back_recv, local = own
    chips = n // 2
    me, core, chip, sibling = line_place(n)
    cols = outbox.shape[1]

    def place(ref, block):
        return ref.at[:, pl.ds(pl.multiple_of(block * cols, cols), cols)]

    def side_copy(d):
        dest = lax.rem(chip + d, chips)
        return ctx_copy(place(x_ref, 2 * dest + 1 - core), from_side.at[d], side_send.at[d], side_recv.at[d], sibling)

    def line_copy(d):
        return ctx_copy(summed.at[d], inbox.at[d], send.at[d], recv.at[d], lax.rem(me + 2 * d, n))

    def out_copy(d):
        return ctx_copy(outbox, place(o_ref, me), out_send.at[d], out_recv.at[d], lax.rem(me + 2 * d, n))

    order = list(range(1, chips)) + [0]
    for d in order:
        side_copy(d).start()
    mail.begin()
    for d in order:
        dest = lax.rem(chip + d, chips)
        side_copy(d).wait_recv()
        block = pl.ds(pl.multiple_of((2 * dest + core) * cols, cols), cols)
        summed[d] = x_ref[:, block] + from_side[d]
        if d:
            line_copy(d).start()
    result = summed[0]
    for d in range(1, chips):
        line_copy(d).wait_recv()
        result = result + inbox[d]
    outbox[...] = result.astype(jnp.bfloat16)
    keep = pltpu.make_async_copy(outbox, place(o_ref, me), local)
    keep.start()
    for d in range(1, chips):
        out_copy(d).start()
    side = ctx_copy(outbox, place(o_ref, me), back_send.at[0], back_recv.at[0], sibling)
    side.start()
    mail.step(0, 1)
    for d in range(1, chips):
        origin = lax.rem(me + n - 2 * d, n)
        ctx_copy(outbox, place(o_ref, origin), out_send.at[d], out_recv.at[d], origin).wait_recv()
        ctx_copy(place(o_ref, origin), place(o_ref, origin), back_send.at[d], back_recv.at[d], sibling).start()
    for d in range(chips):
        mine = lax.rem(me + n - 2 * d, n)
        theirs = lax.rem(sibling + n - 2 * d, n)
        ctx_copy(place(o_ref, mine), place(o_ref, mine), back_send.at[d], back_recv.at[d], sibling).wait_send()
        ctx_copy(outbox, place(o_ref, theirs), back_send.at[d], back_recv.at[d], sibling).wait_recv()
        side_copy(d).wait_send()
        if d:
            line_copy(d).wait_send()
            out_copy(d).wait_send()
    keep.wait()
    mail.end(1)


def total_columns(partial, number, parcels=()):
    n = lax.axis_size("ctx")
    chips = n // 2
    feats, length = partial.shape
    cols = length // n
    vmem = pl.BlockSpec(memory_space=pltpu.VMEM)
    outs, extra = talk(
        total_core,
        [partial],
        [vmem],
        [jax.ShapeDtypeStruct((feats, length), jnp.bfloat16)],
        [vmem],
        [pltpu.VMEM((chips, feats, cols), jnp.float32)] * 3
        + [pltpu.VMEM((feats, cols), jnp.bfloat16)]
        + [pltpu.SemaphoreType.DMA((chips,))] * 8
        + [pltpu.SemaphoreType.DMA],
        list(parcels),
        number,
        32 << 20,
        "total_columns",
        everyone=True,
    )
    return outs[0], extra


def send_core(n, ins, outs, own, mail):
    mail.begin()
    mail.step(0, 1)
    mail.end(1)


def send_only(parcels, number):
    return talk(send_core, [], [], [], [], [], list(parcels), number, 16 << 20, "send_only", everyone=True)[1]


def body(
    tokens,
    out_grad,
    teacher,
    valid,
    w_query,
    w_keyval,
    w_attn_out,
    w_in,
    w_mamba_out,
    w_gate,
    w_up,
    w_down,
    x_proj,
    dt_proj,
    a_log,
    conv_taps,
    conv_bias,
    dt_bias,
    skip_gain,
    norm_gains,
):
    n = lax.axis_size("ctx")
    m = lax.axis_size("fsdp")
    fsdp_index = lax.axis_index("fsdp")
    rows = tokens.shape[1]
    length = rows * n
    depth = w_in.shape[0]
    half = m // 2
    chunks = n // half
    chans = DI // n
    sub = chans // half
    subp = -(-sub // 128) * 128
    wide = half * subp
    units = w_down.shape[0]
    unit_sub = units // m
    unit_pad = -(-unit_sub // 16) * 16
    unit_wide = m * unit_pad
    heads = -(-H // n)
    group_size = H // KVH
    feats = -(-(R + 2 * DS) // 16) * 16
    slots = (heads + group_size - 2) // group_size + 1
    q_part = heads * HD // m
    kv_part = 2 * slots * HD // m
    head_pad = -(-(q_part + kv_part) // 128) * 128
    bases = [min(heads * c, H - 1) // group_size for c in range(n)]
    slot_heads = [[min(bases[c] + s, KVH - 1) for s in range(slots)] for c in range(n)]

    def wide_chans(array):
        array = array.reshape((half, sub) + array.shape[1:])
        return pad_to(array, subp, 1).reshape((wide,) + array.shape[2:])

    def true_chans(array):
        return array.reshape((half, subp) + array.shape[1:])[:, :sub].reshape((chans,) + array.shape[1:])

    mask_rows = valid[0].astype(F32)
    meta = jnp.stack([pad_to(norm_gains.astype(F32), 256, 0), jnp.full((256,), jnp.sum(mask_rows))])
    meta = pad_to(meta, 8, 0)
    in_send = pad_to(w_in.reshape(depth, chunks, half, sub).transpose(2, 1, 0, 3), subp, 3)
    head_send = jnp.concatenate([w_query, w_keyval], 1)
    ff_send = jnp.concatenate(
        [pad_to(w.reshape(depth, n // m, m, unit_sub).transpose(2, 1, 0, 3), unit_pad, 3) for w in (w_gate, w_up)], 3
    )
    small_send = jnp.concatenate(
        [x_proj, dt_proj, a_log, conv_taps, conv_bias[:, None], dt_bias[:, None], skip_gain[:, None]], 1
    )

    def by_chunk(ref, peer, shape):
        if ref is None:
            return shape[2:]
        return ref.at[lax.div(peer, chunks), lax.rem(peer, chunks)]

    (tokens_all, attn_rows), entry = share_tokens(
        [tokens[0], w_attn_out],
        0,
        [
            Parcel(in_send, "swap", "pair", 0),
            Parcel(meta, "gather", "fsdp", 0),
            Parcel(0, "swap", "ctx", 1, by_chunk),
            Parcel(1, "gather", "ctx", 1),
            Parcel(2, "lanes", "fsdp", 2),
            Parcel(head_send, "gather", "fsdp", BULK),
            Parcel(small_send, "gather", "fsdp", BULK),
            Parcel(ff_send, "swap", "fsdp", BULK),
        ],
    )
    meta_all, in_all, head_all, small_all, ff_all = entry[3:]
    gain_set = meta_all[:, :, 0, : norm_gains.shape[0]].reshape(4, D)
    valid_sum = jnp.sum(meta_all[:, :, 1, 0])
    in_weight = in_all.reshape(D, 2 * wide)
    small = wide_chans(small_all.reshape(chans, -1))
    xproj_weight = small[:, : R + 2 * DS]
    dtproj_weight = small[:, R + 2 * DS : 2 * R + 2 * DS]
    rest = small[:, 2 * R + 2 * DS :].astype(F32)
    amat = wide_chans(-jnp.exp(small_all.reshape(chans, -1)[:, 2 * R + 2 * DS : 2 * R + 3 * DS].astype(F32))).T
    rate = amat * LOG2E
    taps = rest[:, DS : DS + KC].T
    conv_bias_vec, dt_bias_vec, skip_vec = rest[:, DS + KC], rest[:, DS + KC + 1], rest[:, DS + KC + 2]
    query_rows = head_all[:, :, : w_query.shape[1]].transpose(1, 0, 2).reshape(depth, H * HD)
    query_rows = pad_to(query_rows, n * heads * HD, 1).reshape(depth, n, m, q_part)
    kv_rows = head_all[:, :, w_query.shape[1] :].transpose(1, 0, 2).reshape(depth, 2, KVH, HD)
    kv_rows = jnp.stack([jnp.stack([kv_rows[:, :, h] for h in slot_heads[c]], 2) for c in range(n)], 1)
    kv_rows = kv_rows.reshape(depth, n, m, kv_part)
    head_rows = lax.dynamic_index_in_dim(jnp.concatenate([query_rows, kv_rows], 3), fsdp_index, 2, False)
    head_rows = pad_to(head_rows.transpose(1, 0, 2), head_pad, 2)

    hidden = tokens[0].astype(F32)
    normed_all = norm_forward(tokens_all.reshape(length, D).astype(F32), gain_set[0])[0].astype(BF)
    normed_all = lax.optimization_barrier(normed_all)
    factor_one = norm_forward(hidden, gain_set[0])[1]

    inner_low = matmul(normed_all, in_weight).astype(BF)
    x_branch = inner_low[:, :wide].astype(F32)
    z_branch = inner_low[:, wide:].astype(F32)
    padded = jnp.pad(x_branch, ((KC - 1, 0), (0, 0)))
    pre_conv = conv_bias_vec
    for k in range(KC):
        pre_conv = pre_conv + taps[k] * padded[k : k + length]
    ssm_in = jax.nn.silu(pre_conv)
    ssm_low = ssm_in.astype(BF)
    xdbl_t, (head_cols, head_cols_all) = total_columns(
        pad_to(contract(xproj_weight, ssm_low, 0, 1), feats, 0),
        1,
        [
            Parcel(head_rows, "swap", "ctx", 0),
            Parcel(0, "lanes", "fsdp", 1),
        ],
    )
    head_weight = head_cols_all.reshape(D, m * head_pad)

    head_t = contract(head_weight, normed_all, 0, 1).astype(BF).reshape(m, head_pad, length)
    query_t = head_t[:, :q_part].reshape(heads * HD, length) * BF(HD**-0.5)
    kv_t = head_t[:, q_part : q_part + kv_part].reshape(2, slots, HD, length)
    keys_t, values_t = kv_t[0], kv_t[1]
    keys, values = jnp.swapaxes(keys_t, 1, 2), jnp.swapaxes(values_t, 1, 2)
    (attn_part, lse), (mamba_all, ff_cols) = attend(
        query_t,
        keys,
        values_t,
        [
            Parcel(wide_chans(w_mamba_out).T, "gather", "fsdp", BULK),
            Parcel(ff_all.reshape(n, depth, 2 * unit_pad), "swap", "ctx", BULK),
        ],
        11,
    )
    attn_part = attn_part.reshape(heads * HD, n, rows).transpose(1, 0, 2)
    mamba_weight_t = mamba_all.reshape(D, wide)
    ff_parts = ff_cols.reshape(D, 2 * unit_pad).T.reshape(2, unit_pad, D)

    dt_in_t = xdbl_t[:R]
    b_wide = jnp.broadcast_to(xdbl_t[R : R + DS].T[:, :, None], (length, DS, 128))
    c_wide = jnp.broadcast_to(xdbl_t[R + DS : R + 2 * DS].T[:, :, None], (length, DS, 128))
    dt_pre = contract(dt_in_t, dtproj_weight, 0, 1) + dt_bias_vec
    step_size = jax.nn.softplus(dt_pre)
    down_send = pad_to(w_down.T.reshape(-1, m, unit_sub), unit_pad, 2).reshape(-1, unit_wide)
    (state_rows, starts), (attn_t, down_all) = ssm_forward(
        step_size,
        ssm_in,
        b_wide,
        c_wide,
        rate,
        [Parcel(attn_part, "swap", "ctx", BULK), Parcel(down_send, "gather", "fsdp", BULK)],
        12,
    )
    down_weight_t = down_all.reshape(D, unit_wide)
    ssm_out = state_rows + skip_vec * ssm_in
    gate_z = jax.nn.silu(z_branch)
    mixed_low = (ssm_out * gate_z).astype(BF)
    (mamba_proj,), (attn_weight_t,) = reduce_tokens(
        [mixed_low], [mamba_weight_t], 2, [Parcel(attn_rows.reshape(H * HD, -1).T, "gather", "fsdp", BULK)]
    )
    attn_t = attn_t.reshape(n * heads * HD, rows)[: H * HD]
    attn_weight_t = attn_weight_t.reshape(D, H * HD)
    attn_proj = contract(attn_t, attn_weight_t, 0, 1)

    attn_norm, factor_attn = norm_forward(attn_proj, gain_set[1])
    mamba_norm, factor_mamba = norm_forward(mamba_proj, gain_set[2])
    residual = hidden + 0.5 * (attn_norm + mamba_norm)
    ffn_in, factor_ffn = norm_forward(residual, gain_set[3])
    (ffn_all,), (gate_rows, up_rows) = share_tokens(
        [ffn_in.astype(BF)],
        3,
        [Parcel(ff_parts[0], "gather", "fsdp", BULK), Parcel(ff_parts[1], "gather", "fsdp", BULK)],
    )
    ffn_all = ffn_all.reshape(length, D)
    gate_rows, up_rows = gate_rows.reshape(unit_wide, D), up_rows.reshape(unit_wide, D)
    gate_pre = matmul_nt(ffn_all, gate_rows)
    up_pre = matmul_nt(ffn_all, up_rows)
    hidden_act = (jax.nn.silu(gate_pre) * up_pre).astype(BF)
    layer_out = residual + reduce_tokens([hidden_act], [down_weight_t], 4)[0][0]

    mismatch = layer_out - teacher[0].astype(F32)
    error_part = jnp.sum(mask_rows[:, None] * mismatch * mismatch)
    grad_layer = out_grad[0].astype(F32) + 2.0 / (valid_sum * D) * mask_rows[:, None] * mismatch

    def feed_forward_back(block, x, held, outs, more, first):
        if block is None:
            outs[2][...] = more[0][...].astype(BF).reshape(outs[2].shape)
            return
        place = pl.ds(pl.multiple_of(block * rows, rows), rows)
        weight, gates, ups, acts = held
        grad = x[block]
        slope = contract(grad, weight[...], 1, 0)
        gate, up = gates[place, :], ups[place, :]
        sigmoid_v = 1.0 / (1.0 + jnp.exp(-gate))
        outs[0][place, :] = (slope * up * (sigmoid_v * (1.0 + gate * (1.0 - sigmoid_v)))).astype(BF)
        outs[1][place, :] = (slope * (gate * sigmoid_v)).astype(BF)
        part = contract(grad, acts[place, :], 0, 0)

        @pl.when(first)
        def _():
            more[0][...] = part

        @pl.when(jnp.logical_not(first))
        def _():
            more[0][...] += part

    (grad_gate, grad_up, down_grad), _ = feed_tokens(
        grad_layer.astype(BF),
        5,
        feed_forward_back,
        [down_weight_t, gate_pre, up_pre, hidden_act],
        [jax.ShapeDtypeStruct((length, unit_wide), BF)] * 2 + [jax.ShapeDtypeStruct((m, D // m, unit_wide), BF)],
        [pltpu.VMEM((D, unit_wide), F32)],
    )
    grad_parts = [jax.ShapeDtypeStruct((m, unit_pad, D), BF)] * 2

    def unit_grads(tick, given, more, outs):
        for piece in range(m):

            @pl.when(tick == piece * n // (2 * m))
            def _():
                for left, out in zip(given, outs):
                    part = left[:, piece * unit_pad : (piece + 1) * unit_pad]
                    out[piece] = contract(part, more[0][...], 0, 0).astype(BF)

    inside = length * D <= 4 << 20
    reduced, (down_grad,) = reduce_tokens(
        [grad_gate, grad_up],
        [gate_rows, up_rows],
        6,
        [Parcel(down_grad, "swap", "fsdp", BULK)],
        unit_grads if inside else None,
        [ffn_all] if inside else [],
        grad_parts if inside else [],
    )
    grad_ffn_in = reduced[0]
    down_grad = jnp.sum(down_grad.astype(F32), 0).T.reshape(m, unit_pad, D // m)[:, :unit_sub].reshape(units, D // m)
    if inside:
        gate_grad, up_grad = reduced[1:]
    else:
        gate_grad, up_grad = [matmul_tn(g, ffn_all).astype(BF).reshape(m, unit_pad, D) for g in (grad_gate, grad_up)]

    grad_norm_res, gain_four = norm_backward(residual, factor_ffn, gain_set[3], grad_ffn_in)
    grad_resid = grad_layer + grad_norm_res
    half_grad = 0.5 * grad_resid
    grad_attn_proj, gain_two = norm_backward(attn_proj, factor_attn, gain_set[1], half_grad)
    grad_mamba_proj, gain_three = norm_backward(mamba_proj, factor_mamba, gain_set[2], half_grad)
    grad_attn_proj_low = grad_attn_proj.astype(BF)

    def state_space_back(block, x, held, outs, more, first):
        if block is None:
            outs[2][...] = more[0][...].astype(BF).reshape(outs[2].shape)
            return
        place = pl.ds(pl.multiple_of(block * rows, rows), rows)
        weight, z_part, rows_out, mixed = held
        grad = x[block]
        slope = contract(grad, weight[...], 1, 0)
        z = z_part[place, :].astype(F32)
        sigmoid_v = 1.0 / (1.0 + jnp.exp(-z))
        outs[0][place, :] = slope * (z * sigmoid_v)
        outs[1][place, :] = (slope * rows_out[place, :] * (sigmoid_v * (1.0 + z * (1.0 - sigmoid_v)))).astype(BF)
        part = contract(grad, mixed[place, :], 0, 0)

        @pl.when(first)
        def _():
            more[0][...] = part

        @pl.when(jnp.logical_not(first))
        def _():
            more[0][...] += part

    (grad_y, grad_z, mamba_out_grad), (gate_grad, up_grad) = feed_tokens(
        grad_mamba_proj.astype(BF),
        7,
        state_space_back,
        [mamba_weight_t, inner_low[:, wide:], ssm_out, mixed_low],
        [
            jax.ShapeDtypeStruct((length, wide), F32),
            jax.ShapeDtypeStruct((length, wide), BF),
            jax.ShapeDtypeStruct((m, D // m, wide), BF),
        ],
        [pltpu.VMEM((D, wide), F32)],
        [Parcel(gate_grad, "swap", "fsdp", BULK), Parcel(up_grad, "swap", "fsdp", BULK)],
    )
    ff_grad = jnp.stack([jnp.sum(g.astype(F32), 0).astype(BF) for g in (gate_grad, up_grad)])
    ff_grad = ff_grad.reshape(2 * unit_pad, n, depth).transpose(1, 0, 2)
    attn_out_grad = contract(grad_attn_proj_low, attn_t, 0, 1).astype(BF).reshape(m, D // m, H * HD)
    grad_attn = contract(attn_weight_t, grad_attn_proj_low, 0, 1).astype(BF)
    grad_attn = pad_to(grad_attn, n * heads * HD, 0).reshape(n, heads * HD, rows)

    z_grad = matmul_tn(normed_all, grad_z).astype(BF)
    step_grad, along_b, b_grad, c_grad, a_accum, (attn_out_grad, grad_attn) = ssm_backward(
        step_size,
        ssm_in,
        grad_y,
        b_wide,
        c_wide,
        rate,
        amat,
        starts,
        [Parcel(attn_out_grad, "swap", "fsdp", BULK), Parcel(grad_attn, "swap", "ctx", BULK)],
        13,
    )
    attn_out_grad = jnp.sum(attn_out_grad.astype(F32), 0).T.astype(BF)
    attn_out_grad = lax.psum_scatter(attn_out_grad, "ctx", scatter_dimension=0, tiled=True).astype(F32)

    grad_attn = grad_attn.transpose(1, 0, 2).reshape(heads * HD, length)
    (grad_query, grad_keys, grad_values), (ff_grad, mamba_out_grad) = attend_back(
        query_t,
        grad_attn,
        keys,
        keys_t,
        values,
        lse,
        [Parcel(ff_grad, "swap", "ctx", BULK), Parcel(mamba_out_grad, "swap", "fsdp", BULK)],
        14,
    )
    grad_kv = jnp.concatenate([grad_keys, grad_values], 0).astype(BF).reshape(m, kv_part, length)
    grad_head_t = jnp.concatenate([grad_query.reshape(m, q_part, length), grad_kv], 1)
    grad_head_t = pad_to(grad_head_t, head_pad, 1).reshape(m * head_pad, length)
    mamba_out_grad = true_chans(jnp.sum(mamba_out_grad.astype(F32), 0).T)
    head_grad = contract(grad_head_t, normed_all, 1, 0).astype(BF).reshape(m, head_pad, D)

    grad_dt_pre = (step_grad * jax.nn.sigmoid(dt_pre)).astype(BF)
    dtproj_grad = contract(grad_dt_pre, dt_in_t, 0, 1)
    grad_xdbl_t = jnp.concatenate([contract(dtproj_weight, grad_dt_pre, 0, 1), b_grad.T, c_grad.T], 0)
    grad_xdbl_t, (head_grad,) = total_columns(
        pad_to(grad_xdbl_t, feats, 0),
        8,
        [Parcel(head_grad, "swap", "fsdp", BULK)],
    )
    grad_xdbl_t = grad_xdbl_t[: R + 2 * DS]
    head_grad = jnp.sum(head_grad.astype(F32), 0).astype(BF).T.reshape(n, depth, head_pad)
    xproj_grad = contract(ssm_low, grad_xdbl_t, 0, 1)
    grad_ssm_in = step_size * along_b + skip_vec * grad_y + contract(grad_xdbl_t, xproj_weight, 0, 1)
    grad_pre = grad_ssm_in * silu_slope(pre_conv)
    taps_grad = jnp.stack([jnp.sum(grad_pre * padded[k : k + length], axis=0) for k in range(KC)], 1)
    grad_after = jnp.pad(grad_pre, ((0, KC - 1), (0, 0)))
    grad_x = jnp.zeros_like(grad_pre)
    for k in range(KC):
        grad_x = grad_x + taps[k] * grad_after[KC - 1 - k : KC - 1 - k + length]
    x_grad = matmul_tn(normed_all, grad_x.astype(BF)).astype(BF)
    small_grad = jnp.concatenate(
        [
            xproj_grad,
            dtproj_grad,
            (a_accum * amat).T,
            taps_grad,
            jnp.sum(grad_pre, axis=0)[:, None],
            jnp.sum(grad_dt_pre.astype(F32), axis=0)[:, None],
            jnp.sum(grad_y * ssm_in, axis=0)[:, None],
        ],
        1,
    )
    small_grad = true_chans(small_grad).reshape(m, chans // m, -1)

    def used(array, dim):
        if head_pad == q_part + kv_part:
            return array
        split = array.reshape(array.shape[:dim] + (m, head_pad) + array.shape[dim + 1 :])
        return lax.slice_in_dim(split, 0, q_part + kv_part, 1, dim + 1).reshape(
            array.shape[:dim] + (-1,) + array.shape[dim + 1 :]
        )

    def by_lanes(ref, peer, shape):
        if ref is None:
            return (shape[0], subp)
        return ref.at[:, pl.ds(pl.multiple_of(peer * subp, subp), subp)]

    (grad_normed,), (ff_grad, small_grad, in_grad, head_grad) = reduce_tokens(
        [used(grad_head_t, 0).T, grad_x.astype(BF), grad_z],
        [used(head_weight, 1), in_weight[:, :wide], in_weight[:, wide:]],
        9,
        [
            Parcel(ff_grad.reshape(m, n // m, 2, unit_pad, depth), "swap", "fsdp", BULK),
            Parcel(small_grad, "swap", "fsdp", BULK),
            Parcel(jnp.concatenate([x_grad, z_grad], 1), "swap", "fsdp", BULK, by_lanes),
            Parcel(head_grad, "swap", "ctx", BULK),
        ],
    )
    ff_grad = ff_grad[:, :, :, :unit_sub].transpose(2, 4, 1, 0, 3)
    ff_grad = ff_grad.reshape(2, depth, units * n // m).astype(F32)
    small_grad = jnp.sum(small_grad, 0)
    in_grad = jnp.sum(in_grad.astype(F32), 0).astype(BF).reshape(n, depth, subp)

    grad_norm_in, gain_one = norm_backward(hidden, factor_one, gain_set[0], grad_normed)
    input_grad = grad_resid + grad_norm_in
    gain_grads = jnp.concatenate([gain_one, gain_two, gain_three, gain_four]).reshape(n, m, 1, -1)
    gain_grads = pad_to(gain_grads, 256, 3)
    meta_grad = pad_to(jnp.concatenate([gain_grads, jnp.full_like(gain_grads, error_part)], 2), 8, 2)

    def by_fsdp(ref, peer, shape):
        if ref is None:
            return (shape[0],) + shape[2:]
        return ref.at[:, peer]

    def by_run(ref, peer, shape):
        if ref is None:
            return (chunks,) + shape[1:]
        return ref.at[pl.ds(peer * chunks, chunks)]

    _, _, head_grad, meta_grad, in_grad = send_only(
        [
            Parcel(meta_grad, "swap", "ctx", 0),
            Parcel(in_grad, "swap", "ctx", 0),
            Parcel(head_grad, "gather", "fsdp", BULK),
            Parcel(0, "swap", "fsdp", 1, by_fsdp),
            Parcel(1, "swap", "pair", 1, by_run),
        ],
        10,
    )
    meta_grad = jnp.sum(meta_grad, (0, 1))
    gains_grad = meta_grad[0, : norm_gains.shape[0]]
    loss = meta_grad[1, 0] / (valid_sum * D)
    in_grad = in_grad[..., :sub].transpose(2, 1, 0, 3).reshape(depth, w_in.shape[1]).astype(F32)
    query_grad = head_grad[..., :q_part].transpose(2, 1, 0, 3).reshape(depth, n * heads * HD)
    query_grad = lax.dynamic_slice_in_dim(query_grad, fsdp_index * w_query.shape[1], w_query.shape[1], 1).astype(F32)
    kv_parts = head_grad[..., q_part : q_part + kv_part].astype(F32)
    kv_parts = kv_parts.transpose(1, 2, 0, 3).reshape(n, depth, 2, slots, HD)
    kv_sums = []
    for h in range(KVH):
        owners = [(c, h - bases[c]) for c in range(n) if 0 <= h - bases[c] < slots]
        kv_sums.append(sum(kv_parts[c, :, :, s] for c, s in owners))
    kv_grad = jnp.stack(kv_sums, 2).reshape(depth, 2 * KVH * HD)
    kv_grad = lax.dynamic_slice_in_dim(kv_grad, fsdp_index * w_keyval.shape[1], w_keyval.shape[1], 1)

    return (
        loss,
        layer_out.astype(BF)[None],
        input_grad[None],
        query_grad,
        kv_grad,
        attn_out_grad,
        in_grad,
        mamba_out_grad,
        ff_grad[0],
        ff_grad[1],
        down_grad,
        small_grad[:, : R + 2 * DS],
        small_grad[:, R + 2 * DS : 2 * R + 2 * DS],
        small_grad[:, 2 * R + 2 * DS : 2 * R + 3 * DS],
        small_grad[:, 2 * R + 3 * DS : 2 * R + 3 * DS + KC],
        small_grad[:, 2 * R + 3 * DS + KC],
        small_grad[:, 2 * R + 3 * DS + KC + 1],
        small_grad[:, 2 * R + 3 * DS + KC + 2],
        gains_grad,
    )


def solution(mesh):
    in_specs = (
        P("fsdp", "ctx", None),
        P("fsdp", "ctx", None),
        P("fsdp", "ctx", None),
        P("fsdp", "ctx"),
        P("ctx", "fsdp"),
        P("ctx", "fsdp"),
        P("ctx", "fsdp"),
        P("ctx", "fsdp"),
        P("ctx", "fsdp"),
        P("ctx", "fsdp"),
        P("ctx", "fsdp"),
        P("ctx", "fsdp"),
        P(("ctx", "fsdp"), None),
        P(("ctx", "fsdp"), None),
        P(("ctx", "fsdp"), None),
        P(("ctx", "fsdp"), None),
        P(("ctx", "fsdp")),
        P(("ctx", "fsdp")),
        P(("ctx", "fsdp")),
        P(("ctx", "fsdp")),
    )
    out_specs = (
        P(),
        P("fsdp", "ctx", None),
        P("fsdp", "ctx", None),
        P("ctx", "fsdp"),
        P("ctx", "fsdp"),
        P("ctx", "fsdp"),
        P("ctx", "fsdp"),
        P("ctx", "fsdp"),
        P("ctx", "fsdp"),
        P("ctx", "fsdp"),
        P("ctx", "fsdp"),
        P(("ctx", "fsdp"), None),
        P(("ctx", "fsdp"), None),
        P(("ctx", "fsdp"), None),
        P(("ctx", "fsdp"), None),
        P(("ctx", "fsdp")),
        P(("ctx", "fsdp")),
        P(("ctx", "fsdp")),
        P(("ctx", "fsdp")),
    )
    return jax.shard_map(body, mesh=mesh, in_specs=in_specs, out_specs=out_specs, check_vma=False)
```

```python
import functools
from typing import Any, NamedTuple

import jax
import jax.numpy as jnp
from jax import lax
from jax.experimental import pallas as pl
from jax.experimental.pallas import tpu as pltpu
from jax.sharding import PartitionSpec as P

D = 1600
H = 25
HD = 64
KVH = 5
WINDOW = 1024
DI = 3200
DS = 16
KC = 4
R = 100
LOG2E = 1.4426950408889634
BF = jnp.bfloat16
F32 = jnp.float32

TC = 128
LW = 512

def fold_rows(parts):
    row = lax.broadcasted_iota(jnp.int32, parts[0].shape, 0)
    for shift in (1, 2, 4):
        keep = (row & shift) == 0
        merged = []
        for first, second in zip(parts[0::2], parts[1::2]):
            stay = jnp.where(keep, first, second)
            move = jnp.where(keep, second, first)
            merged.append(stay + pltpu.roll(move, shift, 0))
        parts = merged
    return parts[0]

def spread(column, lanes):
    return jnp.concatenate([column.astype(jnp.float32)] * (lanes // 128), 1)

def ssm_forward_kernel(step_ref, u_ref, b_ref, c_ref, rate_ref, y_ref, start_ref, state):
    @pl.when(pl.program_id(0) == 0)
    def _():
        state[...] = jnp.zeros_like(state)
    start_ref[0] = state[...]
    width = state.shape[1]
    lw = min(LW, width)
    for low in range(0, width, lw):
        lanes = slice(low, low + lw)
        rate = rate_ref[:, lanes]

        def group(index, running):
            row = pl.multiple_of(index * 8, 8)
            steps = step_ref[pl.ds(row, 8), lanes]
            drive = steps * u_ref[pl.ds(row, 8), lanes]
            sums = []
            for k in range(8):
                b_now, c_now = spread(b_ref[row + k], lw), spread(c_ref[row + k], lw)
                running = jnp.exp2(rate * steps[k : k + 1]) * running + b_now * drive[k : k + 1]
                seen = running * c_now
                sums.append(seen[:8] + seen[8:])
            y_ref[pl.ds(row, 8), lanes] = fold_rows(sums)
            return running

        state[:, lanes] = lax.fori_loop(0, TC // 8, group, state[:, lanes])

def ssm_forward(step, u, b_t, c_t, rate, parcels, number):
    length, width = step.shape
    states = rate.shape[0]
    count = length // TC
    rows = pl.BlockSpec((TC, width), lambda i: (i, 0))
    cols = pl.BlockSpec((TC, states, 128), lambda i: (i, 0, 0))
    return talk(
        ssm_forward_kernel,
        [step, u, b_t, c_t, rate],
        [rows, rows, cols, cols, pl.BlockSpec((states, width), lambda i: (0, 0))],
        [jax.ShapeDtypeStruct((length, width), jnp.float32), jax.ShapeDtypeStruct((count, states, width), jnp.float32)],
        [rows, pl.BlockSpec((1, states, width), lambda i: (i, 0, 0))],
        [pltpu.VMEM((states, width), jnp.float32)],
        parcels,
        number,
        32 << 20,
        "ssm_forward",
        steps=count,
    )

def lane_sums(values):
    high = values.astype(jnp.bfloat16)
    low = (values - high.astype(jnp.float32)).astype(jnp.bfloat16)
    ones = jnp.ones((8, values.shape[1]), jnp.bfloat16)
    dims = (((1,), (1,)), ((), ()))
    return lax.dot_general(ones, high, dims, preferred_element_type=jnp.float32) + lax.dot_general(
        ones, low, dims, preferred_element_type=jnp.float32
    )

def ssm_backward_kernel(
    step_ref, u_ref, dy_ref, b_ref, c_ref, rate_ref, amat_ref, start_ref,
    dstep_ref, along_ref, db_ref, dc_ref, da_ref,
    adjoint, history, decays, b_part, c_part,
):
    states, width = adjoint.shape
    lw = min(LW, width)

    @pl.when(pl.program_id(0) == 0)
    def _():
        adjoint[...] = jnp.zeros_like(adjoint)
        da_ref[...] = jnp.zeros_like(da_ref)

    for low in range(0, width, lw):
        lanes = slice(low, low + lw)
        rate = rate_ref[:, lanes]
        amat = amat_ref[:, lanes]

        def replay(index, running):
            row = pl.multiple_of(index * 8, 8)
            steps = step_ref[pl.ds(row, 8), lanes]
            drive = steps * u_ref[pl.ds(row, 8), lanes]
            for k in range(8):
                decay = jnp.exp2(rate * steps[k : k + 1])
                history[row + k] = running
                decays[row + k] = decay
                running = decay * running + spread(b_ref[row + k], lw) * drive[k : k + 1]
            return running

        final = lax.fori_loop(0, TC // 8, replay, start_ref[0, :, lanes])

        def group(index, carry):
            lam, grown, after = carry
            row = pl.multiple_of(TC - 8 - index * 8, 8)
            steps = step_ref[pl.ds(row, 8), lanes]
            inputs = u_ref[pl.ds(row, 8), lanes]
            drive = steps * inputs
            dys = dy_ref[pl.ds(row, 8), lanes]
            through_sums = [None] * 8
            along_sums = [None] * 8
            for k in reversed(range(8)):
                before = history[row + k]
                lam = lam + spread(c_ref[row + k], lw) * dys[k : k + 1]
                passed = lam * decays[row + k]
                through = passed * before
                grown = grown + through * steps[k : k + 1]
                scaled = through * amat
                through_sums[k] = scaled[:8] + scaled[8:]
                along = lam * spread(b_ref[row + k], lw)
                along_sums[k] = along[:8] + along[8:]
                b_term = lam * drive[k : k + 1]
                c_term = after * dys[k : k + 1]
                b_sum = b_term[:, :128]
                c_sum = c_term[:, :128]
                for more in range(128, lw, 128):
                    b_sum = b_sum + b_term[:, more : more + 128]
                    c_sum = c_sum + c_term[:, more : more + 128]
                place = pl.ds(pl.multiple_of((row + k) * states, states), states)
                if low == 0:
                    b_part[place, :] = b_sum
                    c_part[place, :] = c_sum
                else:
                    b_part[place, :] += b_sum
                    c_part[place, :] += c_sum
                lam = passed
                after = before
            along_all = fold_rows(along_sums)
            along_ref[pl.ds(row, 8), lanes] = along_all
            dstep_ref[pl.ds(row, 8), lanes] = fold_rows(through_sums) + inputs * along_all
            return lam, grown, after

        lam, grown, _ = lax.fori_loop(0, TC // 8, group, (adjoint[:, lanes], da_ref[:, lanes], final))
        adjoint[:, lanes] = lam
        da_ref[:, lanes] = grown
    db_ref[0] = lane_sums(b_part[...])
    dc_ref[0] = lane_sums(c_part[...])

def ssm_backward(step, u, dy, b_t, c_t, rate, amat, starts, parcels, number):
    length, width = step.shape
    states = rate.shape[0]
    count = length // TC
    last = count - 1
    lw = min(LW, width)
    rows = pl.BlockSpec((TC, width), lambda i: (last - i, 0))
    cols = pl.BlockSpec((TC, states, 128), lambda i: (last - i, 0, 0))
    whole = pl.BlockSpec((states, width), lambda i: (0, 0))
    sums = pl.BlockSpec((1, 8, TC * states), lambda i: (last - i, 0, 0))
    (dstep, along, db, dc, da), extra = talk(
        ssm_backward_kernel,
        [step, u, dy, b_t, c_t, rate, amat, starts],
        [rows, rows, rows, cols, cols, whole, whole, pl.BlockSpec((1, states, width), lambda i: (last - i, 0, 0))],
        [
            jax.ShapeDtypeStruct((length, width), jnp.float32),
            jax.ShapeDtypeStruct((length, width), jnp.float32),
            jax.ShapeDtypeStruct((count, 8, TC * states), jnp.float32),
            jax.ShapeDtypeStruct((count, 8, TC * states), jnp.float32),
            jax.ShapeDtypeStruct((states, width), jnp.float32),
        ],
        [rows, rows, sums, sums, whole],
        [
            pltpu.VMEM((states, width), jnp.float32),
            pltpu.VMEM((TC, states, lw), jnp.float32),
            pltpu.VMEM((TC, states, lw), jnp.float32),
            pltpu.VMEM((TC * states, 128), jnp.float32),
            pltpu.VMEM((TC * states, 128), jnp.float32),
        ],
        parcels,
        number,
        40 << 20,
        "ssm_backward",
        steps=count,
    )
    return dstep, along, db[:, 0].reshape(length, states), dc[:, 0].reshape(length, states), da, extra

QB = 256

def dot_nn(a, b):
    return lax.dot_general(a, b, (((1,), (0,)), ((), ())), preferred_element_type=jnp.float32)

def dot_nt(a, b):
    return lax.dot_general(a, b, (((1,), (1,)), ((), ())), preferred_element_type=jnp.float32)

def fill_bias(bias, first_key):
    span, queries = bias.shape
    key = first_key + lax.broadcasted_iota(jnp.int32, bias.shape, 0)
    query = pl.program_id(0) * queries + lax.broadcasted_iota(jnp.int32, bias.shape, 1)
    gap = query - key
    bias[...] = jnp.where((gap >= 0) & (gap < WINDOW), 0.0, -1e30)

def first_key_of(span):
    return pl.multiple_of(jnp.maximum(pl.program_id(0) * QB - (span - QB), 0), QB)

def slot_of(heads, j):
    first = heads * lax.axis_index("ctx")
    group = H // KVH
    return lax.div(jnp.minimum(first + j, H - 1), group) - lax.div(jnp.minimum(first, H - 1), group)

def attend_kernel(q_ref, k_ref, v_ref, o_ref, lse_ref, bias):
    span = bias.shape[0]
    first = first_key_of(span)
    fill_bias(bias, first)
    lse_ref[...] = jnp.zeros_like(lse_ref)

    def head(j, _):
        slot = slot_of(q_ref.shape[0] // HD, j)
        feats = pl.ds(pl.multiple_of(j * HD, HD), HD)
        scores = dot_nn(k_ref[slot, pl.ds(first, span), :], q_ref[feats, :]) + bias[...]
        top = jnp.max(scores, axis=0, keepdims=True)
        grown = jnp.exp(scores - top)
        total = jnp.sum(grown, axis=0, keepdims=True)
        probs = (grown * (1.0 / total)).astype(jnp.bfloat16)
        o_ref[feats, :] = dot_nn(v_ref[slot, :, pl.ds(first, span)], probs).astype(o_ref.dtype)
        lse_ref[pl.ds(j, 1), :] = top + jnp.log(total)
        return 0

    lax.fori_loop(0, q_ref.shape[0] // HD, head, 0)

def attend(q_t, k, v_t, parcels, number):
    feats, length = q_t.shape
    span = min(WINDOW + QB, length)
    tokens = pl.BlockSpec((feats, QB), lambda i: (0, i))
    whole = lambda a: pl.BlockSpec(a.shape, lambda i: (0,) * a.ndim)
    return talk(
        attend_kernel,
        [q_t, k, v_t],
        [tokens, whole(k), whole(v_t)],
        [jax.ShapeDtypeStruct((feats, length), jnp.bfloat16), jax.ShapeDtypeStruct((8, length), jnp.float32)],
        [tokens, pl.BlockSpec((8, QB), lambda i: (0, i))],
        [pltpu.VMEM((span, QB), jnp.float32)],
        parcels,
        number,
        40 << 20,
        "attend",
        steps=length // QB,
    )

def attend_back_kernel(q_ref, do_ref, k_ref, kt_ref, v_ref, lse_ref, dq_ref, dk_ref, dv_ref, bias):
    span = bias.shape[0]
    first = first_key_of(span)
    fill_bias(bias, first)

    @pl.when(pl.program_id(0) == 0)
    def _():
        dk_ref[...] = jnp.zeros_like(dk_ref)
        dv_ref[...] = jnp.zeros_like(dv_ref)

    def head(j, _):
        slot = slot_of(q_ref.shape[0] // HD, j)
        feats = pl.ds(pl.multiple_of(j * HD, HD), HD)
        keys = pl.ds(first, span)
        query = q_ref[feats, :]
        grad = do_ref[feats, :]
        probs = jnp.exp(dot_nn(k_ref[slot, keys, :], query) + bias[...] - lse_ref[pl.ds(j, 1), :])
        slopes = dot_nn(v_ref[slot, keys, :], grad)
        inner = jnp.sum(probs * slopes, axis=0, keepdims=True)
        ds = (probs * (slopes - inner)).astype(jnp.bfloat16)
        dq_ref[feats, :] = (dot_nn(kt_ref[slot, :, keys], ds) * HD**-0.5).astype(dq_ref.dtype)
        dk_ref[slot, :, keys] += dot_nt(query, ds)
        dv_ref[slot, :, keys] += dot_nt(grad, probs.astype(jnp.bfloat16))
        return 0

    lax.fori_loop(0, q_ref.shape[0] // HD, head, 0)

def attend_back(q_t, do_t, k, k_t, v, lse, parcels, number):
    feats, length = q_t.shape
    span = min(WINDOW + QB, length)
    tokens = pl.BlockSpec((feats, QB), lambda i: (0, i))
    whole = lambda a: pl.BlockSpec(a.shape, lambda i: (0,) * a.ndim)
    return talk(
        attend_back_kernel,
        [q_t, do_t, k, k_t, v, lse],
        [tokens, tokens, whole(k), whole(k_t), whole(v), pl.BlockSpec((8, QB), lambda i: (0, i))],
        [
            jax.ShapeDtypeStruct((feats, length), jnp.bfloat16),
            jax.ShapeDtypeStruct(k_t.shape, jnp.float32),
            jax.ShapeDtypeStruct(k_t.shape, jnp.float32),
        ],
        [tokens, whole(k_t), whole(k_t)],
        [pltpu.VMEM((span, QB), jnp.float32)],
        parcels,
        number,
        40 << 20,
        "attend_back",
        steps=length // QB,
    )


def contract(left, right, left_dim, right_dim):
    return lax.dot_general(left, right, (((left_dim,), (right_dim,)), ((), ())), preferred_element_type=F32)


def matmul(left, right):
    return contract(left, right, 1, 0)


def matmul_tn(left, right):
    return contract(left, right, 0, 0)


def matmul_nt(left, right):
    return contract(left, right, 1, 1)


def norm_forward(values, gain_vec):
    factor = lax.rsqrt(jnp.mean(values * values, axis=-1, keepdims=True) + 1e-06)
    return (values * factor * gain_vec, factor)


def norm_backward(values, factor, gain_vec, grad_out):
    weighted = grad_out * gain_vec
    inner_mean = jnp.mean(weighted * values, axis=-1, keepdims=True)
    grad_in = factor * weighted - values * (factor * factor * factor) * inner_mean
    return (grad_in, jnp.sum(grad_out * values * factor, axis=0))


def silu_slope(values):
    sigmoid_v = jax.nn.sigmoid(values)
    return sigmoid_v * (1.0 + values * (1.0 - sigmoid_v))


def pad_to(array, size, dim):
    widths = [(0, 0)] * array.ndim
    widths[dim] = (0, size - array.shape[dim])
    return jnp.pad(array, widths)


MESH = pl.DeviceIdType.MESH


BULK = 9


class Parcel(NamedTuple):
    source: Any
    kind: str
    axis: str
    group: int
    pick: Any = None


class Line(NamedTuple):
    size: int
    me: Any
    device: Any


def line_of(axis, sizes):
    n, m = sizes
    if axis == "ctx":
        return Line(n, lax.axis_index("ctx"), lambda peer: {"ctx": peer})
    me = lax.axis_index("fsdp")
    if axis == "fsdp":
        return Line(m, me, lambda peer: {"fsdp": peer})
    half = m // 2
    own = lax.rem(me, half)
    return Line(half, own, lambda peer: {"fsdp": me - own + peer})


def parcel_shapes(parcels, sizes):
    n, m = sizes
    sizes_of = {"ctx": n, "fsdp": m, "pair": m // 2}
    shapes = []
    for parcel in parcels:
        source = shapes[parcel.source] if isinstance(parcel.source, int) else parcel.source
        size = sizes_of[parcel.axis]
        shape = source.shape
        if parcel.kind == "gather":
            shape = (size,) + shape
        elif parcel.kind == "lanes":
            shape = shape[:-1] + (size * shape[-1],)
        elif parcel.pick is not None:
            shape = (size,) + parcel.pick(None, None, shape)
        shapes.append(jax.ShapeDtypeStruct(shape, source.dtype))
    return shapes


class Mail:
    def __init__(self, parcels, sizes, in_refs, out_refs, sems):
        self.parcels, self.sizes, self.outs = parcels, sizes, out_refs
        self.send, self.recv, self.local = sems if sems else (None,) * 3
        given = iter(in_refs)
        self.sources = [out_refs[p.source] if isinstance(p.source, int) else next(given) for p in parcels]
        self.base = []
        total = 0
        for p in parcels:
            self.base.append(total)
            total += {"ctx": sizes[0], "fsdp": sizes[1], "pair": sizes[1] // 2}[p.axis]

    def parts(self, number, line, peer, owner):
        parcel, source, out = self.parcels[number], self.sources[number], self.outs[number]
        if parcel.kind == "swap":
            source = parcel.pick(source, peer, None) if parcel.pick else source.at[peer]
        if parcel.kind == "lanes":
            lanes = self.sources[number].shape[-1]
            spot = pl.ds(pl.multiple_of(owner * lanes, lanes), lanes)
            return source, out.at[(slice(None),) * (len(out.shape) - 1) + (spot,)]
        return source, out.at[owner]

    def copies(self, group, incoming):
        for number, parcel in enumerate(self.parcels):
            if parcel.group != group:
                continue
            line = line_of(parcel.axis, self.sizes)
            for d in range(1, line.size):
                peer = lax.rem(line.me + d, line.size)
                owner = lax.rem(line.me + line.size - d, line.size) if incoming else line.me
                source, target = self.parts(number, line, peer, owner)
                spot = self.base[number] + d
                yield pltpu.make_async_remote_copy(
                    src_ref=source,
                    dst_ref=target,
                    send_sem=self.send.at[spot],
                    recv_sem=self.recv.at[spot],
                    device_id=line.device(peer),
                    device_id_type=MESH,
                )

    def kept(self, group):
        for number, parcel in enumerate(self.parcels):
            if parcel.group == group:
                line = line_of(parcel.axis, self.sizes)
                source, target = self.parts(number, line, line.me, line.me)
                yield pltpu.make_async_copy(source, target, self.local.at[number])

    def start(self, group):
        for copy in self.copies(group, False):
            copy.start()
        for copy in self.kept(group):
            copy.start()

    def wait(self, group):
        for copy in self.copies(group, True):
            copy.wait_recv()
        for copy in self.copies(group, False):
            copy.wait_send()
        for copy in self.kept(group):
            copy.wait()

    def step(self, done, begun):
        if self.has(done):
            self.wait(done)
            if self.has(begun):
                self.start(begun)

    def begin(self):
        for group in (0, BULK):
            if self.has(group):
                self.start(group)

    def end(self, last):
        for group in (last, BULK):
            if self.has(group):
                self.wait(group)

    def has(self, group):
        return any(p.group == group for p in self.parcels)


def ctx_copy(source, target, send, recv, device):
    return pltpu.make_async_remote_copy(
        src_ref=source, dst_ref=target, send_sem=send, recv_sem=recv, device_id={"ctx": device}, device_id_type=MESH
    )


def line_place(n):
    me = lax.axis_index("ctx")
    core = lax.rem(me, 2)
    return me, core, me // 2, me + 1 - 2 * core


def greet(sizes, everyone, fsdp):
    n, m = sizes
    chips = n // 2
    me, core, chip, sibling = line_place(n)
    barrier = pltpu.get_barrier_semaphore()

    def hello(device):
        pl.semaphore_signal(barrier, inc=1, device_id=device, device_id_type=MESH)

    expected = 0
    if everyone:
        for d in range(1, n):
            hello({"ctx": lax.rem(me + d, n)})
        expected = n - 1
    else:
        hello({"ctx": sibling})

        @pl.when(chip > 0)
        def _():
            hello({"ctx": me - 2})

        @pl.when(chip < chips - 1)
        def _():
            hello({"ctx": me + 2})

        expected = 3 - (chip == 0).astype(jnp.int32) - (chip == chips - 1).astype(jnp.int32)
    if fsdp:
        own = lax.axis_index("fsdp")
        for d in range(1, m):
            hello({"fsdp": lax.rem(own + d, m)})
        expected = expected + m - 1
    pl.semaphore_wait(barrier, expected)


def talk(core_kernel, args, in_specs, out_shapes, out_specs, scratch, parcels, number, vmem, name, everyone=False, steps=0):
    sizes = (lax.axis_size("ctx"), lax.axis_size("fsdp"))
    arrays = [p.source for p in parcels if not isinstance(p.source, int)]
    shapes = parcel_shapes(parcels, sizes)
    total = sum({"ctx": sizes[0], "fsdp": sizes[1], "pair": sizes[1] // 2}[p.axis] for p in parcels)
    everyone = everyone or any(p.axis == "ctx" for p in parcels)
    fsdp = any(p.axis != "ctx" for p in parcels)
    anywhere = pl.BlockSpec(memory_space=pl.ANY)
    sems = []
    if parcels:
        sems = [pltpu.SemaphoreType.DMA((total,)), pltpu.SemaphoreType.DMA((total,)), pltpu.SemaphoreType.DMA((len(parcels),))]

    def kernel(*refs):
        refs = list(refs)
        take = lambda count: [refs.pop(0) for _ in range(count)]
        ins, mail_in, outs, mail_out = take(len(args)), take(len(arrays)), take(len(out_shapes)), take(len(shapes))
        own = take(len(scratch))
        mail = Mail(parcels, sizes, mail_in, mail_out, refs)
        if not steps:
            greet(sizes, everyone, fsdp)
            core_kernel(sizes[0], ins, outs, own, mail)
            return

        @pl.when(pl.program_id(0) == 0)
        def _():
            greet(sizes, everyone, fsdp)
            mail.begin()

        core_kernel(*ins, *outs, *own)

        @pl.when(pl.program_id(0) == steps - 1)
        def _():
            mail.end(0)

    results = pl.pallas_call(
        kernel,
        grid=(steps,) if steps else (),
        out_shape=list(out_shapes) + shapes,
        in_specs=list(in_specs) + [anywhere] * len(arrays),
        out_specs=list(out_specs) + [anywhere] * len(shapes),
        scratch_shapes=list(scratch) + sems,
        compiler_params=pltpu.CompilerParams(collective_id=number, has_side_effects=True, vmem_limit_bytes=vmem),
        name=name,
    )(*args, *arrays)
    return results[: len(out_shapes)], results[len(out_shapes) :]


def share_core(n, xs, outs, sems, mail):
    chips = n // 2
    me, core, chip, sibling = line_place(n)
    send, recv, side_send, side_recv, local = sems
    several = range(len(xs))
    ways = ((0, 1), (1, -1))

    def spot(hop, sign):
        held = chip - sign * hop
        onward = chip + sign
        have = (held >= 0) & (held < chips)
        return 2 * held, have, have & (onward >= 0) & (onward < chips), 2 * onward + core

    def line_copy(a, way, hop, source, block, device):
        return ctx_copy(source, outs[a].at[block], send.at[a, way, hop], recv.at[a, way, hop], device)

    def side_copy(a, way, hop, source, block):
        return ctx_copy(source, outs[a].at[block], side_send.at[a, way, hop], side_recv.at[a, way, hop], sibling)

    keeps = [pltpu.make_async_copy(xs[a], outs[a].at[me], local.at[a]) for a in several]
    for a in several:
        keeps[a].start()
        side_copy(a, 0, 0, xs[a], me).start()
    for hop in range(chips):
        for way, sign in ways:
            base, have, go, onward = spot(hop, sign)
            block = base + core
            if hop > 0:

                @pl.when(have)
                def _():
                    for a in several:
                        line_copy(a, way, hop - 1, xs[a], block, sibling).wait_recv()
                        side_copy(a, way, hop, outs[a].at[block], block).start()

            if hop < chips - 1:

                @pl.when(go)
                def _():
                    for a in several:
                        source = xs[a] if hop == 0 else outs[a].at[block]
                        line_copy(a, way, hop, source, block, onward).start()

        if hop == 0:
            mail.begin()
            mail.step(0, 1)
        if hop == 1:
            mail.step(1, 2)

    for hop in range(chips):
        for way, sign in ways:
            base, have, go, onward = spot(hop, sign)
            block = base + core
            other = base + 1 - core
            if hop > 0:

                @pl.when(have)
                def _():
                    for a in several:
                        side_copy(a, way, hop, outs[a].at[block], block).wait_send()
                        side_copy(a, way, hop, xs[a], other).wait_recv()

            if hop < chips - 1:

                @pl.when(go)
                def _():
                    for a in several:
                        line_copy(a, way, hop, xs[a], block, onward).wait_send()

    for a in several:
        side_copy(a, 0, 0, xs[a], me).wait_send()
        side_copy(a, 0, 0, xs[a], sibling).wait_recv()
        keeps[a].wait()
    mail.end(2)


def share_tokens(blocks, number, parcels=()):
    n = lax.axis_size("ctx")
    anywhere = pl.BlockSpec(memory_space=pl.ANY)
    count = len(blocks)
    return talk(
        share_core,
        blocks,
        [anywhere] * count,
        [jax.ShapeDtypeStruct((n,) + b.shape, b.dtype) for b in blocks],
        [anywhere] * count,
        [pltpu.SemaphoreType.DMA((count, 2, n // 2))] * 4 + [pltpu.SemaphoreType.DMA((count,))],
        list(parcels),
        number,
        16 << 20,
        "share_tokens",
    )


def feed_core(consume, n, ins, outs, own, mail):
    x_ref, given = ins[0], ins[1:]
    count = len(given)
    gathered, held, more = own[0], own[1 : 1 + count], own[1 + count : -6]
    send, recv, side_send, side_recv, local, load = own[-6:]
    chips = n // 2
    me, core, chip, sibling = line_place(n)

    def line_copy(way, hop, source, block, device):
        return ctx_copy(source, gathered.at[block], send.at[way, hop], recv.at[way, hop], device)

    def side_copy(way, hop, source, block):
        return ctx_copy(source, gathered.at[block], side_send.at[way, hop], side_recv.at[way, hop], sibling)

    def spot(hop, way):
        sign = 1 - 2 * way
        at = chip - sign * hop
        onward = chip + sign
        have = (at >= 0) & (at < chips)
        go = have & (onward >= 0) & (onward < chips)
        return 2 * at + core, 2 * at + 1 - core, have, go, 2 * onward + core

    keep = pltpu.make_async_copy(x_ref, gathered.at[me], local)
    keep.start()
    for way in (0, 1):
        _, _, _, go, onward = spot(0, way)

        @pl.when(go)
        def _():
            line_copy(way, 0, x_ref, me, onward).start()

    side_copy(0, 0, x_ref, me).start()
    loads = [pltpu.make_async_copy(source, target, load.at[i]) for i, (source, target) in enumerate(zip(given, held))]
    for copy in loads:
        copy.start()
    mail.begin()
    for copy in loads:
        copy.wait()
    keep.wait()

    def event(number, _):
        later = jnp.maximum(number - 2, 0)
        hop = 1 + lax.div(later, 4)
        kind = lax.rem(later, 4)
        way = lax.rem(kind, 2)

        @pl.when(number == 1)
        def _():
            side_copy(0, 0, x_ref, sibling).wait_recv()

        @pl.when((number >= 2) & (kind == 0))
        def _():
            for w in (0, 1):
                block, _, have, go, onward = spot(hop, w)

                @pl.when(have)
                def _():
                    line_copy(w, hop - 1, x_ref, block, sibling).wait_recv()
                    side_copy(w, hop, gathered.at[block], block).start()

                @pl.when(go)
                def _():
                    line_copy(w, hop, gathered.at[block], block, onward).start()

        block, other, have, _, _ = spot(hop, way)

        @pl.when((number >= 2) & (kind >= 2) & have)
        def _():
            side_copy(way, hop, x_ref, other).wait_recv()

        block = jnp.where(kind >= 2, other, block)
        block = jnp.where(number == 0, me, jnp.where(number == 1, sibling, block))

        @pl.when((number < 2) | have)
        def _():
            consume(block, gathered, held, outs, more, number == 0)

        return 0

    events = 2 + 4 * (chips - 1)
    lax.fori_loop(0, events, event, 0)
    consume(None, gathered, held, outs, more, None)
    for hop in range(chips):
        for way in (0, 1):
            block, other, have, go, onward = spot(hop, way)
            if hop > 0:

                @pl.when(have)
                def _():
                    side_copy(way, hop, gathered.at[block], block).wait_send()

            if hop < chips - 1:

                @pl.when(go)
                def _():
                    line_copy(way, hop, x_ref, block, onward).wait_send()

    side_copy(0, 0, x_ref, me).wait_send()
    mail.end(0)


def feed_tokens(block, number, consume, given, results, scratch, parcels=()):
    n = lax.axis_size("ctx")
    rows, width = block.shape
    vmem = pl.BlockSpec(memory_space=pltpu.VMEM)
    anywhere = pl.BlockSpec(memory_space=pl.ANY)
    return talk(
        functools.partial(feed_core, consume),
        [block] + list(given),
        [anywhere] * (1 + len(given)),
        list(results),
        [vmem] * len(results),
        [pltpu.VMEM((n, rows, width), block.dtype)]
        + [pltpu.VMEM(g.shape, g.dtype) for g in given]
        + list(scratch)
        + [pltpu.SemaphoreType.DMA((2, n // 2))] * 4
        + [pltpu.SemaphoreType.DMA, pltpu.SemaphoreType.DMA((len(given),))],
        list(parcels),
        number,
        56 << 20,
        "feed_tokens",
    )


def reduce_core(job, count, n, ins, outs, own, mail):
    terms = (len(ins) - count) // 2
    pairs = list(zip(ins[:terms], ins[terms : 2 * terms]))
    o_ref = outs[0]
    total, to_side, from_side, inbox, side_send, side_recv, send, recv = own
    chips = n // 2
    me, core, chip, sibling = line_place(n)
    rows = o_ref.shape[0]

    def partial(block):
        place = pl.ds(pl.multiple_of(block * rows, rows), rows)
        return sum(contract(a[place, :], w[...], 1, 0 if w.shape[0] == a.shape[1] else 1) for a, w in pairs)

    def side_copy(dest):
        return ctx_copy(to_side.at[dest], from_side.at[dest], side_send.at[dest], side_recv.at[dest], sibling)

    def line_copy(way, dest, onward):
        return ctx_copy(from_side.at[dest], inbox.at[dest + way], send.at[dest], recv.at[dest + way], onward)

    mail.begin()

    flip = chip >= chips // 2
    near = jnp.where(flip, chips - 1 - chip, chip)
    lead = chips - 1 - 2 * near

    def begin(k):
        later = jnp.maximum(k - lead, 0)
        high = chips - 1 - jnp.minimum(k, lead) - lax.div(later, 2)
        dest = jnp.where(lax.rem(later, 2) == 1, lax.div(later, 2), high)
        dest = jnp.where(flip, chips - 1 - dest, dest)
        to_side[dest] = partial(2 * dest + 1 - core).astype(jnp.bfloat16)
        side_copy(dest).start()
        total[dest] = partial(2 * dest + core)

    begin(0)

    def spot(tick, way):
        far = (chips - 1 - chip) if way == 0 else chip
        k = tick - far
        dest = k if way == 0 else chips - 1 - k
        active = (k >= 0) & ((dest < chip) if way == 0 else (dest > chip))
        return far, k, dest, active, (me - 2 if way == 0 else me + 2)

    def advance(tick, _):
        @pl.when(tick < chips - 1)
        def _():
            begin(tick + 1)

        for way in (0, 1):
            far, k, dest, active, onward = spot(tick, way)
            before = dest - 1 if way == 0 else dest + 1

            @pl.when(active)
            def _():
                side_copy(dest).wait_recv()
                total[dest] += from_side[dest].astype(jnp.float32)

                @pl.when(far > 0)
                def _():
                    line_copy(way, dest, onward).wait_recv()
                    total[dest] += inbox[dest + way].astype(jnp.float32)

                @pl.when((far == 0) & (k > 0))
                def _():
                    line_copy(way, before, onward).wait_send()

                from_side[dest] = total[dest].astype(jnp.bfloat16)
                line_copy(way, dest, onward).start()

        if job:
            job(tick, ins[: len(ins) - count], ins[len(ins) - count :], outs[1:])
        return 0

    lax.fori_loop(0, chips, advance, 0)
    side_copy(chip).wait_recv()
    total[chip] += from_side[chip].astype(jnp.float32)

    @pl.when(chip < chips - 1)
    def _():
        line_copy(0, chip, me - 2).wait_recv()
        total[chip] += inbox[chip].astype(jnp.float32)

    @pl.when(chip > 0)
    def _():
        line_copy(1, chip, me + 2).wait_recv()
        total[chip] += inbox[chip + 1].astype(jnp.float32)

    o_ref[...] = total[chip]

    def finish(tick, _):
        side_copy(tick).wait_send()
        for way in (0, 1):
            far, k, dest, active, onward = spot(tick, way)

            @pl.when(active & ((far > 0) | (k == chips - 2)))
            def _():
                line_copy(way, dest, onward).wait_send()

        return 0

    lax.fori_loop(0, chips, finish, 0)
    mail.end(0)


def reduce_tokens(lefts, rights, number, parcels=(), job=None, job_in=(), job_out=()):
    n = lax.axis_size("ctx")
    chips = n // 2
    rows, width = lefts[0].shape[0] // n, D
    buffer = lambda *lead: pltpu.VMEM(lead + (rows, width), jnp.bfloat16)
    vmem = pl.BlockSpec(memory_space=pltpu.VMEM)

    outs, extra = talk(
        functools.partial(reduce_core, job, len(job_in)),
        lefts + rights + list(job_in),
        [vmem] * (2 * len(lefts) + len(job_in)),
        [jax.ShapeDtypeStruct((rows, width), jnp.float32)] + list(job_out),
        [vmem] * (1 + len(job_out)),
        [pltpu.VMEM((chips, rows, width), jnp.float32), buffer(chips), buffer(chips), buffer(chips + 1)]
        + [pltpu.SemaphoreType.DMA((chips,))] * 3
        + [pltpu.SemaphoreType.DMA((chips + 1,))],
        list(parcels),
        number,
        (56 if chips <= 4 else 60) << 20,
        "reduce_tokens",
    )
    return outs, extra


def total_core(n, ins, outs, own, mail):
    x_ref, o_ref = ins[0], outs[0]
    from_side, summed, inbox, outbox, side_send, side_recv, send, recv, out_send, out_recv, back_send, back_recv, local = own
    chips = n // 2
    me, core, chip, sibling = line_place(n)
    cols = outbox.shape[1]

    def place(ref, block):
        return ref.at[:, pl.ds(pl.multiple_of(block * cols, cols), cols)]

    def side_copy(d):
        dest = lax.rem(chip + d, chips)
        return ctx_copy(place(x_ref, 2 * dest + 1 - core), from_side.at[d], side_send.at[d], side_recv.at[d], sibling)

    def line_copy(d):
        return ctx_copy(summed.at[d], inbox.at[d], send.at[d], recv.at[d], lax.rem(me + 2 * d, n))

    def out_copy(d):
        return ctx_copy(outbox, place(o_ref, me), out_send.at[d], out_recv.at[d], lax.rem(me + 2 * d, n))

    order = list(range(1, chips)) + [0]
    for d in order:
        side_copy(d).start()
    mail.begin()
    for d in order:
        dest = lax.rem(chip + d, chips)
        side_copy(d).wait_recv()
        block = pl.ds(pl.multiple_of((2 * dest + core) * cols, cols), cols)
        summed[d] = x_ref[:, block] + from_side[d]
        if d:
            line_copy(d).start()
    result = summed[0]
    for d in range(1, chips):
        line_copy(d).wait_recv()
        result = result + inbox[d]
    outbox[...] = result.astype(jnp.bfloat16)
    keep = pltpu.make_async_copy(outbox, place(o_ref, me), local)
    keep.start()
    for d in range(1, chips):
        out_copy(d).start()
    side = ctx_copy(outbox, place(o_ref, me), back_send.at[0], back_recv.at[0], sibling)
    side.start()
    mail.step(0, 1)
    for d in range(1, chips):
        origin = lax.rem(me + n - 2 * d, n)
        ctx_copy(outbox, place(o_ref, origin), out_send.at[d], out_recv.at[d], origin).wait_recv()
        ctx_copy(place(o_ref, origin), place(o_ref, origin), back_send.at[d], back_recv.at[d], sibling).start()
    for d in range(chips):
        mine = lax.rem(me + n - 2 * d, n)
        theirs = lax.rem(sibling + n - 2 * d, n)
        ctx_copy(place(o_ref, mine), place(o_ref, mine), back_send.at[d], back_recv.at[d], sibling).wait_send()
        ctx_copy(outbox, place(o_ref, theirs), back_send.at[d], back_recv.at[d], sibling).wait_recv()
        side_copy(d).wait_send()
        if d:
            line_copy(d).wait_send()
            out_copy(d).wait_send()
    keep.wait()
    for number, spread_ref in enumerate(outs[1:]):

        def fill(part, _):
            first = pl.multiple_of(part * 128, 128)
            values = o_ref[number * DS : (number + 1) * DS, pl.ds(first, 128)].astype(jnp.float32)
            for k in range(128):
                column = jnp.broadcast_to(values[:, k : k + 1], (DS, 128))
                spread_ref[first + k] = column.astype(jnp.bfloat16)
            return 0

        lax.fori_loop(0, o_ref.shape[1] // 128, fill, 0)
    mail.end(1)


def total_columns(partial, number, parcels=(), spreads=0):
    n = lax.axis_size("ctx")
    chips = n // 2
    feats, length = partial.shape
    cols = length // n
    vmem = pl.BlockSpec(memory_space=pltpu.VMEM)
    outs, extra = talk(
        total_core,
        [partial],
        [vmem],
        [jax.ShapeDtypeStruct((feats, length), jnp.bfloat16)]
        + [jax.ShapeDtypeStruct((length, DS, 128), jnp.bfloat16)] * spreads,
        [vmem] * (1 + spreads),
        [pltpu.VMEM((chips, feats, cols), jnp.float32)] * 3
        + [pltpu.VMEM((feats, cols), jnp.bfloat16)]
        + [pltpu.SemaphoreType.DMA((chips,))] * 8
        + [pltpu.SemaphoreType.DMA],
        list(parcels),
        number,
        48 << 20,
        "total_columns",
        everyone=True,
    )
    return outs, extra


def send_core(n, ins, outs, own, mail):
    mail.begin()
    mail.step(0, 1)
    mail.end(1)


def send_only(parcels, number):
    return talk(send_core, [], [], [], [], [], list(parcels), number, 16 << 20, "send_only", everyone=True)[1]


def body(
    tokens,
    out_grad,
    teacher,
    valid,
    w_query,
    w_keyval,
    w_attn_out,
    w_in,
    w_mamba_out,
    w_gate,
    w_up,
    w_down,
    x_proj,
    dt_proj,
    a_log,
    conv_taps,
    conv_bias,
    dt_bias,
    skip_gain,
    norm_gains,
):
    n = lax.axis_size("ctx")
    m = lax.axis_size("fsdp")
    fsdp_index = lax.axis_index("fsdp")
    rows = tokens.shape[1]
    length = rows * n
    depth = w_in.shape[0]
    half = m // 2
    chunks = n // half
    chans = DI // n
    sub = chans // half
    subp = -(-sub // 128) * 128
    wide = half * subp
    units = w_down.shape[0]
    unit_sub = units // m
    unit_pad = -(-unit_sub // 16) * 16
    unit_wide = m * unit_pad
    heads = -(-H // n)
    group_size = H // KVH
    feats = -(-(R + 2 * DS) // 16) * 16
    slots = (heads + group_size - 2) // group_size + 1
    q_part = heads * HD // m
    kv_part = 2 * slots * HD // m
    head_pad = -(-(q_part + kv_part) // 128) * 128

    def wide_chans(array):
        array = array.reshape((half, sub) + array.shape[1:])
        return pad_to(array, subp, 1).reshape((wide,) + array.shape[2:])

    def true_chans(array):
        return array.reshape((half, subp) + array.shape[1:])[:, :sub].reshape((chans,) + array.shape[1:])

    mask_rows = valid[0].astype(F32)
    meta = jnp.stack([pad_to(norm_gains.astype(F32), 256, 0), jnp.full((256,), jnp.sum(mask_rows))])
    meta = pad_to(meta, 8, 0)
    in_send = pad_to(w_in.reshape(depth, chunks, half, sub).transpose(2, 1, 0, 3), subp, 3)
    head_send = jnp.concatenate([w_query, w_keyval], 1)
    ff_send = jnp.concatenate(
        [pad_to(w.reshape(depth, n // m, m, unit_sub).transpose(2, 1, 0, 3), unit_pad, 3) for w in (w_gate, w_up)], 3
    )
    small_send = jnp.concatenate(
        [x_proj, dt_proj, a_log, conv_taps, conv_bias[:, None], dt_bias[:, None], skip_gain[:, None]], 1
    )

    def by_chunk(ref, peer, shape):
        if ref is None:
            return shape[2:]
        return ref.at[lax.div(peer, chunks), lax.rem(peer, chunks)]

    (tokens_all, attn_rows), entry = share_tokens(
        [tokens[0], w_attn_out],
        0,
        [
            Parcel(in_send, "swap", "pair", 0),
            Parcel(meta, "gather", "fsdp", 0),
            Parcel(0, "swap", "ctx", 1, by_chunk),
            Parcel(1, "gather", "ctx", 1),
            Parcel(2, "lanes", "fsdp", 2),
            Parcel(head_send, "gather", "fsdp", BULK),
            Parcel(small_send, "gather", "fsdp", BULK),
            Parcel(ff_send, "swap", "fsdp", BULK),
        ],
    )
    meta_all, in_all, head_all, small_all, ff_all = entry[3:]
    gain_set = meta_all[:, :, 0, : norm_gains.shape[0]].reshape(4, D)
    valid_sum = jnp.sum(meta_all[:, :, 1, 0])
    in_weight = in_all.reshape(D, 2 * wide)
    small = wide_chans(small_all.reshape(chans, -1))
    xproj_weight = jnp.concatenate([small[:, R : R + 2 * DS], small[:, :R]], 1)
    dtproj_weight = small[:, R + 2 * DS : 2 * R + 2 * DS]
    rest = small[:, 2 * R + 2 * DS :].astype(F32)
    amat = wide_chans(-jnp.exp(small_all.reshape(chans, -1)[:, 2 * R + 2 * DS : 2 * R + 3 * DS].astype(F32))).T
    rate = amat * LOG2E
    taps = rest[:, DS : DS + KC].T
    conv_bias_vec, dt_bias_vec, skip_vec = rest[:, DS + KC], rest[:, DS + KC + 1], rest[:, DS + KC + 2]
    query_wide, kv_wide = w_query.shape[1], w_keyval.shape[1]
    head_wide = query_wide + kv_wide

    def natural_column(part, shard, lane):
        query = heads * HD * shard + q_part * part + lane
        query_at = query // query_wide * head_wide + query % query_wide
        inner = kv_part * part + lane - q_part
        base = jnp.minimum(heads * shard, H - 1) // group_size
        kv_head = jnp.minimum(base + inner // HD % slots, KVH - 1)
        kv_column = inner // (slots * HD) * (KVH * HD) + kv_head * HD + inner % HD
        kv_at = kv_column // kv_wide * head_wide + query_wide + kv_column % kv_wide
        at = jnp.where(lane < q_part, jnp.where(query < H * HD, query_at, -1), kv_at)
        return jnp.where(lane < q_part + kv_part, at, -1)

    def counted(*shape):
        return [lax.broadcasted_iota(jnp.int32, shape, d) for d in range(len(shape))]

    row, shard, lane = counted(m * head_wide, n, head_pad)
    chosen = (row == natural_column(fsdp_index, shard, lane)).astype(BF).reshape(m, head_wide, n * head_pad)
    head_rows = sum(matmul(head_all[f], chosen[f]) for f in range(m)).astype(BF)
    head_rows = head_rows.reshape(depth, n, head_pad).transpose(1, 0, 2)

    hidden = tokens[0].astype(F32)
    normed_all = norm_forward(tokens_all.reshape(length, D).astype(F32), gain_set[0])[0].astype(BF)
    normed_all = lax.optimization_barrier(normed_all)
    factor_one = norm_forward(hidden, gain_set[0])[1]

    inner_low = matmul(normed_all, in_weight).astype(BF)
    x_branch = inner_low[:, :wide].astype(F32)
    z_branch = inner_low[:, wide:].astype(F32)
    padded = jnp.pad(x_branch, ((KC - 1, 0), (0, 0)))
    pre_conv = conv_bias_vec
    for k in range(KC):
        pre_conv = pre_conv + taps[k] * padded[k : k + length]
    ssm_in = jax.nn.silu(pre_conv)
    ssm_low = ssm_in.astype(BF)
    (xdbl_t, b_wide, c_wide), (_, head_cols_all) = total_columns(
        pad_to(contract(xproj_weight, ssm_low, 0, 1), feats, 0),
        1,
        [
            Parcel(head_rows, "swap", "ctx", 0),
            Parcel(0, "lanes", "fsdp", 1),
        ],
        2,
    )
    head_weight = head_cols_all.reshape(D, m * head_pad)

    head_t = contract(head_weight, normed_all, 0, 1).astype(BF).reshape(m, head_pad, length)
    query_t = head_t[:, :q_part].reshape(heads * HD, length) * BF(HD**-0.5)
    kv_t = head_t[:, q_part : q_part + kv_part].reshape(2, slots, HD, length)
    keys_t, values_t = kv_t[0], kv_t[1]
    keys, values = jnp.swapaxes(keys_t, 1, 2), jnp.swapaxes(values_t, 1, 2)
    row, column = counted(chans, wide)
    chosen = (row // sub * subp + row % sub == column).astype(BF)
    mamba_send = contract(w_mamba_out, chosen, 0, 0).astype(BF)
    (attn_part, lse), (mamba_all, ff_cols) = attend(
        query_t,
        keys,
        values_t,
        [
            Parcel(mamba_send, "gather", "fsdp", BULK),
            Parcel(ff_all.reshape(n, depth, 2 * unit_pad), "swap", "ctx", BULK),
        ],
        11,
    )
    attn_part = attn_part.reshape(heads * HD, n, rows).transpose(1, 0, 2)
    mamba_weight_t = mamba_all.reshape(D, wide)
    ff_parts = ff_cols.reshape(D, 2 * unit_pad).T.reshape(2, unit_pad, D)

    dt_in_t = xdbl_t[2 * DS : 2 * DS + R]
    dt_pre = contract(dt_in_t, dtproj_weight, 0, 1) + dt_bias_vec
    step_size = jax.nn.softplus(dt_pre)
    row, column = counted(units, unit_wide)
    chosen = (row // unit_sub * unit_pad + row % unit_sub == column).astype(BF)
    down_send = contract(w_down, chosen, 0, 0).astype(BF)
    (state_rows, starts), (attn_t, down_all) = ssm_forward(
        step_size,
        ssm_in,
        b_wide,
        c_wide,
        rate,
        [Parcel(attn_part, "swap", "ctx", BULK), Parcel(down_send, "gather", "fsdp", BULK)],
        12,
    )
    down_weight_t = down_all.reshape(D, unit_wide)
    ssm_out = state_rows + skip_vec * ssm_in
    gate_z = jax.nn.silu(z_branch)
    mixed_low = (ssm_out * gate_z).astype(BF)
    (mamba_proj,), (attn_weight_t,) = reduce_tokens(
        [mixed_low], [mamba_weight_t], 2, [Parcel(attn_rows.reshape(H * HD, -1).T, "gather", "fsdp", BULK)]
    )
    attn_t = attn_t.reshape(n * heads * HD, rows)[: H * HD]
    attn_weight_t = attn_weight_t.reshape(D, H * HD)
    attn_proj = contract(attn_t, attn_weight_t, 0, 1)

    attn_norm, factor_attn = norm_forward(attn_proj, gain_set[1])
    mamba_norm, factor_mamba = norm_forward(mamba_proj, gain_set[2])
    residual = hidden + 0.5 * (attn_norm + mamba_norm)
    ffn_in, factor_ffn = norm_forward(residual, gain_set[3])
    (ffn_all,), (gate_rows, up_rows) = share_tokens(
        [ffn_in.astype(BF)],
        3,
        [Parcel(ff_parts[0], "gather", "fsdp", BULK), Parcel(ff_parts[1], "gather", "fsdp", BULK)],
    )
    ffn_all = ffn_all.reshape(length, D)
    gate_rows, up_rows = gate_rows.reshape(unit_wide, D), up_rows.reshape(unit_wide, D)
    gate_pre = matmul_nt(ffn_all, gate_rows)
    up_pre = matmul_nt(ffn_all, up_rows)
    hidden_act = (jax.nn.silu(gate_pre) * up_pre).astype(BF)
    layer_out = residual + reduce_tokens([hidden_act], [down_weight_t], 4)[0][0]

    mismatch = layer_out - teacher[0].astype(F32)
    error_part = jnp.sum(mask_rows[:, None] * mismatch * mismatch)
    grad_layer = out_grad[0].astype(F32) + 2.0 / (valid_sum * D) * mask_rows[:, None] * mismatch

    def feed_forward_back(block, x, held, outs, more, first):
        if block is None:
            outs[2][...] = more[0][...].astype(BF).reshape(outs[2].shape)
            return
        place = pl.ds(pl.multiple_of(block * rows, rows), rows)
        weight, gates, ups, acts = held
        grad = x[block]
        slope = contract(grad, weight[...], 1, 0)
        gate, up = gates[place, :], ups[place, :]
        sigmoid_v = 1.0 / (1.0 + jnp.exp(-gate))
        outs[0][place, :] = (slope * up * (sigmoid_v * (1.0 + gate * (1.0 - sigmoid_v)))).astype(BF)
        outs[1][place, :] = (slope * (gate * sigmoid_v)).astype(BF)
        part = contract(grad, acts[place, :], 0, 0)

        @pl.when(first)
        def _():
            more[0][...] = part

        @pl.when(jnp.logical_not(first))
        def _():
            more[0][...] += part

    (grad_gate, grad_up, down_grad), _ = feed_tokens(
        grad_layer.astype(BF),
        5,
        feed_forward_back,
        [down_weight_t, gate_pre, up_pre, hidden_act],
        [jax.ShapeDtypeStruct((length, unit_wide), BF)] * 2 + [jax.ShapeDtypeStruct((m, D // m, unit_wide), BF)],
        [pltpu.VMEM((D, unit_wide), F32)],
    )
    grad_parts = [jax.ShapeDtypeStruct((m, unit_pad, D), BF)] * 2

    def unit_grads(tick, given, more, outs):
        for piece in range(m):

            @pl.when(tick == piece * n // (2 * m))
            def _():
                for left, out in zip(given, outs):
                    part = left[:, piece * unit_pad : (piece + 1) * unit_pad]
                    out[piece] = contract(part, more[0][...], 0, 0).astype(BF)

    inside = length * D <= 4 << 20
    reduced, (down_grad,) = reduce_tokens(
        [grad_gate, grad_up],
        [gate_rows, up_rows],
        6,
        [Parcel(down_grad, "swap", "fsdp", BULK)],
        unit_grads if inside else None,
        [ffn_all] if inside else [],
        grad_parts if inside else [],
    )
    grad_ffn_in = reduced[0]
    down_grad = jnp.sum(down_grad.astype(F32), 0).T.reshape(m, unit_pad, D // m)[:, :unit_sub].reshape(units, D // m)
    if inside:
        gate_grad, up_grad = reduced[1:]
    else:
        gate_grad, up_grad = [matmul_tn(g, ffn_all).astype(BF).reshape(m, unit_pad, D) for g in (grad_gate, grad_up)]

    grad_norm_res, gain_four = norm_backward(residual, factor_ffn, gain_set[3], grad_ffn_in)
    grad_resid = grad_layer + grad_norm_res
    half_grad = 0.5 * grad_resid
    grad_attn_proj, gain_two = norm_backward(attn_proj, factor_attn, gain_set[1], half_grad)
    grad_mamba_proj, gain_three = norm_backward(mamba_proj, factor_mamba, gain_set[2], half_grad)
    grad_attn_proj_low = grad_attn_proj.astype(BF)

    def state_space_back(block, x, held, outs, more, first):
        if block is None:
            outs[2][...] = more[0][...].astype(BF).reshape(outs[2].shape)
            return
        place = pl.ds(pl.multiple_of(block * rows, rows), rows)
        weight, z_part, rows_out, mixed = held
        grad = x[block]
        slope = contract(grad, weight[...], 1, 0)
        z = z_part[place, :].astype(F32)
        sigmoid_v = 1.0 / (1.0 + jnp.exp(-z))
        outs[0][place, :] = slope * (z * sigmoid_v)
        outs[1][place, :] = (slope * rows_out[place, :] * (sigmoid_v * (1.0 + z * (1.0 - sigmoid_v)))).astype(BF)
        part = contract(grad, mixed[place, :], 0, 0)

        @pl.when(first)
        def _():
            more[0][...] = part

        @pl.when(jnp.logical_not(first))
        def _():
            more[0][...] += part

    (grad_y, grad_z, mamba_out_grad), (gate_grad, up_grad) = feed_tokens(
        grad_mamba_proj.astype(BF),
        7,
        state_space_back,
        [mamba_weight_t, inner_low[:, wide:], ssm_out, mixed_low],
        [
            jax.ShapeDtypeStruct((length, wide), F32),
            jax.ShapeDtypeStruct((length, wide), BF),
            jax.ShapeDtypeStruct((m, D // m, wide), BF),
        ],
        [pltpu.VMEM((D, wide), F32)],
        [Parcel(gate_grad, "swap", "fsdp", BULK), Parcel(up_grad, "swap", "fsdp", BULK)],
    )
    ff_grad = jnp.stack([jnp.sum(g.astype(F32), 0).astype(BF) for g in (gate_grad, up_grad)])
    ff_grad = ff_grad.reshape(2 * unit_pad, n, depth).transpose(1, 0, 2)
    attn_out_grad = contract(grad_attn_proj_low, attn_t, 0, 1).astype(BF).reshape(m, D // m, H * HD)
    grad_attn = contract(attn_weight_t, grad_attn_proj_low, 0, 1).astype(BF)
    grad_attn = pad_to(grad_attn, n * heads * HD, 0).reshape(n, heads * HD, rows)

    z_grad = matmul_tn(normed_all, grad_z).astype(BF)
    step_grad, along_b, b_grad, c_grad, a_accum, (attn_out_grad, grad_attn) = ssm_backward(
        step_size,
        ssm_in,
        grad_y,
        b_wide,
        c_wide,
        rate,
        amat,
        starts,
        [Parcel(attn_out_grad, "swap", "fsdp", BULK), Parcel(grad_attn, "swap", "ctx", BULK)],
        13,
    )
    attn_out_grad = jnp.sum(attn_out_grad.astype(F32), 0).T.astype(BF)
    attn_out_grad = lax.psum_scatter(attn_out_grad, "ctx", scatter_dimension=0, tiled=True).astype(F32)

    grad_attn = grad_attn.transpose(1, 0, 2).reshape(heads * HD, length)
    (grad_query, grad_keys, grad_values), (ff_grad, mamba_out_grad) = attend_back(
        query_t,
        grad_attn,
        keys,
        keys_t,
        values,
        lse,
        [Parcel(ff_grad, "swap", "ctx", BULK), Parcel(mamba_out_grad, "swap", "fsdp", BULK)],
        14,
    )
    grad_kv = jnp.concatenate([grad_keys, grad_values], 0).astype(BF).reshape(m, kv_part, length)
    grad_head_t = jnp.concatenate([grad_query.reshape(m, q_part, length), grad_kv], 1)
    grad_head_t = pad_to(grad_head_t, head_pad, 1).reshape(m * head_pad, length)
    mamba_out_grad = true_chans(jnp.sum(mamba_out_grad.astype(F32), 0).T)
    head_grad = contract(grad_head_t, normed_all, 1, 0).astype(BF).reshape(m, head_pad, D)

    grad_dt_pre = (step_grad * jax.nn.sigmoid(dt_pre)).astype(BF)
    dtproj_grad = contract(grad_dt_pre, dt_in_t, 0, 1)
    grad_xdbl_t = jnp.concatenate([b_grad.T, c_grad.T, contract(dtproj_weight, grad_dt_pre, 0, 1)], 0)
    (grad_xdbl_t,), (head_grad,) = total_columns(
        pad_to(grad_xdbl_t, feats, 0),
        8,
        [Parcel(head_grad, "swap", "fsdp", BULK)],
    )
    grad_xdbl_t = grad_xdbl_t[: R + 2 * DS]
    head_grad = jnp.sum(head_grad.astype(F32), 0).astype(BF).T.reshape(n, depth, head_pad)
    xproj_grad = contract(ssm_low, grad_xdbl_t, 0, 1)
    grad_ssm_in = step_size * along_b + skip_vec * grad_y + contract(grad_xdbl_t, xproj_weight, 0, 1)
    grad_pre = grad_ssm_in * silu_slope(pre_conv)
    taps_grad = jnp.stack([jnp.sum(grad_pre * padded[k : k + length], axis=0) for k in range(KC)], 1)
    grad_after = jnp.pad(grad_pre, ((0, KC - 1), (0, 0)))
    grad_x = jnp.zeros_like(grad_pre)
    for k in range(KC):
        grad_x = grad_x + taps[k] * grad_after[KC - 1 - k : KC - 1 - k + length]
    x_grad = matmul_tn(normed_all, grad_x.astype(BF)).astype(BF)
    small_grad = jnp.concatenate(
        [
            xproj_grad[:, 2 * DS :],
            xproj_grad[:, : 2 * DS],
            dtproj_grad,
            (a_accum * amat).T,
            taps_grad,
            jnp.sum(grad_pre, axis=0)[:, None],
            jnp.sum(grad_dt_pre.astype(F32), axis=0)[:, None],
            jnp.sum(grad_y * ssm_in, axis=0)[:, None],
        ],
        1,
    )
    small_grad = true_chans(small_grad).reshape(m, chans // m, -1)

    def used(array, dim):
        if head_pad == q_part + kv_part:
            return array
        split = array.reshape(array.shape[:dim] + (m, head_pad) + array.shape[dim + 1 :])
        return lax.slice_in_dim(split, 0, q_part + kv_part, 1, dim + 1).reshape(
            array.shape[:dim] + (-1,) + array.shape[dim + 1 :]
        )

    def by_lanes(ref, peer, shape):
        if ref is None:
            return (shape[0], subp)
        return ref.at[:, pl.ds(pl.multiple_of(peer * subp, subp), subp)]

    (grad_normed,), (ff_grad, small_grad, in_grad, head_grad) = reduce_tokens(
        [used(grad_head_t, 0).T, grad_x.astype(BF), grad_z],
        [used(head_weight, 1), in_weight[:, :wide], in_weight[:, wide:]],
        9,
        [
            Parcel(ff_grad.reshape(m, n // m, 2, unit_pad, depth), "swap", "fsdp", BULK),
            Parcel(small_grad, "swap", "fsdp", BULK),
            Parcel(jnp.concatenate([x_grad, z_grad], 1), "swap", "fsdp", BULK, by_lanes),
            Parcel(head_grad, "swap", "ctx", BULK),
        ],
    )
    runs = n // m
    row, column = counted(m * runs * unit_pad, units * runs)
    piece, run, unit = row // (runs * unit_pad), row // unit_pad % runs, row % unit_pad
    chosen = ((unit < unit_sub) & ((run * m + piece) * unit_sub + unit == column)).astype(BF)
    ff_grad = [contract(ff_grad[:, :, i].reshape(-1, depth), chosen, 0, 0) for i in range(2)]
    small_grad = jnp.sum(small_grad, 0)
    in_grad = jnp.sum(in_grad.astype(F32), 0).astype(BF).reshape(n, depth, subp)

    grad_norm_in, gain_one = norm_backward(hidden, factor_one, gain_set[0], grad_normed)
    input_grad = grad_resid + grad_norm_in
    gain_grads = jnp.concatenate([gain_one, gain_two, gain_three, gain_four]).reshape(n, m, 1, -1)
    gain_grads = pad_to(gain_grads, 256, 3)
    meta_grad = pad_to(jnp.concatenate([gain_grads, jnp.full_like(gain_grads, error_part)], 2), 8, 2)

    def by_fsdp(ref, peer, shape):
        if ref is None:
            return (shape[0],) + shape[2:]
        return ref.at[:, peer]

    def by_run(ref, peer, shape):
        if ref is None:
            return (chunks,) + shape[1:]
        return ref.at[pl.ds(peer * chunks, chunks)]

    _, _, head_grad, meta_grad, in_grad = send_only(
        [
            Parcel(meta_grad, "swap", "ctx", 0),
            Parcel(in_grad, "swap", "ctx", 0),
            Parcel(head_grad, "gather", "fsdp", BULK),
            Parcel(0, "swap", "fsdp", 1, by_fsdp),
            Parcel(1, "swap", "pair", 1, by_run),
        ],
        10,
    )
    meta_grad = jnp.sum(meta_grad, (0, 1))
    gains_grad = meta_grad[0, : norm_gains.shape[0]]
    loss = meta_grad[1, 0] / (valid_sum * D)
    in_grad = in_grad[..., :sub].transpose(2, 1, 0, 3).reshape(depth, w_in.shape[1]).astype(F32)
    part, shard, lane, column = counted(m, n, head_pad, head_wide)
    chosen = (natural_column(part, shard, lane) - fsdp_index * head_wide == column).astype(BF)
    head_grad = lax.dot_general(
        head_grad, chosen, (((0, 1, 3), (0, 1, 2)), ((), ())), preferred_element_type=F32
    )
    query_grad, kv_grad = head_grad[:, :query_wide], head_grad[:, query_wide:]

    return (
        loss,
        layer_out.astype(BF)[None],
        input_grad[None],
        query_grad,
        kv_grad,
        attn_out_grad,
        in_grad,
        mamba_out_grad,
        ff_grad[0],
        ff_grad[1],
        down_grad,
        small_grad[:, : R + 2 * DS],
        small_grad[:, R + 2 * DS : 2 * R + 2 * DS],
        small_grad[:, 2 * R + 2 * DS : 2 * R + 3 * DS],
        small_grad[:, 2 * R + 3 * DS : 2 * R + 3 * DS + KC],
        small_grad[:, 2 * R + 3 * DS + KC],
        small_grad[:, 2 * R + 3 * DS + KC + 1],
        small_grad[:, 2 * R + 3 * DS + KC + 2],
        gains_grad,
    )


def solution(mesh):
    in_specs = (
        P("fsdp", "ctx", None),
        P("fsdp", "ctx", None),
        P("fsdp", "ctx", None),
        P("fsdp", "ctx"),
        P("ctx", "fsdp"),
        P("ctx", "fsdp"),
        P("ctx", "fsdp"),
        P("ctx", "fsdp"),
        P("ctx", "fsdp"),
        P("ctx", "fsdp"),
        P("ctx", "fsdp"),
        P("ctx", "fsdp"),
        P(("ctx", "fsdp"), None),
        P(("ctx", "fsdp"), None),
        P(("ctx", "fsdp"), None),
        P(("ctx", "fsdp"), None),
        P(("ctx", "fsdp")),
        P(("ctx", "fsdp")),
        P(("ctx", "fsdp")),
        P(("ctx", "fsdp")),
    )
    out_specs = (
        P(),
        P("fsdp", "ctx", None),
        P("fsdp", "ctx", None),
        P("ctx", "fsdp"),
        P("ctx", "fsdp"),
        P("ctx", "fsdp"),
        P("ctx", "fsdp"),
        P("ctx", "fsdp"),
        P("ctx", "fsdp"),
        P("ctx", "fsdp"),
        P("ctx", "fsdp"),
        P(("ctx", "fsdp"), None),
        P(("ctx", "fsdp"), None),
        P(("ctx", "fsdp"), None),
        P(("ctx", "fsdp"), None),
        P(("ctx", "fsdp")),
        P(("ctx", "fsdp")),
        P(("ctx", "fsdp")),
        P(("ctx", "fsdp")),
    )
    return jax.shard_map(body, mesh=mesh, in_specs=in_specs, out_specs=out_specs, check_vma=False)
```

```python
import functools
from typing import Any, NamedTuple

import jax
import jax.numpy as jnp
from jax import lax
from jax.experimental import pallas as pl
from jax.experimental.pallas import tpu as pltpu
from jax.sharding import PartitionSpec as P

D = 1600
H = 25
HD = 64
KVH = 5
WINDOW = 1024
DI = 3200
DS = 16
KC = 4
R = 100
LOG2E = 1.4426950408889634
BF = jnp.bfloat16
F32 = jnp.float32

TC = 128
LW = 512

def fold_rows(parts):
    row = lax.broadcasted_iota(jnp.int32, parts[0].shape, 0)
    for shift in (1, 2, 4):
        keep = (row & shift) == 0
        merged = []
        for first, second in zip(parts[0::2], parts[1::2]):
            stay = jnp.where(keep, first, second)
            move = jnp.where(keep, second, first)
            merged.append(stay + pltpu.roll(move, shift, 0))
        parts = merged
    return parts[0]

def spread(column, lanes):
    return jnp.concatenate([column.astype(jnp.float32)] * (lanes // 128), 1)

def ssm_forward_kernel(step_ref, u_ref, b_ref, c_ref, rate_ref, y_ref, start_ref, state):
    @pl.when(pl.program_id(0) == 0)
    def _():
        state[...] = jnp.zeros_like(state)
    start_ref[0] = state[...]
    width = state.shape[1]
    lw = min(LW, width)
    for low in range(0, width, lw):
        lanes = slice(low, low + lw)
        rate = rate_ref[:, lanes]

        def group(index, running):
            row = pl.multiple_of(index * 8, 8)
            steps = step_ref[pl.ds(row, 8), lanes]
            drive = steps * u_ref[pl.ds(row, 8), lanes]
            sums = []
            for k in range(8):
                b_now, c_now = spread(b_ref[row + k], lw), spread(c_ref[row + k], lw)
                running = jnp.exp2(rate * steps[k : k + 1]) * running + b_now * drive[k : k + 1]
                seen = running * c_now
                sums.append(seen[:8] + seen[8:])
            y_ref[pl.ds(row, 8), lanes] = fold_rows(sums)
            return running

        state[:, lanes] = lax.fori_loop(0, TC // 8, group, state[:, lanes])

def ssm_forward(step, u, b_t, c_t, rate, parcels, number):
    length, width = step.shape
    states = rate.shape[0]
    count = length // TC
    rows = pl.BlockSpec((TC, width), lambda i: (i, 0))
    cols = pl.BlockSpec((TC, states, 128), lambda i: (i, 0, 0))
    return talk(
        ssm_forward_kernel,
        [step, u, b_t, c_t, rate],
        [rows, rows, cols, cols, pl.BlockSpec((states, width), lambda i: (0, 0))],
        [jax.ShapeDtypeStruct((length, width), jnp.float32), jax.ShapeDtypeStruct((count, states, width), jnp.float32)],
        [rows, pl.BlockSpec((1, states, width), lambda i: (i, 0, 0))],
        [pltpu.VMEM((states, width), jnp.float32)],
        parcels,
        number,
        32 << 20,
        "ssm_forward",
        steps=count,
    )

def lane_sums(values):
    high = values.astype(jnp.bfloat16)
    low = (values - high.astype(jnp.float32)).astype(jnp.bfloat16)
    ones = jnp.ones((8, values.shape[1]), jnp.bfloat16)
    dims = (((1,), (1,)), ((), ()))
    return lax.dot_general(ones, high, dims, preferred_element_type=jnp.float32) + lax.dot_general(
        ones, low, dims, preferred_element_type=jnp.float32
    )

def ssm_backward_kernel(
    step_ref, u_ref, dy_ref, b_ref, c_ref, rate_ref, amat_ref, start_ref,
    dstep_ref, along_ref, db_ref, dc_ref, da_ref,
    adjoint, history, decays, b_part, c_part,
):
    states, width = adjoint.shape
    lw = min(LW, width)

    @pl.when(pl.program_id(0) == 0)
    def _():
        adjoint[...] = jnp.zeros_like(adjoint)
        da_ref[...] = jnp.zeros_like(da_ref)

    for low in range(0, width, lw):
        lanes = slice(low, low + lw)
        rate = rate_ref[:, lanes]
        amat = amat_ref[:, lanes]

        def replay(index, running):
            row = pl.multiple_of(index * 8, 8)
            steps = step_ref[pl.ds(row, 8), lanes]
            drive = steps * u_ref[pl.ds(row, 8), lanes]
            for k in range(8):
                decay = jnp.exp2(rate * steps[k : k + 1])
                history[row + k] = running
                decays[row + k] = decay
                running = decay * running + spread(b_ref[row + k], lw) * drive[k : k + 1]
            return running

        final = lax.fori_loop(0, TC // 8, replay, start_ref[0, :, lanes])

        def group(index, carry):
            lam, grown, after = carry
            row = pl.multiple_of(TC - 8 - index * 8, 8)
            steps = step_ref[pl.ds(row, 8), lanes]
            inputs = u_ref[pl.ds(row, 8), lanes]
            drive = steps * inputs
            dys = dy_ref[pl.ds(row, 8), lanes]
            through_sums = [None] * 8
            along_sums = [None] * 8
            for k in reversed(range(8)):
                before = history[row + k]
                lam = lam + spread(c_ref[row + k], lw) * dys[k : k + 1]
                passed = lam * decays[row + k]
                through = passed * before
                grown = grown + through * steps[k : k + 1]
                scaled = through * amat
                through_sums[k] = scaled[:8] + scaled[8:]
                along = lam * spread(b_ref[row + k], lw)
                along_sums[k] = along[:8] + along[8:]
                b_term = lam * drive[k : k + 1]
                c_term = after * dys[k : k + 1]
                b_sum = b_term[:, :128]
                c_sum = c_term[:, :128]
                for more in range(128, lw, 128):
                    b_sum = b_sum + b_term[:, more : more + 128]
                    c_sum = c_sum + c_term[:, more : more + 128]
                place = pl.ds(pl.multiple_of((row + k) * states, states), states)
                if low == 0:
                    b_part[place, :] = b_sum
                    c_part[place, :] = c_sum
                else:
                    b_part[place, :] += b_sum
                    c_part[place, :] += c_sum
                lam = passed
                after = before
            along_all = fold_rows(along_sums)
            along_ref[pl.ds(row, 8), lanes] = along_all
            dstep_ref[pl.ds(row, 8), lanes] = fold_rows(through_sums) + inputs * along_all
            return lam, grown, after

        lam, grown, _ = lax.fori_loop(0, TC // 8, group, (adjoint[:, lanes], da_ref[:, lanes], final))
        adjoint[:, lanes] = lam
        da_ref[:, lanes] = grown
    db_ref[0] = lane_sums(b_part[...])
    dc_ref[0] = lane_sums(c_part[...])

def ssm_backward(step, u, dy, b_t, c_t, rate, amat, starts, parcels, number):
    length, width = step.shape
    states = rate.shape[0]
    count = length // TC
    last = count - 1
    lw = min(LW, width)
    rows = pl.BlockSpec((TC, width), lambda i: (last - i, 0))
    cols = pl.BlockSpec((TC, states, 128), lambda i: (last - i, 0, 0))
    whole = pl.BlockSpec((states, width), lambda i: (0, 0))
    sums = pl.BlockSpec((1, 8, TC * states), lambda i: (last - i, 0, 0))
    (dstep, along, db, dc, da), extra = talk(
        ssm_backward_kernel,
        [step, u, dy, b_t, c_t, rate, amat, starts],
        [rows, rows, rows, cols, cols, whole, whole, pl.BlockSpec((1, states, width), lambda i: (last - i, 0, 0))],
        [
            jax.ShapeDtypeStruct((length, width), jnp.float32),
            jax.ShapeDtypeStruct((length, width), jnp.float32),
            jax.ShapeDtypeStruct((count, 8, TC * states), jnp.float32),
            jax.ShapeDtypeStruct((count, 8, TC * states), jnp.float32),
            jax.ShapeDtypeStruct((states, width), jnp.float32),
        ],
        [rows, rows, sums, sums, whole],
        [
            pltpu.VMEM((states, width), jnp.float32),
            pltpu.VMEM((TC, states, lw), jnp.float32),
            pltpu.VMEM((TC, states, lw), jnp.float32),
            pltpu.VMEM((TC * states, 128), jnp.float32),
            pltpu.VMEM((TC * states, 128), jnp.float32),
        ],
        parcels,
        number,
        40 << 20,
        "ssm_backward",
        steps=count,
    )
    return dstep, along, db[:, 0].reshape(length, states), dc[:, 0].reshape(length, states), da, extra

QB = 256

def dot_nn(a, b):
    return lax.dot_general(a, b, (((1,), (0,)), ((), ())), preferred_element_type=jnp.float32)

def dot_nt(a, b):
    return lax.dot_general(a, b, (((1,), (1,)), ((), ())), preferred_element_type=jnp.float32)

def fill_bias(bias, first_key):
    span, queries = bias.shape
    key = first_key + lax.broadcasted_iota(jnp.int32, bias.shape, 0)
    query = pl.program_id(0) * queries + lax.broadcasted_iota(jnp.int32, bias.shape, 1)
    gap = query - key
    bias[...] = jnp.where((gap >= 0) & (gap < WINDOW), 0.0, -1e30)

def first_key_of(span):
    return pl.multiple_of(jnp.maximum(pl.program_id(0) * QB - (span - QB), 0), QB)

def slot_of(heads, j):
    first = heads * lax.axis_index("ctx")
    group = H // KVH
    return lax.div(jnp.minimum(first + j, H - 1), group) - lax.div(jnp.minimum(first, H - 1), group)

def attend_kernel(q_ref, k_ref, v_ref, o_ref, lse_ref, bias):
    span = bias.shape[0]
    first = first_key_of(span)
    fill_bias(bias, first)
    lse_ref[...] = jnp.zeros_like(lse_ref)

    def head(j, _):
        slot = slot_of(q_ref.shape[0] // HD, j)
        feats = pl.ds(pl.multiple_of(j * HD, HD), HD)
        scores = dot_nn(k_ref[slot, pl.ds(first, span), :], q_ref[feats, :]) + bias[...]
        top = jnp.max(scores, axis=0, keepdims=True)
        grown = jnp.exp(scores - top)
        total = jnp.sum(grown, axis=0, keepdims=True)
        probs = (grown * (1.0 / total)).astype(jnp.bfloat16)
        o_ref[feats, :] = dot_nn(v_ref[slot, :, pl.ds(first, span)], probs).astype(o_ref.dtype)
        lse_ref[pl.ds(j, 1), :] = top + jnp.log(total)
        return 0

    lax.fori_loop(0, q_ref.shape[0] // HD, head, 0)

def attend(q_t, k, v_t, parcels, number):
    feats, length = q_t.shape
    span = min(WINDOW + QB, length)
    tokens = pl.BlockSpec((feats, QB), lambda i: (0, i))
    whole = lambda a: pl.BlockSpec(a.shape, lambda i: (0,) * a.ndim)
    return talk(
        attend_kernel,
        [q_t, k, v_t],
        [tokens, whole(k), whole(v_t)],
        [jax.ShapeDtypeStruct((feats, length), jnp.bfloat16), jax.ShapeDtypeStruct((8, length), jnp.float32)],
        [tokens, pl.BlockSpec((8, QB), lambda i: (0, i))],
        [pltpu.VMEM((span, QB), jnp.float32)],
        parcels,
        number,
        40 << 20,
        "attend",
        steps=length // QB,
    )

def attend_back_kernel(q_ref, do_ref, k_ref, kt_ref, v_ref, lse_ref, dq_ref, dk_ref, dv_ref, bias):
    span = bias.shape[0]
    first = first_key_of(span)
    fill_bias(bias, first)

    @pl.when(pl.program_id(0) == 0)
    def _():
        dk_ref[...] = jnp.zeros_like(dk_ref)
        dv_ref[...] = jnp.zeros_like(dv_ref)

    def head(j, _):
        slot = slot_of(q_ref.shape[0] // HD, j)
        feats = pl.ds(pl.multiple_of(j * HD, HD), HD)
        keys = pl.ds(first, span)
        query = q_ref[feats, :]
        grad = do_ref[feats, :]
        probs = jnp.exp(dot_nn(k_ref[slot, keys, :], query) + bias[...] - lse_ref[pl.ds(j, 1), :])
        slopes = dot_nn(v_ref[slot, keys, :], grad)
        inner = jnp.sum(probs * slopes, axis=0, keepdims=True)
        ds = (probs * (slopes - inner)).astype(jnp.bfloat16)
        dq_ref[feats, :] = (dot_nn(kt_ref[slot, :, keys], ds) * HD**-0.5).astype(dq_ref.dtype)
        dk_ref[slot, :, keys] += dot_nt(query, ds)
        dv_ref[slot, :, keys] += dot_nt(grad, probs.astype(jnp.bfloat16))
        return 0

    lax.fori_loop(0, q_ref.shape[0] // HD, head, 0)

def attend_back(q_t, do_t, k, k_t, v, lse, parcels, number):
    feats, length = q_t.shape
    span = min(WINDOW + QB, length)
    tokens = pl.BlockSpec((feats, QB), lambda i: (0, i))
    whole = lambda a: pl.BlockSpec(a.shape, lambda i: (0,) * a.ndim)
    return talk(
        attend_back_kernel,
        [q_t, do_t, k, k_t, v, lse],
        [tokens, tokens, whole(k), whole(k_t), whole(v), pl.BlockSpec((8, QB), lambda i: (0, i))],
        [
            jax.ShapeDtypeStruct((feats, length), jnp.bfloat16),
            jax.ShapeDtypeStruct(k_t.shape, jnp.float32),
            jax.ShapeDtypeStruct(k_t.shape, jnp.float32),
        ],
        [tokens, whole(k_t), whole(k_t)],
        [pltpu.VMEM((span, QB), jnp.float32)],
        parcels,
        number,
        40 << 20,
        "attend_back",
        steps=length // QB,
    )


def contract(left, right, left_dim, right_dim):
    return lax.dot_general(left, right, (((left_dim,), (right_dim,)), ((), ())), preferred_element_type=F32)


def matmul(left, right):
    return contract(left, right, 1, 0)


def matmul_tn(left, right):
    return contract(left, right, 0, 0)


def matmul_nt(left, right):
    return contract(left, right, 1, 1)


def norm_forward(values, gain_vec):
    factor = lax.rsqrt(jnp.mean(values * values, axis=-1, keepdims=True) + 1e-06)
    return (values * factor * gain_vec, factor)


def norm_backward(values, factor, gain_vec, grad_out):
    weighted = grad_out * gain_vec
    inner_mean = jnp.mean(weighted * values, axis=-1, keepdims=True)
    grad_in = factor * weighted - values * (factor * factor * factor) * inner_mean
    return (grad_in, jnp.sum(grad_out * values * factor, axis=0))


def silu_slope(values):
    sigmoid_v = jax.nn.sigmoid(values)
    return sigmoid_v * (1.0 + values * (1.0 - sigmoid_v))


def pad_to(array, size, dim):
    widths = [(0, 0)] * array.ndim
    widths[dim] = (0, size - array.shape[dim])
    return jnp.pad(array, widths)


MESH = pl.DeviceIdType.MESH


BULK = 9


class Parcel(NamedTuple):
    source: Any
    kind: str
    axis: str
    group: int
    pick: Any = None


class Line(NamedTuple):
    size: int
    me: Any
    device: Any


def line_of(axis, sizes):
    n, m = sizes
    ctx = lax.axis_index("ctx")
    if axis == "ctx":
        return Line(n, ctx, lambda peer: {"ctx": peer})
    if axis == "chip":
        return Line(n // 2, lax.div(ctx, 2), lambda peer: {"ctx": 2 * peer + lax.rem(ctx, 2)})
    if axis == "core":
        return Line(2, lax.rem(ctx, 2), lambda peer: {"ctx": ctx - lax.rem(ctx, 2) + peer})
    me = lax.axis_index("fsdp")
    if axis == "fsdp":
        return Line(m, me, lambda peer: {"fsdp": peer})
    half = m // 2
    own = lax.rem(me, half)
    return Line(half, own, lambda peer: {"fsdp": me - own + peer})


def size_of(axis, sizes):
    n, m = sizes
    return {"ctx": n, "chip": n // 2, "core": 2, "fsdp": m, "pair": m // 2}[axis]


def parcel_shapes(parcels, sizes):
    shapes = []
    for parcel in parcels:
        source = shapes[parcel.source] if isinstance(parcel.source, int) else parcel.source
        size = size_of(parcel.axis, sizes)
        shape = source.shape
        if parcel.kind == "gather":
            shape = (size,) + shape
        elif parcel.kind == "inner":
            shape = shape[:1] + (size,) + shape[1:]
        elif parcel.kind == "lanes":
            shape = shape[:-1] + (size * shape[-1],)
        elif parcel.pick is not None:
            shape = (size,) + parcel.pick(None, None, shape)
        shapes.append(jax.ShapeDtypeStruct(shape, source.dtype))
    return shapes


class Mail:
    def __init__(self, parcels, sizes, in_refs, out_refs, sems):
        self.parcels, self.sizes, self.outs = parcels, sizes, out_refs
        self.send, self.recv, self.local = sems if sems else (None,) * 3
        given = iter(in_refs)
        self.sources = [out_refs[p.source] if isinstance(p.source, int) else next(given) for p in parcels]
        self.base = []
        total = 0
        for p in parcels:
            self.base.append(total)
            total += size_of(p.axis, sizes)

    def parts(self, number, line, peer, owner):
        parcel, source, out = self.parcels[number], self.sources[number], self.outs[number]
        if parcel.kind == "swap":
            source = parcel.pick(source, peer, None) if parcel.pick else source.at[peer]
        if parcel.kind == "lanes":
            lanes = self.sources[number].shape[-1]
            spot = pl.ds(pl.multiple_of(owner * lanes, lanes), lanes)
            return source, out.at[(slice(None),) * (len(out.shape) - 1) + (spot,)]
        if parcel.kind == "inner":
            return source, out.at[:, owner]
        return source, out.at[owner]

    def copies(self, group, incoming):
        for number, parcel in enumerate(self.parcels):
            if parcel.group != group:
                continue
            line = line_of(parcel.axis, self.sizes)
            for d in range(1, line.size):
                peer = lax.rem(line.me + d, line.size)
                owner = lax.rem(line.me + line.size - d, line.size) if incoming else line.me
                source, target = self.parts(number, line, peer, owner)
                spot = self.base[number] + d
                yield pltpu.make_async_remote_copy(
                    src_ref=source,
                    dst_ref=target,
                    send_sem=self.send.at[spot],
                    recv_sem=self.recv.at[spot],
                    device_id=line.device(peer),
                    device_id_type=MESH,
                )

    def kept(self, group):
        for number, parcel in enumerate(self.parcels):
            if parcel.group == group:
                line = line_of(parcel.axis, self.sizes)
                source, target = self.parts(number, line, line.me, line.me)
                yield pltpu.make_async_copy(source, target, self.local.at[number])

    def start(self, group):
        for copy in self.copies(group, False):
            copy.start()
        for copy in self.kept(group):
            copy.start()

    def wait(self, group):
        for copy in self.copies(group, True):
            copy.wait_recv()
        for copy in self.copies(group, False):
            copy.wait_send()
        for copy in self.kept(group):
            copy.wait()

    def step(self, done, begun):
        if self.has(done):
            self.wait(done)
            if self.has(begun):
                self.start(begun)

    def begin(self):
        for group in (0, BULK):
            if self.has(group):
                self.start(group)

    def end(self, last):
        for group in (last, BULK):
            if self.has(group):
                self.wait(group)

    def has(self, group):
        return any(p.group == group for p in self.parcels)


def ctx_copy(source, target, send, recv, device):
    return pltpu.make_async_remote_copy(
        src_ref=source, dst_ref=target, send_sem=send, recv_sem=recv, device_id={"ctx": device}, device_id_type=MESH
    )


def line_place(n):
    me = lax.axis_index("ctx")
    core = lax.rem(me, 2)
    return me, core, me // 2, me + 1 - 2 * core


def greet(sizes, everyone, fsdp):
    n, m = sizes
    chips = n // 2
    me, core, chip, sibling = line_place(n)
    barrier = pltpu.get_barrier_semaphore()

    def hello(device):
        pl.semaphore_signal(barrier, inc=1, device_id=device, device_id_type=MESH)

    expected = 0
    if everyone:
        for d in range(1, n):
            hello({"ctx": lax.rem(me + d, n)})
        expected = n - 1
    else:
        hello({"ctx": sibling})

        @pl.when(chip > 0)
        def _():
            hello({"ctx": me - 2})

        @pl.when(chip < chips - 1)
        def _():
            hello({"ctx": me + 2})

        expected = 3 - (chip == 0).astype(jnp.int32) - (chip == chips - 1).astype(jnp.int32)
    if fsdp:
        own = lax.axis_index("fsdp")
        for d in range(1, m):
            hello({"fsdp": lax.rem(own + d, m)})
        expected = expected + m - 1
    pl.semaphore_wait(barrier, expected)


def talk(core_kernel, args, in_specs, out_shapes, out_specs, scratch, parcels, number, vmem, name, everyone=False, steps=0):
    sizes = (lax.axis_size("ctx"), lax.axis_size("fsdp"))
    arrays = [p.source for p in parcels if not isinstance(p.source, int)]
    shapes = parcel_shapes(parcels, sizes)
    total = sum(size_of(p.axis, sizes) for p in parcels)
    everyone = everyone or any(p.axis in ("ctx", "chip", "core") for p in parcels)
    fsdp = any(p.axis in ("fsdp", "pair") for p in parcels)
    anywhere = pl.BlockSpec(memory_space=pl.ANY)
    sems = []
    if parcels:
        sems = [pltpu.SemaphoreType.DMA((total,)), pltpu.SemaphoreType.DMA((total,)), pltpu.SemaphoreType.DMA((len(parcels),))]

    def kernel(*refs):
        refs = list(refs)
        take = lambda count: [refs.pop(0) for _ in range(count)]
        ins, mail_in, outs, mail_out = take(len(args)), take(len(arrays)), take(len(out_shapes)), take(len(shapes))
        own = take(len(scratch))
        mail = Mail(parcels, sizes, mail_in, mail_out, refs)
        if not steps:
            greet(sizes, everyone, fsdp)
            core_kernel(sizes[0], ins, outs, own, mail)
            return

        @pl.when(pl.program_id(0) == 0)
        def _():
            greet(sizes, everyone, fsdp)
            mail.begin()

        if mail.has(1):

            @pl.when(pl.program_id(0) == steps // 2)
            def _():
                mail.step(0, 1)

        core_kernel(*ins, *outs, *own)

        @pl.when(pl.program_id(0) == steps - 1)
        def _():
            mail.end(1 if mail.has(1) else 0)

    results = pl.pallas_call(
        kernel,
        grid=(steps,) if steps else (),
        out_shape=list(out_shapes) + shapes,
        in_specs=list(in_specs) + [anywhere] * len(arrays),
        out_specs=list(out_specs) + [anywhere] * len(shapes),
        scratch_shapes=list(scratch) + sems,
        compiler_params=pltpu.CompilerParams(collective_id=number, has_side_effects=True, vmem_limit_bytes=vmem),
        name=name,
    )(*args, *arrays)
    return results[: len(out_shapes)], results[len(out_shapes) :]


def share_core(n, xs, outs, sems, mail):
    chips = n // 2
    me, core, chip, sibling = line_place(n)
    send, recv, side_send, side_recv, local = sems
    several = range(len(xs))
    ways = ((0, 1), (1, -1))

    def spot(hop, sign):
        held = chip - sign * hop
        onward = chip + sign
        have = (held >= 0) & (held < chips)
        return 2 * held, have, have & (onward >= 0) & (onward < chips), 2 * onward + core

    def line_copy(a, way, hop, source, block, device):
        return ctx_copy(source, outs[a].at[block], send.at[a, way, hop], recv.at[a, way, hop], device)

    def side_copy(a, way, hop, source, block):
        return ctx_copy(source, outs[a].at[block], side_send.at[a, way, hop], side_recv.at[a, way, hop], sibling)

    keeps = [pltpu.make_async_copy(xs[a], outs[a].at[me], local.at[a]) for a in several]
    for a in several:
        keeps[a].start()
        side_copy(a, 0, 0, xs[a], me).start()
    for hop in range(chips):
        for way, sign in ways:
            base, have, go, onward = spot(hop, sign)
            block = base + core
            if hop > 0:

                @pl.when(have)
                def _():
                    for a in several:
                        line_copy(a, way, hop - 1, xs[a], block, sibling).wait_recv()
                        side_copy(a, way, hop, outs[a].at[block], block).start()

            if hop < chips - 1:

                @pl.when(go)
                def _():
                    for a in several:
                        source = xs[a] if hop == 0 else outs[a].at[block]
                        line_copy(a, way, hop, source, block, onward).start()

        if hop == 0:
            mail.begin()
            mail.step(0, 1)
        if hop == 1:
            mail.step(1, 2)

    for hop in range(chips):
        for way, sign in ways:
            base, have, go, onward = spot(hop, sign)
            block = base + core
            other = base + 1 - core
            if hop > 0:

                @pl.when(have)
                def _():
                    for a in several:
                        side_copy(a, way, hop, outs[a].at[block], block).wait_send()
                        side_copy(a, way, hop, xs[a], other).wait_recv()

            if hop < chips - 1:

                @pl.when(go)
                def _():
                    for a in several:
                        line_copy(a, way, hop, xs[a], block, onward).wait_send()

    for a in several:
        side_copy(a, 0, 0, xs[a], me).wait_send()
        side_copy(a, 0, 0, xs[a], sibling).wait_recv()
        keeps[a].wait()
    mail.end(2)


def share_tokens(blocks, number, parcels=()):
    n = lax.axis_size("ctx")
    anywhere = pl.BlockSpec(memory_space=pl.ANY)
    count = len(blocks)
    return talk(
        share_core,
        blocks,
        [anywhere] * count,
        [jax.ShapeDtypeStruct((n,) + b.shape, b.dtype) for b in blocks],
        [anywhere] * count,
        [pltpu.SemaphoreType.DMA((count, 2, n // 2))] * 4 + [pltpu.SemaphoreType.DMA((count,))],
        list(parcels),
        number,
        16 << 20,
        "share_tokens",
    )


def feed_core(consume, n, ins, outs, own, mail):
    x_ref, given = ins[0], ins[1:]
    count = len(given)
    gathered, held, more = own[0], own[1 : 1 + count], own[1 + count : -6]
    send, recv, side_send, side_recv, local, load = own[-6:]
    chips = n // 2
    me, core, chip, sibling = line_place(n)

    def line_copy(way, hop, source, block, device):
        return ctx_copy(source, gathered.at[block], send.at[way, hop], recv.at[way, hop], device)

    def side_copy(way, hop, source, block):
        return ctx_copy(source, gathered.at[block], side_send.at[way, hop], side_recv.at[way, hop], sibling)

    def spot(hop, way):
        sign = 1 - 2 * way
        at = chip - sign * hop
        onward = chip + sign
        have = (at >= 0) & (at < chips)
        go = have & (onward >= 0) & (onward < chips)
        return 2 * at + core, 2 * at + 1 - core, have, go, 2 * onward + core

    keep = pltpu.make_async_copy(x_ref, gathered.at[me], local)
    keep.start()
    for way in (0, 1):
        _, _, _, go, onward = spot(0, way)

        @pl.when(go)
        def _():
            line_copy(way, 0, x_ref, me, onward).start()

    side_copy(0, 0, x_ref, me).start()
    loads = [pltpu.make_async_copy(source, target, load.at[i]) for i, (source, target) in enumerate(zip(given, held))]
    for copy in loads:
        copy.start()
    mail.begin()
    for copy in loads:
        copy.wait()
    keep.wait()

    def event(number, _):
        later = jnp.maximum(number - 2, 0)
        hop = 1 + lax.div(later, 4)
        kind = lax.rem(later, 4)
        way = lax.rem(kind, 2)

        @pl.when(number == 1)
        def _():
            side_copy(0, 0, x_ref, sibling).wait_recv()

        @pl.when((number >= 2) & (kind == 0))
        def _():
            for w in (0, 1):
                block, _, have, go, onward = spot(hop, w)

                @pl.when(have)
                def _():
                    line_copy(w, hop - 1, x_ref, block, sibling).wait_recv()
                    side_copy(w, hop, gathered.at[block], block).start()

                @pl.when(go)
                def _():
                    line_copy(w, hop, gathered.at[block], block, onward).start()

        block, other, have, _, _ = spot(hop, way)

        @pl.when((number >= 2) & (kind >= 2) & have)
        def _():
            side_copy(way, hop, x_ref, other).wait_recv()

        block = jnp.where(kind >= 2, other, block)
        block = jnp.where(number == 0, me, jnp.where(number == 1, sibling, block))

        @pl.when((number < 2) | have)
        def _():
            consume(block, gathered, held, outs, more, number == 0)

        return 0

    events = 2 + 4 * (chips - 1)
    lax.fori_loop(0, events, event, 0)
    consume(None, gathered, held, outs, more, None)
    for hop in range(chips):
        for way in (0, 1):
            block, other, have, go, onward = spot(hop, way)
            if hop > 0:

                @pl.when(have)
                def _():
                    side_copy(way, hop, gathered.at[block], block).wait_send()

            if hop < chips - 1:

                @pl.when(go)
                def _():
                    line_copy(way, hop, x_ref, block, onward).wait_send()

    side_copy(0, 0, x_ref, me).wait_send()
    mail.end(0)


def feed_tokens(block, number, consume, given, results, scratch, parcels=()):
    n = lax.axis_size("ctx")
    rows, width = block.shape
    vmem = pl.BlockSpec(memory_space=pltpu.VMEM)
    anywhere = pl.BlockSpec(memory_space=pl.ANY)
    return talk(
        functools.partial(feed_core, consume),
        [block] + list(given),
        [anywhere] * (1 + len(given)),
        list(results),
        [vmem] * len(results),
        [pltpu.VMEM((n, rows, width), block.dtype)]
        + [pltpu.VMEM(g.shape, g.dtype) for g in given]
        + list(scratch)
        + [pltpu.SemaphoreType.DMA((2, n // 2))] * 4
        + [pltpu.SemaphoreType.DMA, pltpu.SemaphoreType.DMA((len(given),))],
        list(parcels),
        number,
        56 << 20,
        "feed_tokens",
    )


def reduce_core(job, count, n, ins, outs, own, mail):
    terms = (len(ins) - count) // 2
    pairs = list(zip(ins[:terms], ins[terms : 2 * terms]))
    o_ref = outs[0]
    total, to_side, from_side, inbox, side_send, side_recv, send, recv = own
    chips = n // 2
    me, core, chip, sibling = line_place(n)
    rows = o_ref.shape[0]

    def partial(block):
        place = pl.ds(pl.multiple_of(block * rows, rows), rows)
        return sum(contract(a[place, :], w[...], 1, 0 if w.shape[0] == a.shape[1] else 1) for a, w in pairs)

    def side_copy(dest):
        return ctx_copy(to_side.at[dest], from_side.at[dest], side_send.at[dest], side_recv.at[dest], sibling)

    def line_copy(way, dest, onward):
        return ctx_copy(from_side.at[dest], inbox.at[dest + way], send.at[dest], recv.at[dest + way], onward)

    mail.begin()

    flip = chip >= chips // 2
    near = jnp.where(flip, chips - 1 - chip, chip)
    lead = chips - 1 - 2 * near

    def begin(k):
        later = jnp.maximum(k - lead, 0)
        high = chips - 1 - jnp.minimum(k, lead) - lax.div(later, 2)
        dest = jnp.where(lax.rem(later, 2) == 1, lax.div(later, 2), high)
        dest = jnp.where(flip, chips - 1 - dest, dest)
        to_side[dest] = partial(2 * dest + 1 - core).astype(jnp.bfloat16)
        side_copy(dest).start()
        total[dest] = partial(2 * dest + core)

    begin(0)

    def spot(tick, way):
        far = (chips - 1 - chip) if way == 0 else chip
        k = tick - far
        dest = k if way == 0 else chips - 1 - k
        active = (k >= 0) & ((dest < chip) if way == 0 else (dest > chip))
        return far, k, dest, active, (me - 2 if way == 0 else me + 2)

    def advance(tick, _):
        @pl.when(tick < chips - 1)
        def _():
            begin(tick + 1)

        for way in (0, 1):
            far, k, dest, active, onward = spot(tick, way)
            before = dest - 1 if way == 0 else dest + 1

            @pl.when(active)
            def _():
                side_copy(dest).wait_recv()
                total[dest] += from_side[dest].astype(jnp.float32)

                @pl.when(far > 0)
                def _():
                    line_copy(way, dest, onward).wait_recv()
                    total[dest] += inbox[dest + way].astype(jnp.float32)

                @pl.when((far == 0) & (k > 0))
                def _():
                    line_copy(way, before, onward).wait_send()

                from_side[dest] = total[dest].astype(jnp.bfloat16)
                line_copy(way, dest, onward).start()

        if job:
            job(tick, ins[: len(ins) - count], ins[len(ins) - count :], outs[1:])
        return 0

    lax.fori_loop(0, chips, advance, 0)
    side_copy(chip).wait_recv()
    total[chip] += from_side[chip].astype(jnp.float32)

    @pl.when(chip < chips - 1)
    def _():
        line_copy(0, chip, me - 2).wait_recv()
        total[chip] += inbox[chip].astype(jnp.float32)

    @pl.when(chip > 0)
    def _():
        line_copy(1, chip, me + 2).wait_recv()
        total[chip] += inbox[chip + 1].astype(jnp.float32)

    o_ref[...] = total[chip]

    def finish(tick, _):
        side_copy(tick).wait_send()
        for way in (0, 1):
            far, k, dest, active, onward = spot(tick, way)

            @pl.when(active & ((far > 0) | (k == chips - 2)))
            def _():
                line_copy(way, dest, onward).wait_send()

        return 0

    lax.fori_loop(0, chips, finish, 0)
    mail.end(0)


def reduce_tokens(lefts, rights, number, parcels=(), job=None, job_in=(), job_out=()):
    n = lax.axis_size("ctx")
    chips = n // 2
    rows, width = lefts[0].shape[0] // n, D
    buffer = lambda *lead: pltpu.VMEM(lead + (rows, width), jnp.bfloat16)
    vmem = pl.BlockSpec(memory_space=pltpu.VMEM)

    outs, extra = talk(
        functools.partial(reduce_core, job, len(job_in)),
        lefts + rights + list(job_in),
        [vmem] * (2 * len(lefts) + len(job_in)),
        [jax.ShapeDtypeStruct((rows, width), jnp.float32)] + list(job_out),
        [vmem] * (1 + len(job_out)),
        [pltpu.VMEM((chips, rows, width), jnp.float32), buffer(chips), buffer(chips), buffer(chips + 1)]
        + [pltpu.SemaphoreType.DMA((chips,))] * 3
        + [pltpu.SemaphoreType.DMA((chips + 1,))],
        list(parcels),
        number,
        (56 if chips <= 4 else 60) << 20,
        "reduce_tokens",
    )
    return outs, extra


def total_core(n, ins, outs, own, mail):
    x_ref, o_ref = ins[0], outs[0]
    from_side, summed, inbox, outbox, side_send, side_recv, send, recv, out_send, out_recv, back_send, back_recv, local = own
    chips = n // 2
    me, core, chip, sibling = line_place(n)
    cols = outbox.shape[1]

    def place(ref, block):
        return ref.at[:, pl.ds(pl.multiple_of(block * cols, cols), cols)]

    def side_copy(d):
        dest = lax.rem(chip + d, chips)
        return ctx_copy(place(x_ref, 2 * dest + 1 - core), from_side.at[d], side_send.at[d], side_recv.at[d], sibling)

    def line_copy(d):
        return ctx_copy(summed.at[d], inbox.at[d], send.at[d], recv.at[d], lax.rem(me + 2 * d, n))

    def out_copy(d):
        return ctx_copy(outbox, place(o_ref, me), out_send.at[d], out_recv.at[d], lax.rem(me + 2 * d, n))

    order = list(range(1, chips)) + [0]
    for d in order:
        side_copy(d).start()
    mail.begin()
    for d in order:
        dest = lax.rem(chip + d, chips)
        side_copy(d).wait_recv()
        block = pl.ds(pl.multiple_of((2 * dest + core) * cols, cols), cols)
        summed[d] = x_ref[:, block] + from_side[d]
        if d:
            line_copy(d).start()
    result = summed[0]
    for d in range(1, chips):
        line_copy(d).wait_recv()
        result = result + inbox[d]
    outbox[...] = result.astype(jnp.bfloat16)
    keep = pltpu.make_async_copy(outbox, place(o_ref, me), local)
    keep.start()
    for d in range(1, chips):
        out_copy(d).start()
    side = ctx_copy(outbox, place(o_ref, me), back_send.at[0], back_recv.at[0], sibling)
    side.start()
    mail.step(0, 1)
    for d in range(1, chips):
        origin = lax.rem(me + n - 2 * d, n)
        ctx_copy(outbox, place(o_ref, origin), out_send.at[d], out_recv.at[d], origin).wait_recv()
        ctx_copy(place(o_ref, origin), place(o_ref, origin), back_send.at[d], back_recv.at[d], sibling).start()
    for d in range(chips):
        mine = lax.rem(me + n - 2 * d, n)
        theirs = lax.rem(sibling + n - 2 * d, n)
        ctx_copy(place(o_ref, mine), place(o_ref, mine), back_send.at[d], back_recv.at[d], sibling).wait_send()
        ctx_copy(outbox, place(o_ref, theirs), back_send.at[d], back_recv.at[d], sibling).wait_recv()
        side_copy(d).wait_send()
        if d:
            line_copy(d).wait_send()
            out_copy(d).wait_send()
    keep.wait()
    for number, spread_ref in enumerate(outs[1:]):

        def fill(part, _):
            first = pl.multiple_of(part * 128, 128)
            values = o_ref[number * DS : (number + 1) * DS, pl.ds(first, 128)].astype(jnp.float32)
            for k in range(128):
                column = jnp.broadcast_to(values[:, k : k + 1], (DS, 128))
                spread_ref[first + k] = column.astype(jnp.bfloat16)
            return 0

        lax.fori_loop(0, o_ref.shape[1] // 128, fill, 0)
    mail.end(1)


def total_columns(partial, number, parcels=(), spreads=0):
    n = lax.axis_size("ctx")
    chips = n // 2
    feats, length = partial.shape
    cols = length // n
    vmem = pl.BlockSpec(memory_space=pltpu.VMEM)
    outs, extra = talk(
        total_core,
        [partial],
        [vmem],
        [jax.ShapeDtypeStruct((feats, length), jnp.bfloat16)]
        + [jax.ShapeDtypeStruct((length, DS, 128), jnp.bfloat16)] * spreads,
        [vmem] * (1 + spreads),
        [pltpu.VMEM((chips, feats, cols), jnp.float32)] * 3
        + [pltpu.VMEM((feats, cols), jnp.bfloat16)]
        + [pltpu.SemaphoreType.DMA((chips,))] * 8
        + [pltpu.SemaphoreType.DMA],
        list(parcels),
        number,
        48 << 20,
        "total_columns",
        everyone=True,
    )
    return outs, extra


def send_core(n, ins, outs, own, mail):
    mail.begin()
    mail.step(0, 1)
    mail.end(1)


def send_only(parcels, number):
    return talk(send_core, [], [], [], [], [], list(parcels), number, 16 << 20, "send_only", everyone=True)[1]


def body(
    tokens,
    out_grad,
    teacher,
    valid,
    w_query,
    w_keyval,
    w_attn_out,
    w_in,
    w_mamba_out,
    w_gate,
    w_up,
    w_down,
    x_proj,
    dt_proj,
    a_log,
    conv_taps,
    conv_bias,
    dt_bias,
    skip_gain,
    norm_gains,
):
    n = lax.axis_size("ctx")
    m = lax.axis_size("fsdp")
    fsdp_index = lax.axis_index("fsdp")
    rows = tokens.shape[1]
    length = rows * n
    depth = w_in.shape[0]
    half = m // 2
    chunks = n // half
    chans = DI // n
    sub = chans // half
    subp = -(-sub // 128) * 128
    wide = half * subp
    units = w_down.shape[0]
    unit_sub = units // m
    unit_pad = -(-unit_sub // 16) * 16
    unit_wide = m * unit_pad
    heads = -(-H // n)
    group_size = H // KVH
    feats = -(-(R + 2 * DS) // 16) * 16
    slots = (heads + group_size - 2) // group_size + 1
    q_part = heads * HD // m
    kv_part = 2 * slots * HD // m
    head_pad = -(-(q_part + kv_part) // 128) * 128

    def wide_chans(array):
        array = array.reshape((half, sub) + array.shape[1:])
        return pad_to(array, subp, 1).reshape((wide,) + array.shape[2:])

    def true_chans(array):
        return array.reshape((half, subp) + array.shape[1:])[:, :sub].reshape((chans,) + array.shape[1:])

    mask_rows = valid[0].astype(F32)
    hidden = tokens[0].astype(F32)
    factor_one = lax.rsqrt(jnp.mean(hidden * hidden, axis=-1, keepdims=True) + 1e-06)
    meta_wide = max(256, rows)
    meta = jnp.stack(
        [
            pad_to(norm_gains.astype(F32), meta_wide, 0),
            jnp.full((meta_wide,), jnp.sum(mask_rows)),
            pad_to(factor_one[:, 0], meta_wide, 0),
        ]
    )
    meta = pad_to(meta, 8, 0)
    in_send = pad_to(w_in.reshape(depth, chunks, half, sub).transpose(2, 1, 0, 3), subp, 3)
    head_send = jnp.concatenate([w_query, w_keyval], 1)
    ff_send = jnp.concatenate(
        [pad_to(w.reshape(depth, n // m, m, unit_sub).transpose(2, 1, 0, 3), unit_pad, 3) for w in (w_gate, w_up)], 3
    )
    small_send = jnp.concatenate(
        [x_proj, dt_proj, a_log, conv_taps, conv_bias[:, None], dt_bias[:, None], skip_gain[:, None]], 1
    )

    def by_chunk(ref, peer, shape):
        if ref is None:
            return shape[2:]
        return ref.at[lax.div(peer, chunks), lax.rem(peer, chunks)]

    (tokens_all,), entry = share_tokens(
        [tokens[0]],
        0,
        [
            Parcel(in_send, "swap", "pair", 0),
            Parcel(meta, "gather", "fsdp", 0),
            Parcel(0, "swap", "ctx", 1, by_chunk),
            Parcel(1, "gather", "ctx", 1),
            Parcel(2, "lanes", "fsdp", 2),
            Parcel(head_send, "gather", "fsdp", BULK),
            Parcel(small_send, "gather", "fsdp", BULK),
        ],
    )
    meta_all, in_all, head_all, small_all = entry[3:]
    gain_set = meta_all[:, :, 0, : norm_gains.shape[0]].reshape(4, D)
    valid_sum = jnp.sum(meta_all[:, :, 1, 0])
    in_weight = in_all.reshape(D, 2 * wide)
    small = wide_chans(small_all.reshape(chans, -1))
    xproj_weight = jnp.concatenate([small[:, R : R + 2 * DS], small[:, :R]], 1)
    dtproj_weight = small[:, R + 2 * DS : 2 * R + 2 * DS]
    rest = small[:, 2 * R + 2 * DS :].astype(F32)
    amat = wide_chans(-jnp.exp(small_all.reshape(chans, -1)[:, 2 * R + 2 * DS : 2 * R + 3 * DS].astype(F32))).T
    rate = amat * LOG2E
    taps = rest[:, DS : DS + KC].T
    conv_bias_vec, dt_bias_vec, skip_vec = rest[:, DS + KC], rest[:, DS + KC + 1], rest[:, DS + KC + 2]
    query_wide, kv_wide = w_query.shape[1], w_keyval.shape[1]
    head_wide = query_wide + kv_wide

    def natural_column(part, shard, lane):
        query = heads * HD * shard + q_part * part + lane
        query_at = query // query_wide * head_wide + query % query_wide
        inner = kv_part * part + lane - q_part
        base = jnp.minimum(heads * shard, H - 1) // group_size
        kv_head = jnp.minimum(base + inner // HD % slots, KVH - 1)
        kv_column = inner // (slots * HD) * (KVH * HD) + kv_head * HD + inner % HD
        kv_at = kv_column // kv_wide * head_wide + query_wide + kv_column % kv_wide
        at = jnp.where(lane < q_part, jnp.where(query < H * HD, query_at, -1), kv_at)
        return jnp.where(lane < q_part + kv_part, at, -1)

    def counted(*shape):
        return [lax.broadcasted_iota(jnp.int32, shape, d) for d in range(len(shape))]

    row, shard, lane = counted(m * head_wide, n, head_pad)
    chosen = (row == natural_column(fsdp_index, shard, lane)).astype(BF).reshape(m, head_wide, n * head_pad)
    head_rows = sum(matmul(head_all[f], chosen[f]) for f in range(m)).astype(BF)
    head_rows = head_rows.reshape(depth, n, head_pad).transpose(1, 0, 2)

    factor_all = lax.dynamic_index_in_dim(meta_all, fsdp_index, 1, False)[:, 2, :rows].reshape(length, 1)
    normed_all = (tokens_all.reshape(length, D).astype(F32) * factor_all * gain_set[0]).astype(BF)
    normed_all = lax.optimization_barrier(normed_all)

    inner_low = matmul(normed_all, in_weight).astype(BF)
    x_branch = inner_low[:, :wide].astype(F32)
    z_branch = inner_low[:, wide:].astype(F32)
    padded = jnp.pad(x_branch, ((KC - 1, 0), (0, 0)))
    pre_conv = conv_bias_vec
    for k in range(KC):
        pre_conv = pre_conv + taps[k] * padded[k : k + length]
    ssm_in = jax.nn.silu(pre_conv)
    ssm_low = ssm_in.astype(BF)
    (xdbl_t, b_wide, c_wide), (_, head_cols_all, ff_all) = total_columns(
        pad_to(contract(xproj_weight, ssm_low, 0, 1), feats, 0),
        1,
        [
            Parcel(head_rows, "swap", "ctx", 0),
            Parcel(0, "lanes", "fsdp", 1),
            Parcel(ff_send, "swap", "fsdp", BULK),
        ],
        2,
    )
    head_weight = head_cols_all.reshape(D, m * head_pad)

    head_t = contract(head_weight, normed_all, 0, 1).astype(BF).reshape(m, head_pad, length)
    query_t = head_t[:, :q_part].reshape(heads * HD, length) * BF(HD**-0.5)
    kv_t = head_t[:, q_part : q_part + kv_part].reshape(2, slots, HD, length)
    keys_t, values_t = kv_t[0], kv_t[1]
    keys, values = jnp.swapaxes(keys_t, 1, 2), jnp.swapaxes(values_t, 1, 2)
    row, column = counted(chans, wide)
    chosen = (row // sub * subp + row % sub == column).astype(BF)
    mamba_send = contract(w_mamba_out, chosen, 0, 0).astype(BF)
    (attn_part, lse), (_, attn_rows, mamba_all, ff_cols) = attend(
        query_t,
        keys,
        values_t,
        [
            Parcel(w_attn_out, "gather", "chip", 0),
            Parcel(0, "inner", "core", 1),
            Parcel(mamba_send, "gather", "fsdp", BULK),
            Parcel(ff_all.reshape(n, depth, 2 * unit_pad), "swap", "ctx", BULK),
        ],
        11,
    )
    attn_part = attn_part.reshape(heads * HD, n, rows).transpose(1, 0, 2)
    mamba_weight_t = mamba_all.reshape(D, wide)
    ff_parts = ff_cols.reshape(D, 2 * unit_pad).T.reshape(2, unit_pad, D)

    dt_in_t = xdbl_t[2 * DS : 2 * DS + R]
    dt_pre = contract(dt_in_t, dtproj_weight, 0, 1) + dt_bias_vec
    step_size = jax.nn.softplus(dt_pre)
    row, column = counted(units, unit_wide)
    chosen = (row // unit_sub * unit_pad + row % unit_sub == column).astype(BF)
    down_send = contract(w_down, chosen, 0, 0).astype(BF)
    (state_rows, starts), (attn_t, down_all) = ssm_forward(
        step_size,
        ssm_in,
        b_wide,
        c_wide,
        rate,
        [Parcel(attn_part, "swap", "ctx", BULK), Parcel(down_send, "gather", "fsdp", BULK)],
        12,
    )
    down_weight_t = down_all.reshape(D, unit_wide)
    ssm_out = state_rows + skip_vec * ssm_in
    gate_z = jax.nn.silu(z_branch)
    mixed_low = (ssm_out * gate_z).astype(BF)
    (mamba_proj,), (attn_weight_t,) = reduce_tokens(
        [mixed_low], [mamba_weight_t], 2, [Parcel(attn_rows.reshape(H * HD, -1).T, "gather", "fsdp", BULK)]
    )
    attn_t = attn_t.reshape(n * heads * HD, rows)[: H * HD]
    attn_weight_t = attn_weight_t.reshape(D, H * HD)
    attn_proj = contract(attn_t, attn_weight_t, 0, 1)

    attn_norm, factor_attn = norm_forward(attn_proj, gain_set[1])
    mamba_norm, factor_mamba = norm_forward(mamba_proj, gain_set[2])
    residual = hidden + 0.5 * (attn_norm + mamba_norm)
    ffn_in, factor_ffn = norm_forward(residual, gain_set[3])
    (ffn_all,), (gate_rows, up_rows) = share_tokens(
        [ffn_in.astype(BF)],
        3,
        [Parcel(ff_parts[0], "gather", "fsdp", BULK), Parcel(ff_parts[1], "gather", "fsdp", BULK)],
    )
    ffn_all = ffn_all.reshape(length, D)
    gate_rows, up_rows = gate_rows.reshape(unit_wide, D), up_rows.reshape(unit_wide, D)
    gate_pre = matmul_nt(ffn_all, gate_rows)
    up_pre = matmul_nt(ffn_all, up_rows)
    hidden_act = (jax.nn.silu(gate_pre) * up_pre).astype(BF)
    layer_out = residual + reduce_tokens([hidden_act], [down_weight_t], 4)[0][0]

    mismatch = layer_out - teacher[0].astype(F32)
    error_part = jnp.sum(mask_rows[:, None] * mismatch * mismatch)
    grad_layer = out_grad[0].astype(F32) + 2.0 / (valid_sum * D) * mask_rows[:, None] * mismatch

    def feed_forward_back(block, x, held, outs, more, first):
        if block is None:
            outs[2][...] = more[0][...].astype(BF).reshape(outs[2].shape)
            return
        place = pl.ds(pl.multiple_of(block * rows, rows), rows)
        weight, gates, ups, acts = held
        grad = x[block]
        slope = contract(grad, weight[...], 1, 0)
        gate, up = gates[place, :], ups[place, :]
        sigmoid_v = 1.0 / (1.0 + jnp.exp(-gate))
        outs[0][place, :] = (slope * up * (sigmoid_v * (1.0 + gate * (1.0 - sigmoid_v)))).astype(BF)
        outs[1][place, :] = (slope * (gate * sigmoid_v)).astype(BF)
        part = contract(grad, acts[place, :], 0, 0)

        @pl.when(first)
        def _():
            more[0][...] = part

        @pl.when(jnp.logical_not(first))
        def _():
            more[0][...] += part

    (grad_gate, grad_up, down_grad), _ = feed_tokens(
        grad_layer.astype(BF),
        5,
        feed_forward_back,
        [down_weight_t, gate_pre, up_pre, hidden_act],
        [jax.ShapeDtypeStruct((length, unit_wide), BF)] * 2 + [jax.ShapeDtypeStruct((m, D // m, unit_wide), BF)],
        [pltpu.VMEM((D, unit_wide), F32)],
    )
    grad_parts = [jax.ShapeDtypeStruct((m, unit_pad, D), BF)] * 2

    def unit_grads(tick, given, more, outs):
        for piece in range(m):

            @pl.when(tick == piece * n // (2 * m))
            def _():
                for left, out in zip(given, outs):
                    part = left[:, piece * unit_pad : (piece + 1) * unit_pad]
                    out[piece] = contract(part, more[0][...], 0, 0).astype(BF)

    inside = length * D <= 4 << 20
    reduced, (down_grad,) = reduce_tokens(
        [grad_gate, grad_up],
        [gate_rows, up_rows],
        6,
        [Parcel(down_grad, "swap", "fsdp", BULK)],
        unit_grads if inside else None,
        [ffn_all] if inside else [],
        grad_parts if inside else [],
    )
    grad_ffn_in = reduced[0]
    down_grad = jnp.sum(down_grad.astype(F32), 0).T.reshape(m, unit_pad, D // m)[:, :unit_sub].reshape(units, D // m)
    if inside:
        gate_grad, up_grad = reduced[1:]
    else:
        gate_grad, up_grad = [matmul_tn(g, ffn_all).astype(BF).reshape(m, unit_pad, D) for g in (grad_gate, grad_up)]

    grad_norm_res, gain_four = norm_backward(residual, factor_ffn, gain_set[3], grad_ffn_in)
    grad_resid = grad_layer + grad_norm_res
    half_grad = 0.5 * grad_resid
    grad_attn_proj, gain_two = norm_backward(attn_proj, factor_attn, gain_set[1], half_grad)
    grad_mamba_proj, gain_three = norm_backward(mamba_proj, factor_mamba, gain_set[2], half_grad)
    grad_attn_proj_low = grad_attn_proj.astype(BF)

    def state_space_back(block, x, held, outs, more, first):
        if block is None:
            outs[2][...] = more[0][...].astype(BF).reshape(outs[2].shape)
            return
        place = pl.ds(pl.multiple_of(block * rows, rows), rows)
        weight, z_part, rows_out, mixed = held
        grad = x[block]
        slope = contract(grad, weight[...], 1, 0)
        z = z_part[place, :].astype(F32)
        sigmoid_v = 1.0 / (1.0 + jnp.exp(-z))
        outs[0][place, :] = slope * (z * sigmoid_v)
        outs[1][place, :] = (slope * rows_out[place, :] * (sigmoid_v * (1.0 + z * (1.0 - sigmoid_v)))).astype(BF)
        part = contract(grad, mixed[place, :], 0, 0)

        @pl.when(first)
        def _():
            more[0][...] = part

        @pl.when(jnp.logical_not(first))
        def _():
            more[0][...] += part

    (grad_y, grad_z, mamba_out_grad), (gate_grad, up_grad) = feed_tokens(
        grad_mamba_proj.astype(BF),
        7,
        state_space_back,
        [mamba_weight_t, inner_low[:, wide:], ssm_out, mixed_low],
        [
            jax.ShapeDtypeStruct((length, wide), F32),
            jax.ShapeDtypeStruct((length, wide), BF),
            jax.ShapeDtypeStruct((m, D // m, wide), BF),
        ],
        [pltpu.VMEM((D, wide), F32)],
        [Parcel(gate_grad, "swap", "fsdp", BULK), Parcel(up_grad, "swap", "fsdp", BULK)],
    )
    ff_grad = jnp.stack([jnp.sum(g.astype(F32), 0).astype(BF) for g in (gate_grad, up_grad)])
    ff_grad = ff_grad.reshape(2 * unit_pad, n, depth).transpose(1, 0, 2)
    attn_out_grad = contract(grad_attn_proj_low, attn_t, 0, 1).astype(BF).reshape(m, D // m, H * HD)
    grad_attn = contract(attn_weight_t, grad_attn_proj_low, 0, 1).astype(BF)
    grad_attn = pad_to(grad_attn, n * heads * HD, 0).reshape(n, heads * HD, rows)

    z_grad = matmul_tn(normed_all, grad_z).astype(BF)
    step_grad, along_b, b_grad, c_grad, a_accum, (attn_out_grad, grad_attn) = ssm_backward(
        step_size,
        ssm_in,
        grad_y,
        b_wide,
        c_wide,
        rate,
        amat,
        starts,
        [Parcel(attn_out_grad, "swap", "fsdp", BULK), Parcel(grad_attn, "swap", "ctx", BULK)],
        13,
    )
    attn_out_grad = jnp.sum(attn_out_grad.astype(F32), 0).T.astype(BF)
    attn_out_grad = lax.psum_scatter(attn_out_grad, "ctx", scatter_dimension=0, tiled=True).astype(F32)

    grad_attn = grad_attn.transpose(1, 0, 2).reshape(heads * HD, length)
    (grad_query, grad_keys, grad_values), (ff_grad, mamba_out_grad) = attend_back(
        query_t,
        grad_attn,
        keys,
        keys_t,
        values,
        lse,
        [Parcel(ff_grad, "swap", "ctx", BULK), Parcel(mamba_out_grad, "swap", "fsdp", BULK)],
        14,
    )
    grad_kv = jnp.concatenate([grad_keys, grad_values], 0).astype(BF).reshape(m, kv_part, length)
    grad_head_t = jnp.concatenate([grad_query.reshape(m, q_part, length), grad_kv], 1)
    grad_head_t = pad_to(grad_head_t, head_pad, 1).reshape(m * head_pad, length)
    mamba_out_grad = true_chans(jnp.sum(mamba_out_grad.astype(F32), 0).T)
    head_grad = contract(grad_head_t, normed_all, 1, 0).astype(BF).reshape(m, head_pad, D)

    grad_dt_pre = (step_grad * jax.nn.sigmoid(dt_pre)).astype(BF)
    dtproj_grad = contract(grad_dt_pre, dt_in_t, 0, 1)
    grad_xdbl_t = jnp.concatenate([b_grad.T, c_grad.T, contract(dtproj_weight, grad_dt_pre, 0, 1)], 0)
    (grad_xdbl_t,), (head_grad,) = total_columns(
        pad_to(grad_xdbl_t, feats, 0),
        8,
        [Parcel(head_grad, "swap", "fsdp", BULK)],
    )
    grad_xdbl_t = grad_xdbl_t[: R + 2 * DS]
    head_grad = jnp.sum(head_grad.astype(F32), 0).astype(BF).T.reshape(n, depth, head_pad)
    xproj_grad = contract(ssm_low, grad_xdbl_t, 0, 1)
    grad_ssm_in = step_size * along_b + skip_vec * grad_y + contract(grad_xdbl_t, xproj_weight, 0, 1)
    grad_pre = grad_ssm_in * silu_slope(pre_conv)
    taps_grad = jnp.stack([jnp.sum(grad_pre * padded[k : k + length], axis=0) for k in range(KC)], 1)
    grad_after = jnp.pad(grad_pre, ((0, KC - 1), (0, 0)))
    grad_x = jnp.zeros_like(grad_pre)
    for k in range(KC):
        grad_x = grad_x + taps[k] * grad_after[KC - 1 - k : KC - 1 - k + length]
    x_grad = matmul_tn(normed_all, grad_x.astype(BF)).astype(BF)
    small_grad = jnp.concatenate(
        [
            xproj_grad[:, 2 * DS :],
            xproj_grad[:, : 2 * DS],
            dtproj_grad,
            (a_accum * amat).T,
            taps_grad,
            jnp.sum(grad_pre, axis=0)[:, None],
            jnp.sum(grad_dt_pre.astype(F32), axis=0)[:, None],
            jnp.sum(grad_y * ssm_in, axis=0)[:, None],
        ],
        1,
    )
    small_grad = true_chans(small_grad).reshape(m, chans // m, -1)

    def used(array, dim):
        if head_pad == q_part + kv_part:
            return array
        split = array.reshape(array.shape[:dim] + (m, head_pad) + array.shape[dim + 1 :])
        return lax.slice_in_dim(split, 0, q_part + kv_part, 1, dim + 1).reshape(
            array.shape[:dim] + (-1,) + array.shape[dim + 1 :]
        )

    def by_lanes(ref, peer, shape):
        if ref is None:
            return (shape[0], subp)
        return ref.at[:, pl.ds(pl.multiple_of(peer * subp, subp), subp)]

    (grad_normed,), (ff_grad, small_grad, in_grad, head_grad) = reduce_tokens(
        [used(grad_head_t, 0).T, grad_x.astype(BF), grad_z],
        [used(head_weight, 1), in_weight[:, :wide], in_weight[:, wide:]],
        9,
        [
            Parcel(ff_grad.reshape(m, n // m, 2, unit_pad, depth), "swap", "fsdp", BULK),
            Parcel(small_grad, "swap", "fsdp", BULK),
            Parcel(jnp.concatenate([x_grad, z_grad], 1), "swap", "fsdp", BULK, by_lanes),
            Parcel(head_grad, "swap", "ctx", BULK),
        ],
    )
    runs = n // m
    row, column = counted(m * runs * unit_pad, units * runs)
    piece, run, unit = row // (runs * unit_pad), row // unit_pad % runs, row % unit_pad
    chosen = ((unit < unit_sub) & ((run * m + piece) * unit_sub + unit == column)).astype(BF)
    ff_grad = [contract(ff_grad[:, :, i].reshape(-1, depth), chosen, 0, 0) for i in range(2)]
    small_grad = jnp.sum(small_grad, 0)
    in_grad = jnp.sum(in_grad.astype(F32), 0).astype(BF).reshape(n, depth, subp)

    grad_norm_in, gain_one = norm_backward(hidden, factor_one, gain_set[0], grad_normed)
    input_grad = grad_resid + grad_norm_in
    gain_grads = jnp.concatenate([gain_one, gain_two, gain_three, gain_four]).reshape(n, m, 1, -1)
    gain_grads = pad_to(gain_grads, 256, 3)
    meta_grad = pad_to(jnp.concatenate([gain_grads, jnp.full_like(gain_grads, error_part)], 2), 8, 2)

    def by_fsdp(ref, peer, shape):
        if ref is None:
            return (shape[0],) + shape[2:]
        return ref.at[:, peer]

    def by_run(ref, peer, shape):
        if ref is None:
            return (chunks,) + shape[1:]
        return ref.at[pl.ds(peer * chunks, chunks)]

    _, _, head_grad, meta_grad, in_grad = send_only(
        [
            Parcel(meta_grad, "swap", "ctx", 0),
            Parcel(in_grad, "swap", "ctx", 0),
            Parcel(head_grad, "gather", "fsdp", BULK),
            Parcel(0, "swap", "fsdp", 1, by_fsdp),
            Parcel(1, "swap", "pair", 1, by_run),
        ],
        10,
    )
    meta_grad = jnp.sum(meta_grad, (0, 1))
    gains_grad = meta_grad[0, : norm_gains.shape[0]]
    loss = meta_grad[1, 0] / (valid_sum * D)
    in_grad = in_grad[..., :sub].transpose(2, 1, 0, 3).reshape(depth, w_in.shape[1]).astype(F32)
    part, shard, lane, column = counted(m, n, head_pad, head_wide)
    chosen = (natural_column(part, shard, lane) - fsdp_index * head_wide == column).astype(BF)
    head_grad = lax.dot_general(
        head_grad, chosen, (((0, 1, 3), (0, 1, 2)), ((), ())), preferred_element_type=F32
    )
    query_grad, kv_grad = head_grad[:, :query_wide], head_grad[:, query_wide:]

    return (
        loss,
        layer_out.astype(BF)[None],
        input_grad[None],
        query_grad,
        kv_grad,
        attn_out_grad,
        in_grad,
        mamba_out_grad,
        ff_grad[0],
        ff_grad[1],
        down_grad,
        small_grad[:, : R + 2 * DS],
        small_grad[:, R + 2 * DS : 2 * R + 2 * DS],
        small_grad[:, 2 * R + 2 * DS : 2 * R + 3 * DS],
        small_grad[:, 2 * R + 3 * DS : 2 * R + 3 * DS + KC],
        small_grad[:, 2 * R + 3 * DS + KC],
        small_grad[:, 2 * R + 3 * DS + KC + 1],
        small_grad[:, 2 * R + 3 * DS + KC + 2],
        gains_grad,
    )


def solution(mesh):
    in_specs = (
        P("fsdp", "ctx", None),
        P("fsdp", "ctx", None),
        P("fsdp", "ctx", None),
        P("fsdp", "ctx"),
        P("ctx", "fsdp"),
        P("ctx", "fsdp"),
        P("ctx", "fsdp"),
        P("ctx", "fsdp"),
        P("ctx", "fsdp"),
        P("ctx", "fsdp"),
        P("ctx", "fsdp"),
        P("ctx", "fsdp"),
        P(("ctx", "fsdp"), None),
        P(("ctx", "fsdp"), None),
        P(("ctx", "fsdp"), None),
        P(("ctx", "fsdp"), None),
        P(("ctx", "fsdp")),
        P(("ctx", "fsdp")),
        P(("ctx", "fsdp")),
        P(("ctx", "fsdp")),
    )
    out_specs = (
        P(),
        P("fsdp", "ctx", None),
        P("fsdp", "ctx", None),
        P("ctx", "fsdp"),
        P("ctx", "fsdp"),
        P("ctx", "fsdp"),
        P("ctx", "fsdp"),
        P("ctx", "fsdp"),
        P("ctx", "fsdp"),
        P("ctx", "fsdp"),
        P("ctx", "fsdp"),
        P(("ctx", "fsdp"), None),
        P(("ctx", "fsdp"), None),
        P(("ctx", "fsdp"), None),
        P(("ctx", "fsdp"), None),
        P(("ctx", "fsdp")),
        P(("ctx", "fsdp")),
        P(("ctx", "fsdp")),
        P(("ctx", "fsdp")),
    )
    return jax.shard_map(body, mesh=mesh, in_specs=in_specs, out_specs=out_specs, check_vma=False)
```
